32 devices in a mesh: ia: 4 (over y, core), ja: 8 (over z, x).
Axes of the slice: x: 2, y: 2, z: 4, core: 2. Of those that a mesh axis runs over, the one named last changes fastest.
Arguments:
- positions: float32 [3, 65536], P(None, 'ja')
- velocities: float32 [3, 65536], P(None, 'ja'), may hold values from -4 to 4
- accels: float32 [3, 65536], P(None, 'ja'), may hold values from -6 to 6
- jerks: float32 [3, 65536], P(None, 'ja'), may hold values from -6 to 6
- masses: float32 [65536], P('ja'), may hold values from 3.0517579e-06 to 7.6293945e-05
- levels: int32 [65536], P('ja'), may hold values from 0 to 7
- active: int32 [512], P('ia'), may hold values from 0 to 65535, as said below
Outputs:
- targets_new: float32 [12, 512], P(None, 'ia')
- stars_new: float32 [12, 65536], P(None, 'ja')
The draws below stay inside these ranges and needn't reach their ends.
Inputs may be any that keep to these rules, and one draw needn't show every extreme that they name: `active`: 512 distinct star indices.
All inputs are finite; a program needn't handle non-finite values.
Results may differ from the reference program's by a relative error of at most 0.0001.
Values sent between devices are 32-bit elements; how exact they have to be, the bound alone decides.
No kernel may reach another device: no remote copies, remote signals or barrier semaphores. Data moves between devices by JAX's collectives and lax.ppermute only.
A program may use at most 64 MiB of HBM per device.

```python
import math
import jax
import jax.numpy as jnp
from jax import lax

SOURCES_PER_PART = 8192
STAR_TOTAL = 65536
ACTIVE = 512


def unit_directions(key):
    raw = jax.random.normal(key, (3, STAR_TOTAL), jnp.float32)
    return raw * lax.rsqrt(jnp.sum(raw * raw, axis=0, keepdims=True) + 1e-12)


def draw_positions(key, part):
    key = jax.random.fold_in(key, 11)
    leading_entry, second = jax.random.split(key)
    directions = unit_directions(leading_entry)
    fraction = jax.random.uniform(second, (STAR_TOTAL,), jnp.float32, 0.001, 0.98)
    radius = 0.5 * lax.rsqrt(fraction ** (-2.0 / 3.0) - 1.0)
    return directions * radius[None, :]


def draw_active(key, part):
    key = jax.random.fold_in(key, 23)
    leading_entry, second, third = jax.random.split(key, 3)
    star_groups = STAR_TOTAL // SOURCES_PER_PART
    extra_reward = jnp.repeat(jax.random.randint(leading_entry, (star_groups,), 0, 512), SOURCES_PER_PART)
    random_perturbation = jax.random.randint(second, (STAR_TOTAL,), 0, 512)
    star_numbers = jnp.arange(STAR_TOTAL, dtype=jnp.int32)
    ranking_value = (extra_reward + random_perturbation) * STAR_TOTAL + star_numbers
    ranking_value = jnp.where(star_numbers == STAR_TOTAL - 1, jnp.int32(2147483001), ranking_value)
    ranking_value = jnp.where(star_numbers == 0, jnp.int32(2147483000), ranking_value)
    chosen = lax.top_k(ranking_value, ACTIVE)[1].astype(jnp.int32)
    return jax.random.permutation(third, chosen)


def set_ends(values, key, smallest, largest):
    extent = values.shape
    index_at = [jax.random.randint(jax.random.fold_in(key, axis), (), 0, extent[axis]) for axis in range(len(extent))]
    values = values.at[tuple(index_at)].set(smallest)
    longest = extent.index(max(extent))
    index_at[longest] = (index_at[longest] + 1) % extent[longest]
    return values.at[tuple(index_at)].set(largest)


def shard_levels(key, extent, pieces, smallest, largest):
    def one(position, parts):
        steps = jax.random.uniform(jax.random.fold_in(jax.random.fold_in(key, 6), position), (parts,), jnp.float32, smallest / len(pieces), largest / len(pieces))
        return jnp.repeat(jnp.exp(steps), extent[position] // parts).reshape((-1,) + (1,) * (len(extent) - position - 1))

    level = one(*pieces[0])
    for cut in pieces[1:]:
        level = level * one(*cut)
    return level


def gaussian(stream_key, extent, deviation, limit, pieces=(), kind=jnp.bfloat16):
    gain = shard_levels(stream_key, extent, pieces, -0.22, 0.18) if pieces else 1.0
    values = jax.random.normal(stream_key, extent, jnp.float32) * deviation * gain
    return jnp.minimum(jnp.maximum(values, -limit), limit).astype(kind)


def setup_inputs(seed: int = 0) -> dict:
    key_list = jax.random.split(jax.random.key(seed), 8)
    return {
        "positions": draw_positions(jax.random.fold_in(key_list[7], 71), 0),
        "velocities": gaussian(key_list[1], (3, STAR_TOTAL), 0.5, 4.0, ((1, 8),), jnp.float32),
        "accels": gaussian(key_list[2], (3, STAR_TOTAL), 1.0, 6.0, ((1, 8),), jnp.float32),
        "jerks": gaussian(key_list[3], (3, STAR_TOTAL), 1.0, 6.0, ((1, 8),), jnp.float32),
        "masses": jnp.clip(jnp.exp(math.log(7.62939453125e-05) - 3.218876 * jax.random.uniform(key_list[4], (STAR_TOTAL,), jnp.float32) ** shard_levels(key_list[4], (STAR_TOTAL,), ((0, 8),), -0.2, 0.2)), 3.051757857974735e-06, 7.62939453125e-05),
        "levels": set_ends(jax.random.randint(key_list[5], (STAR_TOTAL,), 0, 8), jax.random.fold_in(key_list[5], 1), 0, 7).astype(jnp.int32),
        "active": draw_active(jax.random.fold_in(key_list[7], 71), 0),
    }


softening_length = 0.01
base_step = 0.0625

def predict(state, elapsed):
    pos, vel, acc, jrk = (state[0:3], state[3:6], state[6:9], state[9:12])
    half = elapsed * elapsed * 0.5
    sixth = half * elapsed / 3.0
    pred_pos = pos + elapsed * vel + half * acc + sixth * jrk
    pred_vel = vel + elapsed * acc + half * jrk
    return (pred_pos, pred_vel)

def pair_terms(carry, source, tpos, tvel):
    spos, svel, smass = source
    position_offset = spos[:, None, :] - tpos[:, :, None]
    delta_v = svel[:, None, :] - tvel[:, :, None]
    radius_squared = lax.optimization_barrier(jnp.sum(position_offset * position_offset, axis=0)) + softening_length
    reciprocal_distance = lax.rsqrt(radius_squared)
    inv_sq = reciprocal_distance * reciprocal_distance
    weight = smass[None, :] * reciprocal_distance * inv_sq
    radial = 3.0 * lax.optimization_barrier(jnp.sum(position_offset * delta_v, axis=0)) * inv_sq
    acc_part = lax.optimization_barrier(jnp.sum(weight[None] * position_offset, axis=-1))
    jerk_part = lax.optimization_barrier(jnp.sum(weight[None] * (delta_v - radial[None] * position_offset), axis=-1))
    return carry + jnp.concatenate([acc_part, jerk_part], axis=0)

def correct(old, forces):
    x0, v0, a0, j0, step = (old[0:3], old[3:6], old[6:9], old[9:12], old[12:13])
    a1, j1 = (forces[0:3], forces[3:6])
    quad = step * step / 12.0
    v1 = v0 + 0.5 * step * (a0 + a1) + quad * (j0 - j1)
    x1 = x0 + 0.5 * step * (v0 + v1) + quad * (a0 - a1)
    return jnp.concatenate([x1, v1, a1, j1], axis=0)

def reference(positions, velocities, accels, jerks, masses, levels, active):
    state = jnp.concatenate([positions, velocities, accels, jerks], axis=0)
    elapsed = base_step * jnp.exp2(-levels.astype(jnp.float32))
    pred_pos, pred_vel = predict(state, elapsed[None, :])
    total = state.shape[1]
    width = math.gcd(total, 2048)
    count = total // width
    tpos = pred_pos[:, active]
    tvel = pred_vel[:, active]
    blocks = (jnp.moveaxis(pred_pos.reshape(3, count, width), 1, 0), jnp.moveaxis(pred_vel.reshape(3, count, width), 1, 0), masses.reshape(count, width))

    def step_fn(carry, source):
        return (pair_terms(carry, source, tpos, tvel), None)
    init = jnp.zeros((6, active.shape[0]), jnp.float32)
    forces, unused = lax.scan(step_fn, init, blocks)
    old = jnp.concatenate([state[:, active], elapsed[active][None, :]], axis=0)
    targets_new = correct(old, forces)
    stars_new = state.at[:, active].set(targets_new)
    return (targets_new, stars_new)
```

```python
import functools

import jax
import jax.numpy as jnp
from jax import lax
from jax.experimental import pallas as pl
from jax.experimental.pallas import tpu as pltpu
from jax.sharding import PartitionSpec as P

softening_length = 0.01
base_step = 0.0625
LANES = 128
f32 = jnp.float32
VMEM = pl.BlockSpec(memory_space=pltpu.VMEM)
HBM = pl.BlockSpec(memory_space=pltpu.HBM)
PARAMS = pltpu.CompilerParams(vmem_limit_bytes=24 * 1024 * 1024)


def elapsed_of(levels):
    return (128 >> levels).astype(f32) * (base_step / 128.0)


def predict(pos, vel, acc, jrk, elapsed):
    half = elapsed * elapsed * 0.5
    sixth = half * elapsed / 3.0
    pred_pos = pos + elapsed * vel + half * acc + sixth * jrk
    pred_vel = vel + elapsed * acc + half * jrk
    return (pred_pos, pred_vel)


def correct(x0, v0, a0, j0, step, a1, j1):
    quad = step * step / 12.0
    v1 = v0 + 0.5 * step * (a0 + a1) + quad * (j0 - j1)
    x1 = x0 + 0.5 * step * (v0 + v1) + quad * (a0 - a1)
    return (x1, v1)


def tile(t):
    return slice(t * LANES, (t + 1) * LANES)


def gather_kernel(*refs):
    given, out, held, sems, kept = (refs[:6], refs[6], refs[7], refs[8], refs[9:])
    copies = [
        pltpu.make_async_copy(a, b, sems.at[n]) for n, (a, b) in enumerate(zip(given, kept))
    ]
    for copy in copies:
        copy.start()
    for copy in copies:
        copy.wait()
    pos, vel, acc, jrk, levels, active = kept
    groups = levels.shape[0]
    offset = active[...] - lax.axis_index("ja") * (groups * LANES)
    group = jnp.broadcast_to(offset >> 7, (8, LANES))
    lane = jnp.broadcast_to(offset & (LANES - 1), (8, LANES))
    held[0:3, :] = pos[...]
    held[3:6, :] = vel[...]
    held[6:9, :] = acc[...]
    held[9:12, :] = jrk[...]
    elapsed = elapsed_of(levels[...])
    for t in range(groups):
        held[12:16, tile(t)] = jnp.broadcast_to(elapsed[t : t + 1], (4, LANES))
    low = jnp.zeros((8, LANES), f32)
    high = jnp.zeros((8, LANES), f32)
    for t in range(groups):
        here = group == t
        low = jnp.where(here, jnp.take_along_axis(held[0:8, tile(t)], lane, axis=1), low)
        high = jnp.where(here, jnp.take_along_axis(held[8:16, tile(t)], lane, axis=1), high)
    out[0:8, :] = low
    out[8:16, :] = high


def force_kernel(columns, *refs):
    gathered, refs = (refs[:columns], refs[columns:])
    pos, vel, acc, jrk, levels, masses, active, packed, old, sources, targets, sums = refs
    groups = levels.shape[0]
    ntarget = active.shape[1]
    state = gathered[0][...]
    for block in gathered[1:]:
        state = state + block[...]
    old[...] = state
    tpos, tvel = predict(state[0:3], state[3:6], state[6:9], state[9:12], state[12:13])
    columns = jnp.transpose(
        jnp.concatenate([tpos, tvel, jnp.zeros((LANES - 6, ntarget), f32)], axis=0)
    )
    for c in range(6):
        targets[c] = jnp.broadcast_to(columns[:, c : c + 1], (ntarget, LANES))
    elapsed = elapsed_of(levels[...])
    for t in range(groups):
        spos, svel = predict(
            pos[:, tile(t)], vel[:, tile(t)], acc[:, tile(t)], jrk[:, tile(t)], elapsed[t : t + 1]
        )
        for c in range(3):
            sources[t, c] = jnp.broadcast_to(spos[c : c + 1], (8, LANES))
            sources[t, 3 + c] = jnp.broadcast_to(svel[c : c + 1], (8, LANES))
        sources[t, 6] = jnp.broadcast_to(masses[t : t + 1, :], (8, LANES))

    def one_group(g, unused):
        rows = pl.ds(pl.multiple_of(g * 8, 8), 8)
        tx, ty, tz, tu, tv, tw = (targets[c, rows, :] for c in range(6))

        def one_tile(t, carry):
            dx, dy, dz = (sources[t, 0] - tx, sources[t, 1] - ty, sources[t, 2] - tz)
            du, dv, dw = (sources[t, 3] - tu, sources[t, 4] - tv, sources[t, 5] - tw)
            r2 = dx * dx + dy * dy + dz * dz + softening_length
            inv = lax.rsqrt(r2)
            inv_sq = inv * inv
            weight = sources[t, 6] * inv * inv_sq
            radial = (dx * du + dy * dv + dz * dw) * inv_sq
            px, py, pz = (weight * dx, weight * dy, weight * dz)
            ax, ay, az, jx, jy, jz, kx, ky, kz = carry
            return (
                ax + px,
                ay + py,
                az + pz,
                jx + weight * du,
                jy + weight * dv,
                jz + weight * dw,
                kx + radial * px,
                ky + radial * py,
                kz + radial * pz,
            )

        zero = jnp.zeros((8, LANES), f32)
        ax, ay, az, jx, jy, jz, kx, ky, kz = lax.fori_loop(
            0, groups, one_tile, (zero,) * 9, unroll=16
        )
        for c, value in enumerate((ax, ay, az, jx - 3.0 * kx, jy - 3.0 * ky, jz - 3.0 * kz)):
            sums[c, rows, :] = value
        return unused

    lax.fori_loop(0, ntarget // 8, one_group, 0)
    lane = lax.broadcasted_iota(jnp.int32, (ntarget, LANES), 1)
    table = jnp.zeros((ntarget, LANES), f32)
    for c in range(6):
        table = jnp.where(lane == c, jnp.sum(sums[c], axis=1, keepdims=True), table)
    table = jnp.transpose(table)[0:8]
    row = lax.broadcasted_iota(jnp.int32, (8, ntarget), 0)
    table = jnp.where(row == 6, active[...].astype(f32), table)
    for k in range(packed.shape[0]):
        packed[k] = table


def finish_kernel(
    rows, columns, everyone, old, pos, vel, acc, jrk, levels, targets_new, stars_new
):
    groups = levels.shape[0]
    ntarget = everyone.shape[-1]
    me = lax.axis_index("ia")
    base = lax.axis_index("ja") * (groups * LANES)

    forces, where_hi, where_lo = ([], [], [])
    mine = jnp.zeros((8, ntarget), f32)
    for r in range(rows):
        total = everyone[r * columns]
        for c in range(1, columns):
            total = total + everyone[r * columns + c]
        forces.append(total)
        mine = jnp.where(me == r, total, mine)
        offset = everyone[r * columns][6:7].astype(jnp.int32) - base
        where_hi.append(offset >> 7)
        where_lo.append(offset & (LANES - 1))

    o = old[...]
    x1, v1 = correct(o[0:3], o[3:6], o[6:9], o[9:12], o[12:13], mine[0:3], mine[3:6])
    targets_new[0:3, :] = x1
    targets_new[3:6, :] = v1
    targets_new[6:12, :] = mine[0:6]

    group = lax.broadcasted_iota(jnp.int32, (groups, ntarget), 0)
    lane = lax.broadcasted_iota(jnp.int32, (LANES, ntarget), 0)
    number = lax.broadcasted_iota(jnp.int32, (groups, ntarget), 1).astype(f32) + 1.0
    spot = jnp.zeros((groups, LANES), f32)
    part = jnp.zeros((groups, LANES), f32)
    for r in range(rows):
        hit = group == where_hi[r]
        side = (lane == where_lo[r]).astype(jnp.bfloat16)
        found = lax.dot_general(
            jnp.where(hit, number, 0.0).astype(jnp.bfloat16),
            side,
            (((1,), (1,)), ((), ())),
            preferred_element_type=f32,
        )
        part = jnp.where(found > 0.5, float(r), part)
        spot = spot + found
    present = spot > 0.5
    slot = jnp.where(present, spot - 1.0, 0.0).astype(jnp.int32)
    part = jnp.where(present, part, -1.0)
    elapsed = elapsed_of(levels[...])
    for t in range(groups):
        lanes = jnp.broadcast_to(slot[t : t + 1], (8, LANES))
        holder = jnp.broadcast_to(part[t : t + 1], (8, LANES))
        new = jnp.zeros((8, LANES), f32)
        for r in range(rows):
            new = jnp.where(holder == float(r), jnp.take_along_axis(forces[r], lanes, axis=1), new)
        there = holder[0:3] > -0.5
        x0, v0, a0, j0 = (pos[:, tile(t)], vel[:, tile(t)], acc[:, tile(t)], jrk[:, tile(t)])
        a1, j1 = (new[0:3], new[3:6])
        x1, v1 = correct(x0, v0, a0, j0, elapsed[t : t + 1], a1, j1)
        stars_new[0:3, tile(t)] = jnp.where(there, x1, x0)
        stars_new[3:6, tile(t)] = jnp.where(there, v1, v0)
        stars_new[6:9, tile(t)] = jnp.where(there, a1, a0)
        stars_new[9:12, tile(t)] = jnp.where(there, j1, j0)


def local(rows, columns, positions, velocities, accels, jerks, masses, levels, active):
    nlocal = positions.shape[1]
    ntarget = active.shape[0]
    groups = nlocal // LANES
    levels = levels.reshape(groups, LANES)
    masses = masses.reshape(groups, LANES)
    active = active.reshape(1, ntarget)
    state = (positions, velocities, accels, jerks)

    mine = pl.pallas_call(
        gather_kernel,
        out_shape=jax.ShapeDtypeStruct((16, ntarget), f32),
        in_specs=[HBM] * 6,
        out_specs=VMEM,
        scratch_shapes=[
            pltpu.VMEM((16, nlocal), f32),
            pltpu.SemaphoreType.DMA((6,)),
            *(pltpu.VMEM(x.shape, x.dtype) for x in (*state, levels, active)),
        ],
        compiler_params=pltpu.CompilerParams(vmem_limit_bytes=60 * 1024 * 1024),
        name="gather",
    )(*state, levels, active)
    gathered = [mine]
    for k in range(1, columns):
        ring = [(c, (c + k) % columns) for c in range(columns)]
        gathered.append(lax.ppermute(mine, "ja", ring))
    packed, old = pl.pallas_call(
        functools.partial(force_kernel, columns),
        out_shape=(
            jax.ShapeDtypeStruct((rows * columns, 8, ntarget), f32),
            jax.ShapeDtypeStruct((16, ntarget), f32),
        ),
        in_specs=[VMEM] * (columns + 7),
        out_specs=(VMEM, VMEM),
        scratch_shapes=[
            pltpu.VMEM((groups, 7, 8, LANES), f32),
            pltpu.VMEM((6, ntarget, LANES), f32),
            pltpu.VMEM((6, ntarget, LANES), f32),
        ],
        compiler_params=PARAMS,
        name="forces",
    )(*gathered, *state, levels, masses, active)
    everyone = lax.all_to_all(packed, ("ia", "ja"), 0, 0)
    return pl.pallas_call(
        functools.partial(finish_kernel, rows, columns),
        out_shape=(
            jax.ShapeDtypeStruct((12, ntarget), f32),
            jax.ShapeDtypeStruct((12, nlocal), f32),
        ),
        in_specs=[VMEM] * 7,
        out_specs=(VMEM, VMEM),
        compiler_params=PARAMS,
        name="finish",
    )(everyone, old, *state, levels)


def solution(mesh):
    rows, columns = mesh.shape["ia"], mesh.shape["ja"]

    def body(*args):
        return local(rows, columns, *args)

    return jax.shard_map(
        body,
        mesh=mesh,
        in_specs=(
            P(None, "ja"),
            P(None, "ja"),
            P(None, "ja"),
            P(None, "ja"),
            P("ja"),
            P("ja"),
            P("ia"),
        ),
        out_specs=(P(None, "ia"), P(None, "ja")),
        check_vma=False,
    )
```

```python
import functools

import jax
import jax.numpy as jnp
from jax import lax
from jax.experimental import pallas as pl
from jax.experimental.pallas import tpu as pltpu
from jax.sharding import PartitionSpec as P

softening_length = 0.01
base_step = 0.0625
LANES = 128
PIECES = 4
f32 = jnp.float32
VMEM = pl.BlockSpec(memory_space=pltpu.VMEM)
HBM = pl.BlockSpec(memory_space=pltpu.HBM)
PARAMS = pltpu.CompilerParams(vmem_limit_bytes=24 * 1024 * 1024)


def elapsed_of(levels):
    return (128 >> levels).astype(f32) * (base_step / 128.0)


def predict(pos, vel, acc, jrk, elapsed):
    half = elapsed * elapsed * 0.5
    sixth = half * elapsed / 3.0
    pred_pos = pos + elapsed * vel + half * acc + sixth * jrk
    pred_vel = vel + elapsed * acc + half * jrk
    return (pred_pos, pred_vel)


def correct(x0, v0, a0, j0, step, a1, j1):
    quad = step * step / 12.0
    v1 = v0 + 0.5 * step * (a0 + a1) + quad * (j0 - j1)
    x1 = x0 + 0.5 * step * (v0 + v1) + quad * (a0 - a1)
    return (x1, v1)


def tile(t):
    return slice(t * LANES, (t + 1) * LANES)


def gather_kernel(*refs):
    given, out, kept, held, sems = (refs[:7], refs[7], refs[8:15], refs[15], refs[16])
    copies = [
        pltpu.make_async_copy(a, b, sems.at[n]) for n, (a, b) in enumerate(zip(given, kept))
    ]
    for copy in copies:
        copy.start()
    for copy in copies:
        copy.wait()
    pos, vel, acc, jrk, levels, masses, active = kept
    groups = levels.shape[0]
    offset = active[...] - lax.axis_index("ja") * (groups * LANES)
    group = jnp.broadcast_to(offset >> 7, (8, LANES))
    lane = jnp.broadcast_to(offset & (LANES - 1), (8, LANES))
    held[0:3, :] = pos[...]
    held[3:6, :] = vel[...]
    held[6:9, :] = acc[...]
    held[9:12, :] = jrk[...]
    elapsed = elapsed_of(levels[...])
    for t in range(groups):
        held[12:16, tile(t)] = jnp.broadcast_to(elapsed[t : t + 1], (4, LANES))
    low = jnp.zeros((8, LANES), f32)
    high = jnp.zeros((8, LANES), f32)
    for t in range(groups):
        here = group == t
        low = jnp.where(here, jnp.take_along_axis(held[0:8, tile(t)], lane, axis=1), low)
        high = jnp.where(here, jnp.take_along_axis(held[8:16, tile(t)], lane, axis=1), high)
    for k in range(out.shape[0]):
        out[k, 0:8, :] = low
        out[k, 8:16, :] = high


def force_kernel(
    gathered, pos, vel, acc, jrk, levels, masses, active, packed, old, sources, targets, sums
):
    groups = levels.shape[0]
    ntarget = active.shape[1]
    state = gathered[0]
    for k in range(1, gathered.shape[0]):
        state = state + gathered[k]
    old[...] = state
    tpos, tvel = predict(state[0:3], state[3:6], state[6:9], state[9:12], state[12:13])
    columns = jnp.transpose(
        jnp.concatenate([tpos, tvel, jnp.zeros((LANES - 6, ntarget), f32)], axis=0)
    )
    for c in range(6):
        targets[c] = jnp.broadcast_to(columns[:, c : c + 1], (ntarget, LANES))
    elapsed = elapsed_of(levels[...])
    for t in range(groups):
        spos, svel = predict(
            pos[:, tile(t)], vel[:, tile(t)], acc[:, tile(t)], jrk[:, tile(t)], elapsed[t : t + 1]
        )
        for c in range(3):
            sources[t, c] = jnp.broadcast_to(spos[c : c + 1], (8, LANES))
            sources[t, 3 + c] = jnp.broadcast_to(svel[c : c + 1], (8, LANES))
        sources[t, 6] = jnp.broadcast_to(masses[t : t + 1, :], (8, LANES))

    def one_group(g, unused):
        rows = pl.ds(pl.multiple_of(g * 8, 8), 8)
        tx, ty, tz, tu, tv, tw = (targets[c, rows, :] for c in range(6))

        def one_tile(t, carry):
            dx, dy, dz = (sources[t, 0] - tx, sources[t, 1] - ty, sources[t, 2] - tz)
            du, dv, dw = (sources[t, 3] - tu, sources[t, 4] - tv, sources[t, 5] - tw)
            r2 = dx * dx + dy * dy + dz * dz + softening_length
            inv = lax.rsqrt(r2)
            inv_sq = inv * inv
            weight = sources[t, 6] * inv * inv_sq
            radial = (dx * du + dy * dv + dz * dw) * inv_sq
            px, py, pz = (weight * dx, weight * dy, weight * dz)
            ax, ay, az, jx, jy, jz, kx, ky, kz = carry
            return (
                ax + px,
                ay + py,
                az + pz,
                jx + weight * du,
                jy + weight * dv,
                jz + weight * dw,
                kx + radial * px,
                ky + radial * py,
                kz + radial * pz,
            )

        zero = jnp.zeros((8, LANES), f32)
        ax, ay, az, jx, jy, jz, kx, ky, kz = lax.fori_loop(
            0, groups, one_tile, (zero,) * 9, unroll=16
        )
        for c, value in enumerate((ax, ay, az, jx - 3.0 * kx, jy - 3.0 * ky, jz - 3.0 * kz)):
            sums[c, rows, :] = value
        return unused

    lax.fori_loop(0, ntarget // 8, one_group, 0)
    lane = lax.broadcasted_iota(jnp.int32, (ntarget, LANES), 1)
    table = jnp.zeros((ntarget, LANES), f32)
    for c in range(6):
        table = jnp.where(lane == c, jnp.sum(sums[c], axis=1, keepdims=True), table)
    table = jnp.transpose(table)[0:8]
    row = lax.broadcasted_iota(jnp.int32, (8, ntarget), 0)
    table = jnp.where(row == 6, active[...].astype(f32), table)
    for k in range(packed.shape[0]):
        packed[k] = table


def finish_kernel(
    rows, columns, everyone, old, pos, vel, acc, jrk, levels, targets_out, stars_out,
    targets_new, stars_new, sems
):
    groups = levels.shape[0]
    ntarget = everyone.shape[-1]
    me = lax.axis_index("ia")
    base = lax.axis_index("ja") * (groups * LANES)

    forces, where_hi, where_lo = ([], [], [])
    mine = jnp.zeros((8, ntarget), f32)
    for r in range(rows):
        total = everyone[r * columns]
        for c in range(1, columns):
            total = total + everyone[r * columns + c]
        forces.append(total)
        mine = jnp.where(me == r, total, mine)
        offset = everyone[r * columns][6:7].astype(jnp.int32) - base
        where_hi.append(offset >> 7)
        where_lo.append(offset & (LANES - 1))

    o = old[...]
    x1, v1 = correct(o[0:3], o[3:6], o[6:9], o[9:12], o[12:13], mine[0:3], mine[3:6])
    targets_new[0:3, :] = x1
    targets_new[3:6, :] = v1
    targets_new[6:12, :] = mine[0:6]
    copies = [pltpu.make_async_copy(targets_new, targets_out, sems.at[0])]
    copies[0].start()
    piece = groups // PIECES

    group = lax.broadcasted_iota(jnp.int32, (groups, ntarget), 0)
    lane = lax.broadcasted_iota(jnp.int32, (LANES, ntarget), 0)
    number = lax.broadcasted_iota(jnp.int32, (groups, ntarget), 1).astype(f32) + 1.0
    spot = jnp.zeros((groups, LANES), f32)
    part = jnp.zeros((groups, LANES), f32)
    for r in range(rows):
        hit = group == where_hi[r]
        side = (lane == where_lo[r]).astype(jnp.bfloat16)
        found = lax.dot_general(
            jnp.where(hit, number, 0.0).astype(jnp.bfloat16),
            side,
            (((1,), (1,)), ((), ())),
            preferred_element_type=f32,
        )
        part = jnp.where(found > 0.5, float(r), part)
        spot = spot + found
    present = spot > 0.5
    slot = jnp.where(present, spot - 1.0, 0.0).astype(jnp.int32)
    part = jnp.where(present, part, -1.0)
    elapsed = elapsed_of(levels[...])
    for t in range(groups):
        lanes = jnp.broadcast_to(slot[t : t + 1], (8, LANES))
        holder = jnp.broadcast_to(part[t : t + 1], (8, LANES))
        new = jnp.zeros((8, LANES), f32)
        for r in range(rows):
            new = jnp.where(holder == float(r), jnp.take_along_axis(forces[r], lanes, axis=1), new)
        there = holder[0:3] > -0.5
        x0, v0, a0, j0 = (pos[:, tile(t)], vel[:, tile(t)], acc[:, tile(t)], jrk[:, tile(t)])
        a1, j1 = (new[0:3], new[3:6])
        x1, v1 = correct(x0, v0, a0, j0, elapsed[t : t + 1], a1, j1)
        stars_new[0:3, tile(t)] = jnp.where(there, x1, x0)
        stars_new[3:6, tile(t)] = jnp.where(there, v1, v0)
        stars_new[6:9, tile(t)] = jnp.where(there, a1, a0)
        stars_new[9:12, tile(t)] = jnp.where(there, j1, j0)
        if (t + 1) % piece == 0:
            part_of = (slice(None), slice((t + 1 - piece) * LANES, (t + 1) * LANES))
            copies.append(
                pltpu.make_async_copy(
                    stars_new.at[part_of], stars_out.at[part_of], sems.at[len(copies)]
                )
            )
            copies[-1].start()
    for copy in copies:
        copy.wait()


def local(rows, columns, positions, velocities, accels, jerks, masses, levels, active):
    nlocal = positions.shape[1]
    ntarget = active.shape[0]
    groups = nlocal // LANES
    given = (
        positions,
        velocities,
        accels,
        jerks,
        levels.reshape(groups, LANES),
        masses.reshape(groups, LANES),
        active.reshape(1, ntarget),
    )
    mine, *kept = pl.pallas_call(
        gather_kernel,
        out_shape=(
            pltpu.VMEM((columns, 16, ntarget), f32),
            *(pltpu.VMEM(x.shape, x.dtype) for x in given),
        ),
        in_specs=[HBM] * 7,
        out_specs=(VMEM,) * 8,
        scratch_shapes=[pltpu.VMEM((16, nlocal), f32), pltpu.SemaphoreType.DMA((7,))],
        compiler_params=PARAMS,
        name="gather",
    )(*(pltpu.with_memory_space_constraint(x, pltpu.HBM) for x in given))
    gathered = lax.all_to_all(mine, "ja", 0, 0)
    packed, old = pl.pallas_call(
        force_kernel,
        out_shape=(
            pltpu.VMEM((rows * columns, 8, ntarget), f32),
            pltpu.VMEM((16, ntarget), f32),
        ),
        in_specs=[VMEM] * 8,
        out_specs=(VMEM, VMEM),
        scratch_shapes=[
            pltpu.VMEM((groups, 7, 8, LANES), f32),
            pltpu.VMEM((6, ntarget, LANES), f32),
            pltpu.VMEM((6, ntarget, LANES), f32),
        ],
        compiler_params=PARAMS,
        name="forces",
    )(gathered, *kept)
    everyone = lax.all_to_all(packed, ("ia", "ja"), 0, 0)
    return pl.pallas_call(
        functools.partial(finish_kernel, rows, columns),
        out_shape=(
            jax.ShapeDtypeStruct((12, ntarget), f32),
            jax.ShapeDtypeStruct((12, nlocal), f32),
        ),
        in_specs=[VMEM] * 7,
        out_specs=(HBM, HBM),
        scratch_shapes=[
            pltpu.VMEM((12, ntarget), f32),
            pltpu.VMEM((12, nlocal), f32),
            pltpu.SemaphoreType.DMA((1 + PIECES,)),
        ],
        compiler_params=PARAMS,
        name="finish",
    )(everyone, old, *kept[:5])


def solution(mesh):
    rows, columns = mesh.shape["ia"], mesh.shape["ja"]

    def body(*args):
        return local(rows, columns, *args)

    return jax.shard_map(
        body,
        mesh=mesh,
        in_specs=(
            P(None, "ja"),
            P(None, "ja"),
            P(None, "ja"),
            P(None, "ja"),
            P("ja"),
            P("ja"),
            P("ia"),
        ),
        out_specs=(P(None, "ia"), P(None, "ja")),
        check_vma=False,
    )
```

```python
import functools

import jax
import jax.numpy as jnp
from jax import lax
from jax.experimental import pallas as pl
from jax.experimental.pallas import tpu as pltpu
from jax.sharding import PartitionSpec as P

softening_length = 0.01
base_step = 0.0625
LANES = 128
PIECES = 4
CHUNK = 16
f32 = jnp.float32
VMEM = pl.BlockSpec(memory_space=pltpu.VMEM)
HBM = pl.BlockSpec(memory_space=pltpu.HBM)
PARAMS = pltpu.CompilerParams(vmem_limit_bytes=24 * 1024 * 1024)


def elapsed_of(levels):
    return (128 >> levels).astype(f32) * (base_step / 128.0)


def predict(pos, vel, acc, jrk, elapsed):
    half = elapsed * elapsed * 0.5
    sixth = half * elapsed / 3.0
    pred_pos = pos + elapsed * vel + half * acc + sixth * jrk
    pred_vel = vel + elapsed * acc + half * jrk
    return (pred_pos, pred_vel)


def correct(x0, v0, a0, j0, step, a1, j1):
    quad = step * step / 12.0
    v1 = v0 + 0.5 * step * (a0 + a1) + quad * (j0 - j1)
    x1 = x0 + 0.5 * step * (v0 + v1) + quad * (a0 - a1)
    return (x1, v1)


def tile(t):
    return slice(t * LANES, (t + 1) * LANES)


def gather_kernel(*refs):
    given, out, kept, held, sems = (refs[:7], refs[7], refs[8:15], refs[15], refs[16])
    copies = [
        pltpu.make_async_copy(a, b, sems.at[n]) for n, (a, b) in enumerate(zip(given, kept))
    ]
    for copy in copies:
        copy.start()
    for copy in copies:
        copy.wait()
    pos, vel, acc, jrk, levels, masses, active = kept
    groups = levels.shape[0]
    offset = active[...] - lax.axis_index("ja") * (groups * LANES)
    group = jnp.broadcast_to(offset >> 7, (8, LANES))
    lane = jnp.broadcast_to(offset & (LANES - 1), (8, LANES))
    held[0:3, :] = pos[...]
    held[3:6, :] = vel[...]
    held[6:9, :] = acc[...]
    held[9:12, :] = jrk[...]
    elapsed = elapsed_of(levels[...])
    for t in range(groups):
        held[12:16, tile(t)] = jnp.broadcast_to(elapsed[t : t + 1], (4, LANES))
    low = jnp.zeros((8, LANES), f32)
    high = jnp.zeros((8, LANES), f32)
    for t in range(groups):
        here = group == t
        low = jnp.where(here, jnp.take_along_axis(held[0:8, tile(t)], lane, axis=1), low)
        high = jnp.where(here, jnp.take_along_axis(held[8:16, tile(t)], lane, axis=1), high)
    for k in range(out.shape[0]):
        out[k, 0:8, :] = low
        out[k, 8:16, :] = high


def force_kernel(
    gathered, pos, vel, acc, jrk, levels, masses, active, packed, old, sources, targets, sums,
    even, odd
):
    groups = levels.shape[0]
    ntarget = active.shape[1]
    state = gathered[0]
    for k in range(1, gathered.shape[0]):
        state = state + gathered[k]
    old[...] = state
    tpos, tvel = predict(state[0:3], state[3:6], state[6:9], state[9:12], state[12:13])
    columns = jnp.transpose(
        jnp.concatenate([tpos, tvel, jnp.zeros((LANES - 6, ntarget), f32)], axis=0)
    )
    for c in range(6):
        targets[c] = jnp.broadcast_to(columns[:, c : c + 1], (ntarget, LANES))
    elapsed = elapsed_of(levels[...])
    for t in range(groups):
        spos, svel = predict(
            pos[:, tile(t)], vel[:, tile(t)], acc[:, tile(t)], jrk[:, tile(t)], elapsed[t : t + 1]
        )
        for c in range(3):
            sources[t, c] = jnp.broadcast_to(spos[c : c + 1], (8, LANES))
            sources[t, 3 + c] = jnp.broadcast_to(svel[c : c + 1], (8, LANES))
        sources[t, 6] = jnp.broadcast_to(masses[t : t + 1, :], (8, LANES))

    def rows_of(g):
        return pl.ds(pl.multiple_of(g * 8, 8), 8)

    def first_stage(t, place, held):
        dx, dy, dz = (sources[t, c] - place[c] for c in range(3))
        held[t, 0], held[t, 1], held[t, 2] = (dx, dy, dz)
        held[t, 3] = lax.rsqrt(dx * dx + dy * dy + dz * dz + softening_length)

    def second_stage(t, speed, held, carry):
        dx, dy, dz, inv = (held[t, c] for c in range(4))
        du, dv, dw = (sources[t, 3 + c] - speed[c] for c in range(3))
        inv_sq = inv * inv
        weight = sources[t, 6] * inv * inv_sq
        radial = (dx * du + dy * dv + dz * dw) * inv_sq
        px, py, pz = (weight * dx, weight * dy, weight * dz)
        terms = (
            *(px, py, pz),
            *(weight * du, weight * dv, weight * dw),
            *(radial * px, radial * py, radial * pz),
        )
        return tuple(total + term for total, term in zip(carry, terms))

    def stages(g, later, earlier):
        if later is not None:
            place = [targets[c, rows_of(g), :] for c in range(3)]
        if earlier is not None:
            speed = [targets[3 + c, rows_of(g - 1), :] for c in range(3)]

        def some_tiles(n, carry):
            for k in range(CHUNK):
                t = n * CHUNK + k
                if earlier is not None:
                    carry = second_stage(t, speed, earlier, carry)
                if later is not None:
                    first_stage(t, place, later)
            return carry

        zero = jnp.zeros((8, LANES), f32)
        ax, ay, az, jx, jy, jz, kx, ky, kz = lax.fori_loop(
            0, groups // CHUNK, some_tiles, (zero,) * 9
        )
        if earlier is not None:
            forces = (ax, ay, az, jx - 3.0 * kx, jy - 3.0 * ky, jz - 3.0 * kz)
            for c, value in enumerate(forces):
                sums[c, rows_of(g - 1), :] = value

    def two_groups(n, unused):
        stages(2 * n + 1, odd, even)
        stages(2 * n + 2, even, odd)
        return unused

    last = ntarget // 8
    stages(0, even, None)
    lax.fori_loop(0, last // 2 - 1, two_groups, 0)
    stages(last - 1, odd, even)
    stages(last, None, odd)
    lane = lax.broadcasted_iota(jnp.int32, (ntarget, LANES), 1)
    table = jnp.zeros((ntarget, LANES), f32)
    for c in range(6):
        table = jnp.where(lane == c, jnp.sum(sums[c], axis=1, keepdims=True), table)
    table = jnp.transpose(table)[0:8]
    row = lax.broadcasted_iota(jnp.int32, (8, ntarget), 0)
    table = jnp.where(row == 6, active[...].astype(f32), table)
    for k in range(packed.shape[0]):
        packed[k] = table


def finish_kernel(
    rows, columns, everyone, old, pos, vel, acc, jrk, levels, targets_out, stars_out,
    targets_new, stars_new, sems
):
    groups = levels.shape[0]
    ntarget = everyone.shape[-1]
    me = lax.axis_index("ia")
    base = lax.axis_index("ja") * (groups * LANES)

    forces, where_hi, where_lo = ([], [], [])
    mine = jnp.zeros((8, ntarget), f32)
    for r in range(rows):
        total = everyone[r]
        for c in range(1, columns):
            total = total + everyone[c * rows + r]
        forces.append(total)
        mine = jnp.where(me == r, total, mine)
        offset = everyone[r][6:7].astype(jnp.int32) - base
        where_hi.append(offset >> 7)
        where_lo.append(offset & (LANES - 1))

    o = old[...]
    x1, v1 = correct(o[0:3], o[3:6], o[6:9], o[9:12], o[12:13], mine[0:3], mine[3:6])
    targets_new[0:3, :] = x1
    targets_new[3:6, :] = v1
    targets_new[6:12, :] = mine[0:6]
    copies = [pltpu.make_async_copy(targets_new, targets_out, sems.at[0])]
    copies[0].start()
    piece = groups // PIECES

    group = lax.broadcasted_iota(jnp.int32, (groups, ntarget), 0)
    lane = lax.broadcasted_iota(jnp.int32, (LANES, ntarget), 0)
    number = lax.broadcasted_iota(jnp.int32, (groups, ntarget), 1).astype(f32) + 1.0
    spot = jnp.zeros((groups, LANES), f32)
    part = jnp.zeros((groups, LANES), f32)
    for r in range(rows):
        hit = group == where_hi[r]
        side = (lane == where_lo[r]).astype(jnp.bfloat16)
        found = lax.dot_general(
            jnp.where(hit, number, 0.0).astype(jnp.bfloat16),
            side,
            (((1,), (1,)), ((), ())),
            preferred_element_type=f32,
        )
        part = jnp.where(found > 0.5, float(r), part)
        spot = spot + found
    present = spot > 0.5
    slot = jnp.where(present, spot - 1.0, 0.0).astype(jnp.int32)
    part = jnp.where(present, part, -1.0)
    elapsed = elapsed_of(levels[...])
    for t in range(groups):
        lanes = jnp.broadcast_to(slot[t : t + 1], (8, LANES))
        holder = jnp.broadcast_to(part[t : t + 1], (8, LANES))
        new = jnp.zeros((8, LANES), f32)
        for r in range(rows):
            new = jnp.where(holder == float(r), jnp.take_along_axis(forces[r], lanes, axis=1), new)
        there = holder[0:3] > -0.5
        x0, v0, a0, j0 = (pos[:, tile(t)], vel[:, tile(t)], acc[:, tile(t)], jrk[:, tile(t)])
        a1, j1 = (new[0:3], new[3:6])
        x1, v1 = correct(x0, v0, a0, j0, elapsed[t : t + 1], a1, j1)
        stars_new[0:3, tile(t)] = jnp.where(there, x1, x0)
        stars_new[3:6, tile(t)] = jnp.where(there, v1, v0)
        stars_new[6:9, tile(t)] = jnp.where(there, a1, a0)
        stars_new[9:12, tile(t)] = jnp.where(there, j1, j0)
        if (t + 1) % piece == 0:
            part_of = (slice(None), slice((t + 1 - piece) * LANES, (t + 1) * LANES))
            copies.append(
                pltpu.make_async_copy(
                    stars_new.at[part_of], stars_out.at[part_of], sems.at[len(copies)]
                )
            )
            copies[-1].start()
    for copy in copies:
        copy.wait()


def local(rows, columns, positions, velocities, accels, jerks, masses, levels, active):
    nlocal = positions.shape[1]
    ntarget = active.shape[0]
    groups = nlocal // LANES
    given = (
        positions,
        velocities,
        accels,
        jerks,
        levels.reshape(groups, LANES),
        masses.reshape(groups, LANES),
        active.reshape(1, ntarget),
    )
    mine, *kept = pl.pallas_call(
        gather_kernel,
        out_shape=(
            pltpu.VMEM((columns, 16, ntarget), f32),
            *(pltpu.VMEM(x.shape, x.dtype) for x in given),
        ),
        in_specs=[HBM] * 7,
        out_specs=(VMEM,) * 8,
        scratch_shapes=[pltpu.VMEM((16, nlocal), f32), pltpu.SemaphoreType.DMA((7,))],
        compiler_params=PARAMS,
        name="gather",
    )(*(pltpu.with_memory_space_constraint(x, pltpu.HBM) for x in given))
    gathered = lax.all_to_all(mine, "ja", 0, 0)
    packed, old = pl.pallas_call(
        force_kernel,
        out_shape=(
            pltpu.VMEM((rows * columns, 8, ntarget), f32),
            pltpu.VMEM((16, ntarget), f32),
        ),
        in_specs=[VMEM] * 8,
        out_specs=(VMEM, VMEM),
        scratch_shapes=[
            pltpu.VMEM((groups, 7, 8, LANES), f32),
            pltpu.VMEM((6, ntarget, LANES), f32),
            pltpu.VMEM((6, ntarget, LANES), f32),
            pltpu.VMEM((groups, 4, 8, LANES), f32),
            pltpu.VMEM((groups, 4, 8, LANES), f32),
        ],
        compiler_params=PARAMS,
        name="forces",
    )(gathered, *kept)
    everyone = lax.all_to_all(packed, ("ja", "ia"), 0, 0)
    return pl.pallas_call(
        functools.partial(finish_kernel, rows, columns),
        out_shape=(
            jax.ShapeDtypeStruct((12, ntarget), f32),
            jax.ShapeDtypeStruct((12, nlocal), f32),
        ),
        in_specs=[VMEM] * 7,
        out_specs=(HBM, HBM),
        scratch_shapes=[
            pltpu.VMEM((12, ntarget), f32),
            pltpu.VMEM((12, nlocal), f32),
            pltpu.SemaphoreType.DMA((1 + PIECES,)),
        ],
        compiler_params=PARAMS,
        name="finish",
    )(everyone, old, *kept[:5])


def solution(mesh):
    rows, columns = mesh.shape["ia"], mesh.shape["ja"]

    def body(*args):
        return local(rows, columns, *args)

    return jax.shard_map(
        body,
        mesh=mesh,
        in_specs=(
            P(None, "ja"),
            P(None, "ja"),
            P(None, "ja"),
            P(None, "ja"),
            P("ja"),
            P("ja"),
            P("ia"),
        ),
        out_specs=(P(None, "ia"), P(None, "ja")),
        check_vma=False,
    )
```

```python
import functools

import jax
import jax.numpy as jnp
from jax import lax
from jax.experimental import pallas as pl
from jax.experimental.pallas import tpu as pltpu
from jax.sharding import PartitionSpec as P

softening_length = 0.01
base_step = 0.0625
LANES = 128
PIECES = 4
OLD_ROWS = 13
NEW_ROWS = 7
f32 = jnp.float32
VMEM = pl.BlockSpec(memory_space=pltpu.VMEM)
HBM = pl.BlockSpec(memory_space=pltpu.HBM)
PARAMS = pltpu.CompilerParams(vmem_limit_bytes=24 * 1024 * 1024)


def elapsed_of(levels):
    return (128 >> levels).astype(f32) * (base_step / 128.0)


def predict(pos, vel, acc, jrk, elapsed):
    half = elapsed * elapsed * 0.5
    sixth = half * elapsed / 3.0
    pred_pos = pos + elapsed * vel + half * acc + sixth * jrk
    pred_vel = vel + elapsed * acc + half * jrk
    return (pred_pos, pred_vel)


def correct(x0, v0, a0, j0, step, a1, j1):
    quad = step * step / 12.0
    v1 = v0 + 0.5 * step * (a0 + a1) + quad * (j0 - j1)
    x1 = x0 + 0.5 * step * (v0 + v1) + quad * (a0 - a1)
    return (x1, v1)


def tile(t):
    return slice(t * LANES, (t + 1) * LANES)


def gather_kernel(*refs):
    given, out, kept, held, sems = (refs[:7], refs[7], refs[8:15], refs[15], refs[16])
    copies = [
        pltpu.make_async_copy(a, b, sems.at[n]) for n, (a, b) in enumerate(zip(given, kept))
    ]
    for copy in copies:
        copy.start()
    for copy in copies:
        copy.wait()
    pos, vel, acc, jrk, levels, masses, active = kept
    groups = levels.shape[0]
    offset = active[...] - lax.axis_index("ja") * (groups * LANES)
    group = jnp.broadcast_to(offset >> 7, (8, LANES))
    lane = jnp.broadcast_to(offset & (LANES - 1), (8, LANES))
    held[0:3, :] = pos[...]
    held[3:6, :] = vel[...]
    held[6:9, :] = acc[...]
    held[9:12, :] = jrk[...]
    elapsed = elapsed_of(levels[...])
    for t in range(groups):
        held[12:16, tile(t)] = jnp.broadcast_to(elapsed[t : t + 1], (4, LANES))
    low = jnp.zeros((8, LANES), f32)
    high = jnp.zeros((8, LANES), f32)
    for t in range(groups):
        here = group == t
        low = jnp.where(here, jnp.take_along_axis(held[0:8, tile(t)], lane, axis=1), low)
        high = jnp.where(here, jnp.take_along_axis(held[8:16, tile(t)], lane, axis=1), high)
    for k in range(out.shape[0]):
        for c in range(OLD_ROWS):
            out[k, :, tile(c)] = (low if c < 8 else high)[c % 8 : c % 8 + 1]


def force_kernel(
    gathered, pos, vel, acc, jrk, levels, masses, active, packed, old, sources, targets, sums
):
    groups = levels.shape[0]
    ntarget = active.shape[1]
    flat = gathered[0]
    for k in range(1, gathered.shape[0]):
        flat = flat + gathered[k]
    for c in range(OLD_ROWS):
        old[c : c + 1, :] = flat[:, tile(c)]
    state = old[...]
    tpos, tvel = predict(state[0:3], state[3:6], state[6:9], state[9:12], state[12:13])
    columns = jnp.transpose(
        jnp.concatenate([tpos, tvel, jnp.zeros((LANES - 6, ntarget), f32)], axis=0)
    )
    for c in range(6):
        targets[c] = jnp.broadcast_to(columns[:, c : c + 1], (ntarget, LANES))
    elapsed = elapsed_of(levels[...])
    for t in range(groups):
        spos, svel = predict(
            pos[:, tile(t)], vel[:, tile(t)], acc[:, tile(t)], jrk[:, tile(t)], elapsed[t : t + 1]
        )
        for c in range(3):
            sources[t, c] = jnp.broadcast_to(spos[c : c + 1], (8, LANES))
            sources[t, 3 + c] = jnp.broadcast_to(svel[c : c + 1], (8, LANES))
        sources[t, 6] = jnp.broadcast_to(masses[t : t + 1, :], (8, LANES))

    def one_group(g, unused):
        rows = pl.ds(pl.multiple_of(g * 8, 8), 8)
        tx, ty, tz, tu, tv, tw = (targets[c, rows, :] for c in range(6))

        def one_tile(t, carry):
            dx, dy, dz = (sources[t, 0] - tx, sources[t, 1] - ty, sources[t, 2] - tz)
            du, dv, dw = (sources[t, 3] - tu, sources[t, 4] - tv, sources[t, 5] - tw)
            r2 = dx * dx + dy * dy + dz * dz + softening_length
            inv = lax.rsqrt(r2)
            inv_sq = inv * inv
            weight = sources[t, 6] * inv * inv_sq
            radial = (dx * du + dy * dv + dz * dw) * inv_sq
            px, py, pz = (weight * dx, weight * dy, weight * dz)
            ax, ay, az, jx, jy, jz, kx, ky, kz = carry
            return (
                ax + px,
                ay + py,
                az + pz,
                jx + weight * du,
                jy + weight * dv,
                jz + weight * dw,
                kx + radial * px,
                ky + radial * py,
                kz + radial * pz,
            )

        zero = jnp.zeros((8, LANES), f32)
        ax, ay, az, jx, jy, jz, kx, ky, kz = lax.fori_loop(
            0, groups, one_tile, (zero,) * 9, unroll=32
        )
        for c, value in enumerate((ax, ay, az, jx - 3.0 * kx, jy - 3.0 * ky, jz - 3.0 * kz)):
            sums[c, rows, :] = value
        return unused

    lax.fori_loop(0, ntarget // 8, one_group, 0)
    lane = lax.broadcasted_iota(jnp.int32, (ntarget, LANES), 1)
    table = jnp.zeros((ntarget, LANES), f32)
    for c in range(6):
        table = jnp.where(lane == c, jnp.sum(sums[c], axis=1, keepdims=True), table)
    table = jnp.transpose(table)[0:8]
    row = lax.broadcasted_iota(jnp.int32, (8, ntarget), 0)
    table = jnp.where(row == 6, active[...].astype(f32), table)
    for k in range(packed.shape[0]):
        for c in range(NEW_ROWS):
            packed[k, :, tile(c)] = table[c : c + 1]


def finish_kernel(
    rows, columns, everyone, old, pos, vel, acc, jrk, levels, targets_out, stars_out,
    targets_new, stars_new, rowed, sems
):
    groups = levels.shape[0]
    ntarget = old.shape[1]
    me = lax.axis_index("ia")
    base = lax.axis_index("ja") * (groups * LANES)

    forces, where_hi, where_lo = ([], [], [])
    mine = jnp.zeros((8, ntarget), f32)
    for r in range(rows):
        total = everyone[r * columns]
        for c in range(1, columns):
            total = total + everyone[r * columns + c]
        for c in range(6):
            rowed[r, c : c + 1, :] = total[:, tile(c)]
        forces.append(rowed[r])
        mine = jnp.where(me == r, forces[r], mine)
        offset = everyone[r * columns][:, tile(6)].astype(jnp.int32) - base
        where_hi.append(offset >> 7)
        where_lo.append(offset & (LANES - 1))

    o = old[...]
    x1, v1 = correct(o[0:3], o[3:6], o[6:9], o[9:12], o[12:13], mine[0:3], mine[3:6])
    targets_new[0:3, :] = x1
    targets_new[3:6, :] = v1
    targets_new[6:12, :] = mine[0:6]
    copies = [pltpu.make_async_copy(targets_new, targets_out, sems.at[0])]
    copies[0].start()
    piece = groups // PIECES

    group = lax.broadcasted_iota(jnp.int32, (groups, ntarget), 0)
    lane = lax.broadcasted_iota(jnp.int32, (LANES, ntarget), 0)
    number = lax.broadcasted_iota(jnp.int32, (groups, ntarget), 1).astype(f32) + 1.0
    spot = jnp.zeros((groups, LANES), f32)
    part = jnp.zeros((groups, LANES), f32)
    for r in range(rows):
        hit = group == where_hi[r]
        side = (lane == where_lo[r]).astype(jnp.bfloat16)
        found = lax.dot_general(
            jnp.where(hit, number, 0.0).astype(jnp.bfloat16),
            side,
            (((1,), (1,)), ((), ())),
            preferred_element_type=f32,
        )
        part = jnp.where(found > 0.5, float(r), part)
        spot = spot + found
    present = spot > 0.5
    slot = jnp.where(present, spot - 1.0, 0.0).astype(jnp.int32)
    part = jnp.where(present, part, -1.0)
    elapsed = elapsed_of(levels[...])
    for t in range(groups):
        lanes = jnp.broadcast_to(slot[t : t + 1], (8, LANES))
        holder = jnp.broadcast_to(part[t : t + 1], (8, LANES))
        new = jnp.zeros((8, LANES), f32)
        for r in range(rows):
            new = jnp.where(holder == float(r), jnp.take_along_axis(forces[r], lanes, axis=1), new)
        there = holder[0:3] > -0.5
        x0, v0, a0, j0 = (pos[:, tile(t)], vel[:, tile(t)], acc[:, tile(t)], jrk[:, tile(t)])
        a1, j1 = (new[0:3], new[3:6])
        x1, v1 = correct(x0, v0, a0, j0, elapsed[t : t + 1], a1, j1)
        stars_new[0:3, tile(t)] = jnp.where(there, x1, x0)
        stars_new[3:6, tile(t)] = jnp.where(there, v1, v0)
        stars_new[6:9, tile(t)] = jnp.where(there, a1, a0)
        stars_new[9:12, tile(t)] = jnp.where(there, j1, j0)
        if (t + 1) % piece == 0:
            part_of = (slice(None), slice((t + 1 - piece) * LANES, (t + 1) * LANES))
            copies.append(
                pltpu.make_async_copy(
                    stars_new.at[part_of], stars_out.at[part_of], sems.at[len(copies)]
                )
            )
            copies[-1].start()
    for copy in copies:
        copy.wait()


def local(rows, columns, positions, velocities, accels, jerks, masses, levels, active):
    nlocal = positions.shape[1]
    ntarget = active.shape[0]
    groups = nlocal // LANES
    given = (
        positions,
        velocities,
        accels,
        jerks,
        levels.reshape(groups, LANES),
        masses.reshape(groups, LANES),
        active.reshape(1, ntarget),
    )
    mine, *kept = pl.pallas_call(
        gather_kernel,
        out_shape=(
            pltpu.VMEM((columns, 1, OLD_ROWS * ntarget), f32),
            *(pltpu.VMEM(x.shape, x.dtype) for x in given),
        ),
        in_specs=[HBM] * 7,
        out_specs=(VMEM,) * 8,
        scratch_shapes=[pltpu.VMEM((16, nlocal), f32), pltpu.SemaphoreType.DMA((7,))],
        compiler_params=PARAMS,
        name="gather",
    )(*(pltpu.with_memory_space_constraint(x, pltpu.HBM) for x in given))
    gathered = lax.all_to_all(mine, "ja", 0, 0)
    packed, old = pl.pallas_call(
        force_kernel,
        out_shape=(
            pltpu.VMEM((rows * columns, 1, NEW_ROWS * ntarget), f32),
            pltpu.VMEM((16, ntarget), f32),
        ),
        in_specs=[VMEM] * 8,
        out_specs=(VMEM, VMEM),
        scratch_shapes=[
            pltpu.VMEM((groups, 7, 8, LANES), f32),
            pltpu.VMEM((6, ntarget, LANES), f32),
            pltpu.VMEM((6, ntarget, LANES), f32),
        ],
        compiler_params=PARAMS,
        name="forces",
    )(gathered, *kept)
    everyone = lax.all_to_all(packed, ("ia", "ja"), 0, 0)
    return pl.pallas_call(
        functools.partial(finish_kernel, rows, columns),
        out_shape=(
            jax.ShapeDtypeStruct((12, ntarget), f32),
            jax.ShapeDtypeStruct((12, nlocal), f32),
        ),
        in_specs=[VMEM] * 7,
        out_specs=(HBM, HBM),
        scratch_shapes=[
            pltpu.VMEM((12, ntarget), f32),
            pltpu.VMEM((12, nlocal), f32),
            pltpu.VMEM((rows, 8, ntarget), f32),
            pltpu.SemaphoreType.DMA((1 + PIECES,)),
        ],
        compiler_params=PARAMS,
        name="finish",
    )(everyone, old, *kept[:5])


def solution(mesh):
    rows, columns = mesh.shape["ia"], mesh.shape["ja"]

    def body(*args):
        return local(rows, columns, *args)

    return jax.shard_map(
        body,
        mesh=mesh,
        in_specs=(
            P(None, "ja"),
            P(None, "ja"),
            P(None, "ja"),
            P(None, "ja"),
            P("ja"),
            P("ja"),
            P("ia"),
        ),
        out_specs=(P(None, "ia"), P(None, "ja")),
        check_vma=False,
    )
```

```python
import functools

import jax
import jax.numpy as jnp
from jax import lax
from jax.experimental import pallas as pl
from jax.experimental.pallas import tpu as pltpu
from jax.sharding import PartitionSpec as P

softening_length = 0.01
base_step = 0.0625
LANES = 128
PIECES = 4
NEW_ROWS = 7
f32 = jnp.float32
VMEM = pl.BlockSpec(memory_space=pltpu.VMEM)
HBM = pl.BlockSpec(memory_space=pltpu.HBM)
PARAMS = pltpu.CompilerParams(vmem_limit_bytes=24 * 1024 * 1024)


def elapsed_of(levels):
    return (128 >> levels).astype(f32) * (base_step / 128.0)


def step_factors(elapsed):
    half = elapsed * elapsed * 0.5
    return (elapsed, half, half * elapsed * (1.0 / 3.0))


def predict(pos, vel, acc, jrk, factors):
    elapsed, half, sixth = factors
    pred_pos = pos + elapsed * vel + half * acc + sixth * jrk
    pred_vel = vel + elapsed * acc + half * jrk
    return (pred_pos, pred_vel)


def correction_factors(step):
    return (0.5 * step, step * step * (1.0 / 12.0))


def correct(x0, v0, a0, j0, factors, a1, j1):
    half, quad = factors
    v1 = v0 + half * (a0 + a1) + quad * (j0 - j1)
    x1 = x0 + half * (v0 + v1) + quad * (a0 - a1)
    return (x1, v1)


def tile(t):
    return slice(t * LANES, (t + 1) * LANES)


def gather_kernel(*refs):
    given, out, kept, sems = (refs[:7], refs[7], refs[8:15], refs[15])
    pos, vel, acc, jrk, levels, masses, active = kept
    groups = levels.shape[0]
    half = groups // 2

    def copy_of(n, sem, columns=None):
        if columns is None:
            return pltpu.make_async_copy(given[n], kept[n], sems.at[sem])
        part = (slice(None), columns)
        return pltpu.make_async_copy(given[n].at[part], kept[n].at[part], sems.at[sem])

    small = [copy_of(6, 0), copy_of(4, 1)]
    parts = [
        [copy_of(n, 2 + 4 * h + n, slice(h * half * LANES, (h + 1) * half * LANES)) for n in range(4)]
        for h in range(2)
    ]
    late = copy_of(5, 10)
    for copy in (*small, *parts[0], *parts[1], late):
        copy.start()
    for copy in small:
        copy.wait()
    offset = active[...] - lax.axis_index("ja") * (groups * LANES)
    group = jnp.broadcast_to(offset >> 7, (8, LANES))
    lane = jnp.broadcast_to(offset & (LANES - 1), (8, LANES))
    row = lax.broadcasted_iota(jnp.int32, (8, LANES), 0)
    elapsed = elapsed_of(levels[...])
    steps = jnp.zeros((8, LANES), f32)
    for t in range(0, groups, 8):
        here = group == row + t
        steps = jnp.where(here, jnp.take_along_axis(elapsed[t : t + 8], lane, axis=1), steps)
    found = [jnp.zeros((3, LANES), f32)] * 4
    for h in range(2):
        for copy in parts[h]:
            copy.wait()
        for t in range(h * half, (h + 1) * half):
            here = group[0:3] == t
            found = [
                jnp.where(here, jnp.take_along_axis(x[:, tile(t)], lane[0:3], axis=1), old)
                for x, old in zip((pos, vel, acc, jrk), found)
            ]
    steps = jnp.broadcast_to(jnp.sum(steps, axis=0, keepdims=True), (4, LANES))
    for k in range(out.shape[0]):
        for n, value in enumerate(found):
            out[k, 3 * n : 3 * n + 3, :] = value
        out[k, 12:16, :] = steps
    late.wait()


def force_kernel(
    gathered, pos, vel, acc, jrk, levels, masses, active, packed, old, sources, targets, sums
):
    groups = levels.shape[0]
    ntarget = active.shape[1]
    state = gathered[0]
    for k in range(1, gathered.shape[0]):
        state = state + gathered[k]
    old[...] = state
    tpos, tvel = predict(
        state[0:3], state[3:6], state[6:9], state[9:12], step_factors(state[12:13])
    )
    columns = jnp.transpose(
        jnp.concatenate([tpos, tvel, jnp.zeros((LANES - 6, ntarget), f32)], axis=0)
    )
    for c in range(6):
        targets[c] = jnp.broadcast_to(columns[:, c : c + 1], (ntarget, LANES))
    factors = step_factors(elapsed_of(levels[...]))
    for t in range(groups):
        spos, svel = predict(
            *(x[:, tile(t)] for x in (pos, vel, acc, jrk)), [f[t : t + 1] for f in factors]
        )
        for c in range(3):
            sources[t, c] = jnp.broadcast_to(spos[c : c + 1], (8, LANES))
            sources[t, 3 + c] = jnp.broadcast_to(svel[c : c + 1], (8, LANES))
        sources[t, 6] = jnp.broadcast_to(masses[t : t + 1, :], (8, LANES))

    def one_group(g, unused):
        rows = pl.ds(pl.multiple_of(g * 8, 8), 8)
        tx, ty, tz, tu, tv, tw = (targets[c, rows, :] for c in range(6))

        def one_tile(t, carry):
            dx, dy, dz = (sources[t, 0] - tx, sources[t, 1] - ty, sources[t, 2] - tz)
            du, dv, dw = (sources[t, 3] - tu, sources[t, 4] - tv, sources[t, 5] - tw)
            r2 = dx * dx + dy * dy + dz * dz + softening_length
            inv = lax.rsqrt(r2)
            inv_sq = pl.reciprocal(r2, approx=True)
            weight = sources[t, 6] * inv * inv_sq
            radial = (dx * du + dy * dv + dz * dw) * inv_sq
            px, py, pz = (weight * dx, weight * dy, weight * dz)
            ax, ay, az, jx, jy, jz, kx, ky, kz = carry
            return (
                ax + px,
                ay + py,
                az + pz,
                jx + weight * du,
                jy + weight * dv,
                jz + weight * dw,
                kx + radial * px,
                ky + radial * py,
                kz + radial * pz,
            )

        zero = jnp.zeros((8, LANES), f32)
        ax, ay, az, jx, jy, jz, kx, ky, kz = lax.fori_loop(
            0, groups, one_tile, (zero,) * 9, unroll=32
        )
        for c, value in enumerate((ax, ay, az, jx - 3.0 * kx, jy - 3.0 * ky, jz - 3.0 * kz)):
            sums[c, rows, :] = value
        return unused

    lax.fori_loop(0, ntarget // 8, one_group, 0)
    lane = lax.broadcasted_iota(jnp.int32, (ntarget, LANES), 1)
    table = jnp.zeros((ntarget, LANES), f32)
    for c in range(6):
        table = jnp.where(lane == c, jnp.sum(sums[c], axis=1, keepdims=True), table)
    table = jnp.transpose(table)[0:8]
    row = lax.broadcasted_iota(jnp.int32, (8, ntarget), 0)
    table = jnp.where(row == 6, active[...].astype(f32), table)
    for k in range(packed.shape[0]):
        for c in range(NEW_ROWS):
            packed[k, :, tile(c)] = table[c : c + 1]


def finish_kernel(
    rows, columns, everyone, old, pos, vel, acc, jrk, levels, targets_out, stars_out,
    targets_new, stars_new, rowed, sems
):
    groups = levels.shape[0]
    ntarget = old.shape[1]
    me = lax.axis_index("ia")
    base = lax.axis_index("ja") * (groups * LANES)

    forces, where_hi, where_lo = ([], [], [])
    mine = jnp.zeros((8, ntarget), f32)
    for r in range(rows):
        total = everyone[r * columns]
        for c in range(1, columns):
            total = total + everyone[r * columns + c]
        for c in range(6):
            rowed[r, c : c + 1, :] = total[:, tile(c)]
        forces.append(rowed[r])
        mine = jnp.where(me == r, forces[r], mine)
        offset = everyone[r * columns][:, tile(6)].astype(jnp.int32) - base
        where_hi.append(offset >> 7)
        where_lo.append(offset & (LANES - 1))

    o = old[...]
    factors = correction_factors(o[12:13])
    x1, v1 = correct(o[0:3], o[3:6], o[6:9], o[9:12], factors, mine[0:3], mine[3:6])
    targets_new[0:3, :] = x1
    targets_new[3:6, :] = v1
    targets_new[6:12, :] = mine[0:6]
    copies = [pltpu.make_async_copy(targets_new, targets_out, sems.at[0])]
    copies[0].start()
    piece = groups // PIECES

    group = lax.broadcasted_iota(jnp.int32, (groups, ntarget), 0)
    lane = lax.broadcasted_iota(jnp.int32, (LANES, ntarget), 0)
    number = lax.broadcasted_iota(jnp.int32, (groups, ntarget), 1).astype(f32) + 1.0
    spot = jnp.zeros((groups, LANES), f32)
    part = jnp.zeros((groups, LANES), f32)
    for r in range(rows):
        hit = group == where_hi[r]
        side = (lane == where_lo[r]).astype(jnp.bfloat16)
        found = lax.dot_general(
            jnp.where(hit, number, 0.0).astype(jnp.bfloat16),
            side,
            (((1,), (1,)), ((), ())),
            preferred_element_type=f32,
        )
        part = jnp.where(found > 0.5, float(r), part)
        spot = spot + found
    present = spot > 0.5
    slot = jnp.where(present, spot - 1.0, 0.0).astype(jnp.int32)
    part = jnp.where(present, part, -1.0)
    factors = correction_factors(elapsed_of(levels[...]))
    for t in range(groups):
        lanes = jnp.broadcast_to(slot[t : t + 1], (8, LANES))
        holder = jnp.broadcast_to(part[t : t + 1], (8, LANES))
        new = jnp.zeros((8, LANES), f32)
        for r in range(rows):
            new = jnp.where(holder == float(r), jnp.take_along_axis(forces[r], lanes, axis=1), new)
        there = holder[0:3] > -0.5
        x0, v0, a0, j0 = (pos[:, tile(t)], vel[:, tile(t)], acc[:, tile(t)], jrk[:, tile(t)])
        a1, j1 = (new[0:3], new[3:6])
        x1, v1 = correct(x0, v0, a0, j0, [f[t : t + 1] for f in factors], a1, j1)
        stars_new[0:3, tile(t)] = jnp.where(there, x1, x0)
        stars_new[3:6, tile(t)] = jnp.where(there, v1, v0)
        stars_new[6:9, tile(t)] = jnp.where(there, a1, a0)
        stars_new[9:12, tile(t)] = jnp.where(there, j1, j0)
        if (t + 1) % piece == 0:
            part_of = (slice(None), slice((t + 1 - piece) * LANES, (t + 1) * LANES))
            copies.append(
                pltpu.make_async_copy(
                    stars_new.at[part_of], stars_out.at[part_of], sems.at[len(copies)]
                )
            )
            copies[-1].start()
    for copy in copies:
        copy.wait()


def local(rows, columns, positions, velocities, accels, jerks, masses, levels, active):
    nlocal = positions.shape[1]
    ntarget = active.shape[0]
    groups = nlocal // LANES
    given = (
        positions,
        velocities,
        accels,
        jerks,
        levels.reshape(groups, LANES),
        masses.reshape(groups, LANES),
        active.reshape(1, ntarget),
    )
    mine, *kept = pl.pallas_call(
        gather_kernel,
        out_shape=(
            pltpu.VMEM((columns, 16, ntarget), f32),
            *(pltpu.VMEM(x.shape, x.dtype) for x in given),
        ),
        in_specs=[HBM] * 7,
        out_specs=(VMEM,) * 8,
        scratch_shapes=[pltpu.SemaphoreType.DMA((11,))],
        compiler_params=PARAMS,
        name="gather",
    )(*(pltpu.with_memory_space_constraint(x, pltpu.HBM) for x in given))
    gathered = lax.all_to_all(mine, "ja", 0, 0)
    packed, old = pl.pallas_call(
        force_kernel,
        out_shape=(
            pltpu.VMEM((rows * columns, 1, NEW_ROWS * ntarget), f32),
            pltpu.VMEM((16, ntarget), f32),
        ),
        in_specs=[VMEM] * 8,
        out_specs=(VMEM, VMEM),
        scratch_shapes=[
            pltpu.VMEM((groups, 7, 8, LANES), f32),
            pltpu.VMEM((6, ntarget, LANES), f32),
            pltpu.VMEM((6, ntarget, LANES), f32),
        ],
        compiler_params=PARAMS,
        name="forces",
    )(gathered, *kept)
    everyone = lax.all_to_all(packed, ("ia", "ja"), 0, 0)
    return pl.pallas_call(
        functools.partial(finish_kernel, rows, columns),
        out_shape=(
            jax.ShapeDtypeStruct((12, ntarget), f32),
            jax.ShapeDtypeStruct((12, nlocal), f32),
        ),
        in_specs=[VMEM] * 7,
        out_specs=(HBM, HBM),
        scratch_shapes=[
            pltpu.VMEM((12, ntarget), f32),
            pltpu.VMEM((12, nlocal), f32),
            pltpu.VMEM((rows, 8, ntarget), f32),
            pltpu.SemaphoreType.DMA((1 + PIECES,)),
        ],
        compiler_params=PARAMS,
        name="finish",
    )(everyone, old, *kept[:5])


def solution(mesh):
    rows, columns = mesh.shape["ia"], mesh.shape["ja"]

    def body(*args):
        return local(rows, columns, *args)

    return jax.shard_map(
        body,
        mesh=mesh,
        in_specs=(
            P(None, "ja"),
            P(None, "ja"),
            P(None, "ja"),
            P(None, "ja"),
            P("ja"),
            P("ja"),
            P("ia"),
        ),
        out_specs=(P(None, "ia"), P(None, "ja")),
        check_vma=False,
    )
```

```python
import functools

import jax
import jax.numpy as jnp
from jax import lax
from jax.experimental import pallas as pl
from jax.experimental.pallas import tpu as pltpu
from jax.sharding import PartitionSpec as P

softening_length = 0.01
base_step = 0.0625
LANES = 128
PIECES = 4
TILES = 2
NEW_ROWS = 7
f32 = jnp.float32
VMEM = pl.BlockSpec(memory_space=pltpu.VMEM)
HBM = pl.BlockSpec(memory_space=pltpu.HBM)
PARAMS = pltpu.CompilerParams(vmem_limit_bytes=24 * 1024 * 1024)


def elapsed_of(levels):
    return (128 >> levels).astype(f32) * (base_step / 128.0)


def step_factors(elapsed):
    half = elapsed * elapsed * 0.5
    return (elapsed, half, half * elapsed * (1.0 / 3.0))


def predict(pos, vel, acc, jrk, factors):
    elapsed, half, sixth = factors
    pred_pos = pos + elapsed * vel + half * acc + sixth * jrk
    pred_vel = vel + elapsed * acc + half * jrk
    return (pred_pos, pred_vel)


def correction_factors(step):
    return (0.5 * step, step * step * (1.0 / 12.0))


def correct(x0, v0, a0, j0, factors, a1, j1):
    half, quad = factors
    v1 = v0 + half * (a0 + a1) + quad * (j0 - j1)
    x1 = x0 + half * (v0 + v1) + quad * (a0 - a1)
    return (x1, v1)


def tile(t):
    return slice(t * LANES, (t + 1) * LANES)


def gather_kernel(*refs):
    given, out, kept, sems = (refs[:7], refs[7], refs[8:15], refs[15])
    pos, vel, acc, jrk, levels, masses, active = kept
    groups = levels.shape[0]
    half = groups // 2

    def copy_of(n, sem, columns=None):
        if columns is None:
            return pltpu.make_async_copy(given[n], kept[n], sems.at[sem])
        part = (slice(None), columns)
        return pltpu.make_async_copy(given[n].at[part], kept[n].at[part], sems.at[sem])

    small = [copy_of(6, 0), copy_of(4, 1)]
    parts = [
        [copy_of(n, 2 + 4 * h + n, slice(h * half * LANES, (h + 1) * half * LANES)) for n in range(4)]
        for h in range(2)
    ]
    late = copy_of(5, 10)
    for copy in (*small, *parts[0], *parts[1], late):
        copy.start()
    for copy in small:
        copy.wait()
    offset = active[...] - lax.axis_index("ja") * (groups * LANES)
    group = jnp.broadcast_to(offset >> 7, (8, LANES))
    lane = jnp.broadcast_to(offset & (LANES - 1), (8, LANES))
    row = lax.broadcasted_iota(jnp.int32, (8, LANES), 0)
    elapsed = elapsed_of(levels[...])
    steps = jnp.zeros((8, LANES), f32)
    for t in range(0, groups, 8):
        here = group == row + t
        steps = jnp.where(here, jnp.take_along_axis(elapsed[t : t + 8], lane, axis=1), steps)
    found = [jnp.zeros((3, LANES), f32)] * 4
    for h in range(2):
        for copy in parts[h]:
            copy.wait()
        for t in range(h * half, (h + 1) * half):
            here = group[0:3] == t
            found = [
                jnp.where(here, jnp.take_along_axis(x[:, tile(t)], lane[0:3], axis=1), old)
                for x, old in zip((pos, vel, acc, jrk), found)
            ]
    steps = jnp.broadcast_to(jnp.sum(steps, axis=0, keepdims=True), (4, LANES))
    for k in range(out.shape[0]):
        for n, value in enumerate(found):
            out[k, 3 * n : 3 * n + 3, :] = value
        out[k, 12:16, :] = steps
    late.wait()


def force_kernel(
    gathered, pos, vel, acc, jrk, levels, masses, active, packed, old, sources, targets, sums
):
    groups = levels.shape[0]
    ntarget = active.shape[1]
    state = gathered[0]
    for k in range(1, gathered.shape[0]):
        state = state + gathered[k]
    old[...] = state
    tpos, tvel = predict(
        state[0:3], state[3:6], state[6:9], state[9:12], step_factors(state[12:13])
    )
    columns = jnp.transpose(
        jnp.concatenate([tpos, tvel, jnp.zeros((LANES - 6, ntarget), f32)], axis=0)
    )
    for c in range(6):
        targets[c] = jnp.broadcast_to(columns[:, c : c + 1], (ntarget, LANES))
    factors = step_factors(elapsed_of(levels[...]))
    for t in range(groups):
        spos, svel = predict(
            *(x[:, tile(t)] for x in (pos, vel, acc, jrk)), [f[t : t + 1] for f in factors]
        )
        for c in range(3):
            sources[t, c] = jnp.broadcast_to(spos[c : c + 1], (8, LANES))
            sources[t, 3 + c] = jnp.broadcast_to(svel[c : c + 1], (8, LANES))
        sources[t, 6] = jnp.broadcast_to(masses[t : t + 1, :], (8, LANES))

    sums[...] = jnp.zeros(sums.shape, f32)

    def some_tiles(n, unused):
        held = [[sources[n * TILES + k, c] for c in range(7)] for k in range(TILES)]
        for g in range(ntarget // 8):
            rows = slice(8 * g, 8 * g + 8)
            target = [targets[c, rows, :] for c in range(6)]
            total = [sums[c, rows, :] for c in range(9)]
            for source in held:
                dx, dy, dz, du, dv, dw = (source[c] - target[c] for c in range(6))
                r2 = dx * dx + dy * dy + dz * dz + softening_length
                weight = source[6] * lax.rsqrt(r2)
                inv_sq = pl.reciprocal(r2, approx=True)
                weight = weight * inv_sq
                radial = (dx * du + dy * dv + dz * dw) * inv_sq
                px, py, pz = (weight * dx, weight * dy, weight * dz)
                terms = (
                    *(px, py, pz),
                    *(weight * du, weight * dv, weight * dw),
                    *(radial * px, radial * py, radial * pz),
                )
                total = [old + new for old, new in zip(total, terms)]
            for c in range(9):
                sums[c, rows, :] = total[c]
        return unused

    lax.fori_loop(0, groups // TILES, some_tiles, 0)
    for c in range(3, 6):
        sums[c] = sums[c] - 3.0 * sums[c + 3]
    lane = lax.broadcasted_iota(jnp.int32, (ntarget, LANES), 1)
    table = jnp.zeros((ntarget, LANES), f32)
    for c in range(6):
        table = jnp.where(lane == c, jnp.sum(sums[c], axis=1, keepdims=True), table)
    table = jnp.transpose(table)[0:8]
    row = lax.broadcasted_iota(jnp.int32, (8, ntarget), 0)
    table = jnp.where(row == 6, active[...].astype(f32), table)
    for k in range(packed.shape[0]):
        for c in range(NEW_ROWS):
            packed[k, :, tile(c)] = table[c : c + 1]


def finish_kernel(
    rows, columns, everyone, old, pos, vel, acc, jrk, levels, targets_out, stars_out,
    targets_new, stars_new, rowed, sems
):
    groups = levels.shape[0]
    ntarget = old.shape[1]
    me = lax.axis_index("ia")
    base = lax.axis_index("ja") * (groups * LANES)

    forces, where_hi, where_lo = ([], [], [])
    mine = jnp.zeros((8, ntarget), f32)
    for r in range(rows):
        total = everyone[r * columns]
        for c in range(1, columns):
            total = total + everyone[r * columns + c]
        for c in range(6):
            rowed[r, c : c + 1, :] = total[:, tile(c)]
        forces.append(rowed[r])
        mine = jnp.where(me == r, forces[r], mine)
        offset = everyone[r * columns][:, tile(6)].astype(jnp.int32) - base
        where_hi.append(offset >> 7)
        where_lo.append(offset & (LANES - 1))

    o = old[...]
    factors = correction_factors(o[12:13])
    x1, v1 = correct(o[0:3], o[3:6], o[6:9], o[9:12], factors, mine[0:3], mine[3:6])
    targets_new[0:3, :] = x1
    targets_new[3:6, :] = v1
    targets_new[6:12, :] = mine[0:6]
    copies = [pltpu.make_async_copy(targets_new, targets_out, sems.at[0])]
    copies[0].start()
    piece = groups // PIECES

    group = lax.broadcasted_iota(jnp.int32, (groups, ntarget), 0)
    lane = lax.broadcasted_iota(jnp.int32, (LANES, ntarget), 0)
    number = lax.broadcasted_iota(jnp.int32, (groups, ntarget), 1).astype(f32) + 1.0
    spot = jnp.zeros((groups, LANES), f32)
    part = jnp.zeros((groups, LANES), f32)
    for r in range(rows):
        hit = group == where_hi[r]
        side = (lane == where_lo[r]).astype(jnp.bfloat16)
        found = lax.dot_general(
            jnp.where(hit, number, 0.0).astype(jnp.bfloat16),
            side,
            (((1,), (1,)), ((), ())),
            preferred_element_type=f32,
        )
        part = jnp.where(found > 0.5, float(r), part)
        spot = spot + found
    present = spot > 0.5
    slot = jnp.where(present, spot - 1.0, 0.0).astype(jnp.int32)
    part = jnp.where(present, part, -1.0)
    factors = correction_factors(elapsed_of(levels[...]))
    for t in range(groups):
        lanes = jnp.broadcast_to(slot[t : t + 1], (8, LANES))
        holder = jnp.broadcast_to(part[t : t + 1], (8, LANES))
        new = jnp.zeros((8, LANES), f32)
        for r in range(rows):
            new = jnp.where(holder == float(r), jnp.take_along_axis(forces[r], lanes, axis=1), new)
        there = holder[0:3] > -0.5
        x0, v0, a0, j0 = (pos[:, tile(t)], vel[:, tile(t)], acc[:, tile(t)], jrk[:, tile(t)])
        a1, j1 = (new[0:3], new[3:6])
        x1, v1 = correct(x0, v0, a0, j0, [f[t : t + 1] for f in factors], a1, j1)
        stars_new[0:3, tile(t)] = jnp.where(there, x1, x0)
        stars_new[3:6, tile(t)] = jnp.where(there, v1, v0)
        stars_new[6:9, tile(t)] = jnp.where(there, a1, a0)
        stars_new[9:12, tile(t)] = jnp.where(there, j1, j0)
        if (t + 1) % piece == 0:
            part_of = (slice(None), slice((t + 1 - piece) * LANES, (t + 1) * LANES))
            copies.append(
                pltpu.make_async_copy(
                    stars_new.at[part_of], stars_out.at[part_of], sems.at[len(copies)]
                )
            )
            copies[-1].start()
    for copy in copies:
        copy.wait()


def local(rows, columns, positions, velocities, accels, jerks, masses, levels, active):
    nlocal = positions.shape[1]
    ntarget = active.shape[0]
    groups = nlocal // LANES
    given = (
        positions,
        velocities,
        accels,
        jerks,
        levels.reshape(groups, LANES),
        masses.reshape(groups, LANES),
        active.reshape(1, ntarget),
    )
    mine, *kept = pl.pallas_call(
        gather_kernel,
        out_shape=(
            pltpu.VMEM((columns, 16, ntarget), f32),
            *(pltpu.VMEM(x.shape, x.dtype) for x in given),
        ),
        in_specs=[HBM] * 7,
        out_specs=(VMEM,) * 8,
        scratch_shapes=[pltpu.SemaphoreType.DMA((11,))],
        compiler_params=PARAMS,
        name="gather",
    )(*(pltpu.with_memory_space_constraint(x, pltpu.HBM) for x in given))
    gathered = lax.all_to_all(mine, "ja", 0, 0)
    packed, old = pl.pallas_call(
        force_kernel,
        out_shape=(
            pltpu.VMEM((rows * columns, 1, NEW_ROWS * ntarget), f32),
            pltpu.VMEM((16, ntarget), f32),
        ),
        in_specs=[VMEM] * 8,
        out_specs=(VMEM, VMEM),
        scratch_shapes=[
            pltpu.VMEM((groups, 7, 8, LANES), f32),
            pltpu.VMEM((6, ntarget, LANES), f32),
            pltpu.VMEM((9, ntarget, LANES), f32),
        ],
        compiler_params=PARAMS,
        name="forces",
    )(gathered, *kept)
    everyone = lax.all_to_all(packed, ("ia", "ja"), 0, 0)
    return pl.pallas_call(
        functools.partial(finish_kernel, rows, columns),
        out_shape=(
            jax.ShapeDtypeStruct((12, ntarget), f32),
            jax.ShapeDtypeStruct((12, nlocal), f32),
        ),
        in_specs=[VMEM] * 7,
        out_specs=(HBM, HBM),
        scratch_shapes=[
            pltpu.VMEM((12, ntarget), f32),
            pltpu.VMEM((12, nlocal), f32),
            pltpu.VMEM((rows, 8, ntarget), f32),
            pltpu.SemaphoreType.DMA((1 + PIECES,)),
        ],
        compiler_params=PARAMS,
        name="finish",
    )(everyone, old, *kept[:5])


def solution(mesh):
    rows, columns = mesh.shape["ia"], mesh.shape["ja"]

    def body(*args):
        return local(rows, columns, *args)

    return jax.shard_map(
        body,
        mesh=mesh,
        in_specs=(
            P(None, "ja"),
            P(None, "ja"),
            P(None, "ja"),
            P(None, "ja"),
            P("ja"),
            P("ja"),
            P("ia"),
        ),
        out_specs=(P(None, "ia"), P(None, "ja")),
        check_vma=False,
    )
```

```python
import functools

import jax
import jax.numpy as jnp
from jax import lax
from jax.experimental import pallas as pl
from jax.experimental.pallas import tpu as pltpu
from jax.sharding import PartitionSpec as P

softening_length = 0.01
base_step = 0.0625
LANES = 128
PIECES = 8
NEW_ROWS = 7
f32 = jnp.float32
VMEM = pl.BlockSpec(memory_space=pltpu.VMEM)
HBM = pl.BlockSpec(memory_space=pltpu.HBM)
PARAMS = pltpu.CompilerParams(vmem_limit_bytes=24 * 1024 * 1024)


def elapsed_of(levels):
    return (128 >> levels).astype(f32) * (base_step / 128.0)


def step_factors(elapsed):
    half = elapsed * elapsed * 0.5
    return (elapsed, half, half * elapsed * (1.0 / 3.0))


def predict(pos, vel, acc, jrk, factors):
    elapsed, half, sixth = factors
    pred_pos = pos + elapsed * vel + half * acc + sixth * jrk
    pred_vel = vel + elapsed * acc + half * jrk
    return (pred_pos, pred_vel)


def correction_factors(step):
    return (0.5 * step, step * step * (1.0 / 12.0))


def correct(x0, v0, a0, j0, factors, a1, j1):
    half, quad = factors
    v1 = v0 + half * (a0 + a1) + quad * (j0 - j1)
    x1 = x0 + half * (v0 + v1) + quad * (a0 - a1)
    return (x1, v1)


def tile(t):
    return slice(t * LANES, (t + 1) * LANES)


def gather_kernel(*refs):
    given, out, kept, sems = (refs[:7], refs[7], refs[8:15], refs[15])
    pos, vel, acc, jrk, levels, masses, active = kept
    groups = levels.shape[0]
    half = groups // 2

    def copy_of(n, sem, columns=None):
        if columns is None:
            return pltpu.make_async_copy(given[n], kept[n], sems.at[sem])
        part = (slice(None), columns)
        return pltpu.make_async_copy(given[n].at[part], kept[n].at[part], sems.at[sem])

    small = [copy_of(6, 0), copy_of(4, 1)]
    parts = [
        [copy_of(n, 2 + 4 * h + n, slice(h * half * LANES, (h + 1) * half * LANES)) for n in range(4)]
        for h in range(2)
    ]
    late = copy_of(5, 10)
    for copy in (*small, *parts[0], *parts[1], late):
        copy.start()
    for copy in small:
        copy.wait()
    offset = active[...] - lax.axis_index("ja") * (groups * LANES)
    group = jnp.broadcast_to(offset >> 7, (8, LANES))
    lane = jnp.broadcast_to(offset & (LANES - 1), (8, LANES))
    row = lax.broadcasted_iota(jnp.int32, (8, LANES), 0)
    elapsed = elapsed_of(levels[...])
    steps = jnp.zeros((8, LANES), f32)
    for t in range(0, groups, 8):
        here = group == row + t
        steps = jnp.where(here, jnp.take_along_axis(elapsed[t : t + 8], lane, axis=1), steps)
    found = [jnp.zeros((3, LANES), f32)] * 4
    for h in range(2):
        for copy in parts[h]:
            copy.wait()
        for t in range(h * half, (h + 1) * half):
            here = group[0:3] == t
            found = [
                jnp.where(here, jnp.take_along_axis(x[:, tile(t)], lane[0:3], axis=1), old)
                for x, old in zip((pos, vel, acc, jrk), found)
            ]
    steps = jnp.broadcast_to(jnp.sum(steps, axis=0, keepdims=True), (4, LANES))
    for k in range(out.shape[0]):
        for n, value in enumerate(found):
            out[k, 3 * n : 3 * n + 3, :] = value
        out[k, 12:16, :] = steps
    late.wait()


def force_kernel(
    gathered, pos, vel, acc, jrk, levels, masses, active, packed, old, sources, targets, sums
):
    groups = levels.shape[0]
    ntarget = active.shape[1]
    state = gathered[0]
    for k in range(1, gathered.shape[0]):
        state = state + gathered[k]
    old[...] = state
    tpos, tvel = predict(
        state[0:3], state[3:6], state[6:9], state[9:12], step_factors(state[12:13])
    )
    columns = jnp.transpose(
        jnp.concatenate([tpos, tvel, jnp.zeros((LANES - 6, ntarget), f32)], axis=0)
    )
    for c in range(6):
        targets[c] = jnp.broadcast_to(columns[:, c : c + 1], (ntarget, LANES))
    factors = step_factors(elapsed_of(levels[...]))
    for t in range(groups):
        spos, svel = predict(
            *(x[:, tile(t)] for x in (pos, vel, acc, jrk)), [f[t : t + 1] for f in factors]
        )
        for c in range(3):
            sources[t, c] = jnp.broadcast_to(spos[c : c + 1], (8, LANES))
            sources[t, 3 + c] = jnp.broadcast_to(svel[c : c + 1], (8, LANES))
        sources[t, 6] = jnp.broadcast_to(masses[t : t + 1, :], (8, LANES))

    def one_group(g, unused):
        rows = pl.ds(pl.multiple_of(g * 8, 8), 8)
        tx, ty, tz, tu, tv, tw = (targets[c, rows, :] for c in range(6))

        def one_tile(t, carry):
            dx, dy, dz = (sources[t, 0] - tx, sources[t, 1] - ty, sources[t, 2] - tz)
            du, dv, dw = (sources[t, 3] - tu, sources[t, 4] - tv, sources[t, 5] - tw)
            r2 = dx * dx + dy * dy + dz * dz + softening_length
            inv = lax.rsqrt(r2)
            inv_sq = inv * inv
            weight = sources[t, 6] * inv * inv_sq
            radial = (dx * du + dy * dv + dz * dw) * inv_sq
            px, py, pz = (weight * dx, weight * dy, weight * dz)
            ax, ay, az, jx, jy, jz, kx, ky, kz = carry
            return (
                ax + px,
                ay + py,
                az + pz,
                jx + weight * du,
                jy + weight * dv,
                jz + weight * dw,
                kx + radial * px,
                ky + radial * py,
                kz + radial * pz,
            )

        zero = jnp.zeros((8, LANES), f32)
        ax, ay, az, jx, jy, jz, kx, ky, kz = lax.fori_loop(
            0, groups, one_tile, (zero,) * 9, unroll=32
        )
        for c, value in enumerate((ax, ay, az, jx - 3.0 * kx, jy - 3.0 * ky, jz - 3.0 * kz)):
            sums[c, rows, :] = value
        return unused

    lax.fori_loop(0, ntarget // 8, one_group, 0)
    lane = lax.broadcasted_iota(jnp.int32, (ntarget, LANES), 1)
    table = jnp.zeros((ntarget, LANES), f32)
    for c in range(6):
        table = jnp.where(lane == c, jnp.sum(sums[c], axis=1, keepdims=True), table)
    table = jnp.transpose(table)[0:8]
    row = lax.broadcasted_iota(jnp.int32, (8, ntarget), 0)
    table = jnp.where(row == 6, active[...].astype(f32), table)
    for k in range(packed.shape[0]):
        for c in range(NEW_ROWS):
            packed[k, :, tile(c)] = table[c : c + 1]


def finish_kernel(
    rows, columns, everyone, old, pos, vel, acc, jrk, levels, targets_out, stars_out,
    targets_new, stars_new, rowed, sems
):
    groups = levels.shape[0]
    ntarget = old.shape[1]
    me = lax.axis_index("ia")
    base = lax.axis_index("ja") * (groups * LANES)

    forces, where_hi, where_lo = ([], [], [])
    mine = jnp.zeros((8, ntarget), f32)
    for r in range(rows):
        total = everyone[r * columns]
        for c in range(1, columns):
            total = total + everyone[r * columns + c]
        for c in range(6):
            rowed[r, c : c + 1, :] = total[:, tile(c)]
        forces.append(rowed[r])
        mine = jnp.where(me == r, forces[r], mine)
        offset = everyone[r * columns][:, tile(6)].astype(jnp.int32) - base
        where_hi.append(offset >> 7)
        where_lo.append(offset & (LANES - 1))

    o = old[...]
    factors = correction_factors(o[12:13])
    x1, v1 = correct(o[0:3], o[3:6], o[6:9], o[9:12], factors, mine[0:3], mine[3:6])
    targets_new[0:3, :] = x1
    targets_new[3:6, :] = v1
    targets_new[6:12, :] = mine[0:6]
    copies = [pltpu.make_async_copy(targets_new, targets_out, sems.at[0])]
    copies[0].start()
    piece = groups // PIECES

    group = lax.broadcasted_iota(jnp.int32, (groups, ntarget), 0)
    lane = lax.broadcasted_iota(jnp.int32, (LANES, ntarget), 0)
    number = lax.broadcasted_iota(jnp.int32, (groups, ntarget), 1).astype(f32) + 1.0
    spot = jnp.zeros((groups, LANES), f32)
    part = jnp.zeros((groups, LANES), f32)
    for r in range(rows):
        hit = group == where_hi[r]
        side = (lane == where_lo[r]).astype(jnp.bfloat16)
        found = lax.dot_general(
            jnp.where(hit, number, 0.0).astype(jnp.bfloat16),
            side,
            (((1,), (1,)), ((), ())),
            preferred_element_type=f32,
        )
        part = jnp.where(found > 0.5, float(r), part)
        spot = spot + found
    present = spot > 0.5
    slot = jnp.where(present, spot - 1.0, 0.0).astype(jnp.int32)
    part = jnp.where(present, part, -1.0)
    factors = correction_factors(elapsed_of(levels[...]))
    for t in range(groups):
        lanes = jnp.broadcast_to(slot[t : t + 1], (8, LANES))
        holder = jnp.broadcast_to(part[t : t + 1], (8, LANES))
        new = jnp.zeros((8, LANES), f32)
        for r in range(rows):
            new = jnp.where(holder == float(r), jnp.take_along_axis(forces[r], lanes, axis=1), new)
        there = holder[0:3] > -0.5
        x0, v0, a0, j0 = (pos[:, tile(t)], vel[:, tile(t)], acc[:, tile(t)], jrk[:, tile(t)])
        a1, j1 = (new[0:3], new[3:6])
        x1, v1 = correct(x0, v0, a0, j0, [f[t : t + 1] for f in factors], a1, j1)
        stars_new[0:3, tile(t)] = jnp.where(there, x1, x0)
        stars_new[3:6, tile(t)] = jnp.where(there, v1, v0)
        stars_new[6:9, tile(t)] = jnp.where(there, a1, a0)
        stars_new[9:12, tile(t)] = jnp.where(there, j1, j0)
        if (t + 1) % piece == 0:
            part_of = (slice(None), slice((t + 1 - piece) * LANES, (t + 1) * LANES))
            copies.append(
                pltpu.make_async_copy(
                    stars_new.at[part_of], stars_out.at[part_of], sems.at[len(copies)]
                )
            )
            copies[-1].start()
    for copy in copies:
        copy.wait()


def local(rows, columns, positions, velocities, accels, jerks, masses, levels, active):
    nlocal = positions.shape[1]
    ntarget = active.shape[0]
    groups = nlocal // LANES
    given = (
        positions,
        velocities,
        accels,
        jerks,
        levels.reshape(groups, LANES),
        masses.reshape(groups, LANES),
        active.reshape(1, ntarget),
    )
    mine, *kept = pl.pallas_call(
        gather_kernel,
        out_shape=(
            pltpu.VMEM((columns, 16, ntarget), f32),
            *(pltpu.VMEM(x.shape, x.dtype) for x in given),
        ),
        in_specs=[HBM] * 7,
        out_specs=(VMEM,) * 8,
        scratch_shapes=[pltpu.SemaphoreType.DMA((11,))],
        compiler_params=PARAMS,
        name="gather",
    )(*(pltpu.with_memory_space_constraint(x, pltpu.HBM) for x in given))
    backwards = [list(range(columns - 1, -1, -1))]
    gathered = lax.all_to_all(mine, "ja", 0, 0, axis_index_groups=backwards)
    packed, old = pl.pallas_call(
        force_kernel,
        out_shape=(
            pltpu.VMEM((rows * columns, 1, NEW_ROWS * ntarget), f32),
            pltpu.VMEM((16, ntarget), f32),
        ),
        in_specs=[VMEM] * 8,
        out_specs=(VMEM, VMEM),
        scratch_shapes=[
            pltpu.VMEM((groups, 7, 8, LANES), f32),
            pltpu.VMEM((6, ntarget, LANES), f32),
            pltpu.VMEM((6, ntarget, LANES), f32),
        ],
        compiler_params=PARAMS,
        name="forces",
    )(gathered, *kept)
    everyone = lax.all_to_all(packed, ("ia", "ja"), 0, 0)
    return pl.pallas_call(
        functools.partial(finish_kernel, rows, columns),
        out_shape=(
            jax.ShapeDtypeStruct((12, ntarget), f32),
            jax.ShapeDtypeStruct((12, nlocal), f32),
        ),
        in_specs=[VMEM] * 7,
        out_specs=(HBM, HBM),
        scratch_shapes=[
            pltpu.VMEM((12, ntarget), f32),
            pltpu.VMEM((12, nlocal), f32),
            pltpu.VMEM((rows, 8, ntarget), f32),
            pltpu.SemaphoreType.DMA((1 + PIECES,)),
        ],
        compiler_params=PARAMS,
        name="finish",
    )(everyone, old, *kept[:5])


def solution(mesh):
    rows, columns = mesh.shape["ia"], mesh.shape["ja"]

    def body(*args):
        return local(rows, columns, *args)

    return jax.shard_map(
        body,
        mesh=mesh,
        in_specs=(
            P(None, "ja"),
            P(None, "ja"),
            P(None, "ja"),
            P(None, "ja"),
            P("ja"),
            P("ja"),
            P("ia"),
        ),
        out_specs=(P(None, "ia"), P(None, "ja")),
        check_vma=False,
    )
```

```python
import functools

import jax
import jax.numpy as jnp
from jax import lax
from jax.experimental import pallas as pl
from jax.experimental.pallas import tpu as pltpu
from jax.sharding import PartitionSpec as P

softening_length = 0.01
base_step = 0.0625
LANES = 128
PIECES = 8
NEW_ROWS = 7
f32 = jnp.float32
VMEM = pl.BlockSpec(memory_space=pltpu.VMEM)
HBM = pl.BlockSpec(memory_space=pltpu.HBM)
PARAMS = pltpu.CompilerParams(vmem_limit_bytes=24 * 1024 * 1024)


def elapsed_of(levels):
    return (128 >> levels).astype(f32) * (base_step / 128.0)


def step_factors(elapsed):
    half = elapsed * elapsed * 0.5
    return (elapsed, half, half * elapsed * (1.0 / 3.0))


def predict(pos, vel, acc, jrk, factors):
    elapsed, half, sixth = factors
    pred_pos = pos + elapsed * vel + half * acc + sixth * jrk
    pred_vel = vel + elapsed * acc + half * jrk
    return (pred_pos, pred_vel)


def correction_factors(step):
    return (0.5 * step, step * step * (1.0 / 12.0))


def correct(x0, v0, a0, j0, factors, a1, j1):
    half, quad = factors
    v1 = v0 + half * (a0 + a1) + quad * (j0 - j1)
    x1 = x0 + half * (v0 + v1) + quad * (a0 - a1)
    return (x1, v1)


def tile(t):
    return slice(t * LANES, (t + 1) * LANES)


def gather_kernel(*refs):
    given, out, kept, sems = (refs[:7], refs[7], refs[8:15], refs[15])
    pos, vel, acc, jrk, levels, masses, active = kept
    groups = levels.shape[0]
    half = groups // 2

    def copy_of(n, sem, columns=None):
        if columns is None:
            return pltpu.make_async_copy(given[n], kept[n], sems.at[sem])
        part = (slice(None), columns)
        return pltpu.make_async_copy(given[n].at[part], kept[n].at[part], sems.at[sem])

    small = [copy_of(6, 0), copy_of(4, 1)]
    parts = [
        [copy_of(n, 2 + 4 * h + n, slice(h * half * LANES, (h + 1) * half * LANES)) for n in range(4)]
        for h in range(2)
    ]
    late = copy_of(5, 10)
    for copy in (*small, *parts[0], *parts[1], late):
        copy.start()
    for copy in small:
        copy.wait()
    offset = active[...] - lax.axis_index("ja") * (groups * LANES)
    group = jnp.broadcast_to(offset >> 7, (8, LANES))
    lane = jnp.broadcast_to(offset & (LANES - 1), (8, LANES))
    row = lax.broadcasted_iota(jnp.int32, (8, LANES), 0)
    elapsed = elapsed_of(levels[...])
    steps = jnp.zeros((8, LANES), f32)
    for t in range(0, groups, 8):
        here = group == row + t
        steps = jnp.where(here, jnp.take_along_axis(elapsed[t : t + 8], lane, axis=1), steps)
    found = [jnp.zeros((3, LANES), f32)] * 4
    for h in range(2):
        for copy in parts[h]:
            copy.wait()
        for t in range(h * half, (h + 1) * half):
            here = group[0:3] == t
            found = [
                jnp.where(here, jnp.take_along_axis(x[:, tile(t)], lane[0:3], axis=1), old)
                for x, old in zip((pos, vel, acc, jrk), found)
            ]
    steps = jnp.broadcast_to(jnp.sum(steps, axis=0, keepdims=True), (4, LANES))
    for k in range(out.shape[0]):
        for n, value in enumerate(found):
            out[k, 3 * n : 3 * n + 3, :] = value
        out[k, 12:16, :] = steps
    late.wait()


def force_kernel(
    gathered, pos, vel, acc, jrk, levels, masses, active, packed, old, sources, targets, sums
):
    groups = levels.shape[0]
    ntarget = active.shape[1]
    state = gathered[0]
    for k in range(1, gathered.shape[0]):
        state = state + gathered[k]
    old[...] = state
    tpos, tvel = predict(
        state[0:3], state[3:6], state[6:9], state[9:12], step_factors(state[12:13])
    )
    columns = jnp.transpose(
        jnp.concatenate([tpos, tvel, jnp.zeros((LANES - 6, ntarget), f32)], axis=0)
    )
    for c in range(6):
        targets[c] = jnp.broadcast_to(columns[:, c : c + 1], (ntarget, LANES))
    factors = step_factors(elapsed_of(levels[...]))
    for t in range(groups):
        spos, svel = predict(
            *(x[:, tile(t)] for x in (pos, vel, acc, jrk)), [f[t : t + 1] for f in factors]
        )
        for c in range(3):
            sources[t, c] = jnp.broadcast_to(spos[c : c + 1], (8, LANES))
            sources[t, 3 + c] = jnp.broadcast_to(svel[c : c + 1], (8, LANES))
        sources[t, 6] = jnp.broadcast_to(masses[t : t + 1, :], (8, LANES))

    def one_group(g, unused):
        rows = pl.ds(pl.multiple_of(g * 8, 8), 8)
        tx, ty, tz, tu, tv, tw = (targets[c, rows, :] for c in range(6))

        def one_tile(t, carry):
            dx, dy, dz = (sources[t, 0] - tx, sources[t, 1] - ty, sources[t, 2] - tz)
            du, dv, dw = (sources[t, 3] - tu, sources[t, 4] - tv, sources[t, 5] - tw)
            r2 = dx * dx + dy * dy + dz * dz + softening_length
            inv = lax.rsqrt(r2)
            inv_sq = inv * inv
            weight = sources[t, 6] * inv * inv_sq
            radial = (dx * du + dy * dv + dz * dw) * inv_sq
            px, py, pz = (weight * dx, weight * dy, weight * dz)
            ax, ay, az, jx, jy, jz, kx, ky, kz = carry
            return (
                ax + px,
                ay + py,
                az + pz,
                jx + weight * du,
                jy + weight * dv,
                jz + weight * dw,
                kx + radial * px,
                ky + radial * py,
                kz + radial * pz,
            )

        zero = jnp.zeros((8, LANES), f32)
        ax, ay, az, jx, jy, jz, kx, ky, kz = lax.fori_loop(
            0, groups, one_tile, (zero,) * 9, unroll=32
        )
        for c, value in enumerate((ax, ay, az, jx - 3.0 * kx, jy - 3.0 * ky, jz - 3.0 * kz)):
            sums[c, rows, :] = value
        return unused

    lax.fori_loop(0, ntarget // 8, one_group, 0)
    lane = lax.broadcasted_iota(jnp.int32, (ntarget, LANES), 1)
    table = jnp.zeros((ntarget, LANES), f32)
    for c in range(6):
        table = jnp.where(lane == c, jnp.sum(sums[c], axis=1, keepdims=True), table)
    table = jnp.transpose(table)[0:8]
    row = lax.broadcasted_iota(jnp.int32, (8, ntarget), 0)
    table = jnp.where(row == 6, active[...].astype(f32), table)
    for k in range(packed.shape[0]):
        for c in range(NEW_ROWS):
            packed[k, :, tile(c)] = table[c : c + 1]


def finish_kernel(
    rows, columns, same_core, other_core, old, pos, vel, acc, jrk, levels, targets_out, stars_out,
    targets_new, stars_new, rowed, sems
):
    groups = levels.shape[0]
    ntarget = old.shape[1]
    me = lax.axis_index("ia")
    base = lax.axis_index("ja") * (groups * LANES)

    forces, where_hi, where_lo = ([], [], [])
    mine = jnp.zeros((8, ntarget), f32)
    for r in range(rows):
        everyone = same_core if r < rows // 2 else other_core
        first = r % (rows // 2) * columns
        total = everyone[first]
        for c in range(1, columns):
            total = total + everyone[first + c]
        for c in range(6):
            rowed[r, c : c + 1, :] = total[:, tile(c)]
        forces.append(rowed[r])
        mine = jnp.where(rows // 2 - 1 - (me >> 1) == r, forces[r], mine)
        offset = everyone[first][:, tile(6)].astype(jnp.int32) - base
        where_hi.append(offset >> 7)
        where_lo.append(offset & (LANES - 1))

    o = old[...]
    factors = correction_factors(o[12:13])
    x1, v1 = correct(o[0:3], o[3:6], o[6:9], o[9:12], factors, mine[0:3], mine[3:6])
    targets_new[0:3, :] = x1
    targets_new[3:6, :] = v1
    targets_new[6:12, :] = mine[0:6]
    copies = [pltpu.make_async_copy(targets_new, targets_out, sems.at[0])]
    copies[0].start()
    piece = groups // PIECES

    group = lax.broadcasted_iota(jnp.int32, (groups, ntarget), 0)
    lane = lax.broadcasted_iota(jnp.int32, (LANES, ntarget), 0)
    number = lax.broadcasted_iota(jnp.int32, (groups, ntarget), 1).astype(f32) + 1.0
    spot = jnp.zeros((groups, LANES), f32)
    part = jnp.zeros((groups, LANES), f32)
    for r in range(rows):
        hit = group == where_hi[r]
        side = (lane == where_lo[r]).astype(jnp.bfloat16)
        found = lax.dot_general(
            jnp.where(hit, number, 0.0).astype(jnp.bfloat16),
            side,
            (((1,), (1,)), ((), ())),
            preferred_element_type=f32,
        )
        part = jnp.where(found > 0.5, float(r), part)
        spot = spot + found
    present = spot > 0.5
    slot = jnp.where(present, spot - 1.0, 0.0).astype(jnp.int32)
    part = jnp.where(present, part, -1.0)
    factors = correction_factors(elapsed_of(levels[...]))
    for t in range(groups):
        lanes = jnp.broadcast_to(slot[t : t + 1], (8, LANES))
        holder = jnp.broadcast_to(part[t : t + 1], (8, LANES))
        new = jnp.zeros((8, LANES), f32)
        for r in range(rows):
            new = jnp.where(holder == float(r), jnp.take_along_axis(forces[r], lanes, axis=1), new)
        there = holder[0:3] > -0.5
        x0, v0, a0, j0 = (pos[:, tile(t)], vel[:, tile(t)], acc[:, tile(t)], jrk[:, tile(t)])
        a1, j1 = (new[0:3], new[3:6])
        x1, v1 = correct(x0, v0, a0, j0, [f[t : t + 1] for f in factors], a1, j1)
        stars_new[0:3, tile(t)] = jnp.where(there, x1, x0)
        stars_new[3:6, tile(t)] = jnp.where(there, v1, v0)
        stars_new[6:9, tile(t)] = jnp.where(there, a1, a0)
        stars_new[9:12, tile(t)] = jnp.where(there, j1, j0)
        if (t + 1) % piece == 0:
            part_of = (slice(None), slice((t + 1 - piece) * LANES, (t + 1) * LANES))
            copies.append(
                pltpu.make_async_copy(
                    stars_new.at[part_of], stars_out.at[part_of], sems.at[len(copies)]
                )
            )
            copies[-1].start()
    for copy in copies:
        copy.wait()


def local(rows, columns, positions, velocities, accels, jerks, masses, levels, active):
    nlocal = positions.shape[1]
    ntarget = active.shape[0]
    groups = nlocal // LANES
    given = (
        positions,
        velocities,
        accels,
        jerks,
        levels.reshape(groups, LANES),
        masses.reshape(groups, LANES),
        active.reshape(1, ntarget),
    )
    mine, *kept = pl.pallas_call(
        gather_kernel,
        out_shape=(
            pltpu.VMEM((columns, 16, ntarget), f32),
            *(pltpu.VMEM(x.shape, x.dtype) for x in given),
        ),
        in_specs=[HBM] * 7,
        out_specs=(VMEM,) * 8,
        scratch_shapes=[pltpu.SemaphoreType.DMA((11,))],
        compiler_params=PARAMS,
        name="gather",
    )(*(pltpu.with_memory_space_constraint(x, pltpu.HBM) for x in given))
    backwards = [list(range(columns - 1, -1, -1))]
    gathered = lax.all_to_all(mine, "ja", 0, 0, axis_index_groups=backwards)
    packed, old = pl.pallas_call(
        force_kernel,
        out_shape=(
            pltpu.VMEM((rows // 2 * columns, 1, NEW_ROWS * ntarget), f32),
            pltpu.VMEM((16, ntarget), f32),
        ),
        in_specs=[VMEM] * 8,
        out_specs=(VMEM, VMEM),
        scratch_shapes=[
            pltpu.VMEM((groups, 7, 8, LANES), f32),
            pltpu.VMEM((6, ntarget, LANES), f32),
            pltpu.VMEM((6, ntarget, LANES), f32),
        ],
        compiler_params=PARAMS,
        name="forces",
    )(gathered, *kept)
    backwards = [
        [r * columns + c for r in range(rows - 2 + core, -1, -2) for c in range(columns - 1, -1, -1)]
        for core in range(2)
    ]
    same_core = lax.all_to_all(packed, ("ia", "ja"), 0, 0, axis_index_groups=backwards)
    other_core = lax.ppermute(same_core, "ia", [(r, r ^ 1) for r in range(rows)])
    return pl.pallas_call(
        functools.partial(finish_kernel, rows, columns),
        out_shape=(
            jax.ShapeDtypeStruct((12, ntarget), f32),
            jax.ShapeDtypeStruct((12, nlocal), f32),
        ),
        in_specs=[VMEM] * 8,
        out_specs=(HBM, HBM),
        scratch_shapes=[
            pltpu.VMEM((12, ntarget), f32),
            pltpu.VMEM((12, nlocal), f32),
            pltpu.VMEM((rows, 8, ntarget), f32),
            pltpu.SemaphoreType.DMA((1 + PIECES,)),
        ],
        compiler_params=PARAMS,
        name="finish",
    )(same_core, other_core, old, *kept[:5])


def solution(mesh):
    rows, columns = mesh.shape["ia"], mesh.shape["ja"]

    def body(*args):
        return local(rows, columns, *args)

    return jax.shard_map(
        body,
        mesh=mesh,
        in_specs=(
            P(None, "ja"),
            P(None, "ja"),
            P(None, "ja"),
            P(None, "ja"),
            P("ja"),
            P("ja"),
            P("ia"),
        ),
        out_specs=(P(None, "ia"), P(None, "ja")),
        check_vma=False,
    )
```

```python
import functools

import jax
import jax.numpy as jnp
from jax import lax
from jax.experimental import pallas as pl
from jax.experimental.pallas import tpu as pltpu
from jax.sharding import PartitionSpec as P

softening_length = 0.01
base_step = 0.0625
LANES = 128
PIECES = 8
NEW_ROWS = 7
f32 = jnp.float32
VMEM = pl.BlockSpec(memory_space=pltpu.VMEM)
HBM = pl.BlockSpec(memory_space=pltpu.HBM)
PARAMS = pltpu.CompilerParams(vmem_limit_bytes=24 * 1024 * 1024)


def elapsed_of(levels):
    return (128 >> levels).astype(f32) * (base_step / 128.0)


def step_factors(elapsed):
    half = elapsed * elapsed * 0.5
    return (elapsed, half, half * elapsed * (1.0 / 3.0))


def predict(pos, vel, acc, jrk, factors):
    elapsed, half, sixth = factors
    pred_pos = pos + elapsed * vel + half * acc + sixth * jrk
    pred_vel = vel + elapsed * acc + half * jrk
    return (pred_pos, pred_vel)


def correction_factors(step):
    return (0.5 * step, step * step * (1.0 / 12.0))


def correct(x0, v0, a0, j0, factors, a1, j1):
    half, quad = factors
    v1 = v0 + half * (a0 + a1) + quad * (j0 - j1)
    x1 = x0 + half * (v0 + v1) + quad * (a0 - a1)
    return (x1, v1)


def column_order(columns):
    first = max(columns - 3, 0)
    return [first, *(c for c in range(columns - 1, -1, -1) if c != first)]


def pair_order(rows, columns):
    late = [columns - 1, columns - 2]
    return [(h, c) for c in (*late, *range(columns - 2)) for h in range(rows // 2)]


def tile(t):
    return slice(t * LANES, (t + 1) * LANES)


def gather_kernel(*refs):
    given, out, kept, sems = (refs[:7], refs[7], refs[8:15], refs[15])
    pos, vel, acc, jrk, levels, masses, active = kept
    groups = levels.shape[0]
    half = groups // 2

    def copy_of(n, sem, columns=None):
        if columns is None:
            return pltpu.make_async_copy(given[n], kept[n], sems.at[sem])
        part = (slice(None), columns)
        return pltpu.make_async_copy(given[n].at[part], kept[n].at[part], sems.at[sem])

    small = [copy_of(6, 0), copy_of(4, 1)]
    parts = [
        [copy_of(n, 2 + 4 * h + n, slice(h * half * LANES, (h + 1) * half * LANES)) for n in range(4)]
        for h in range(2)
    ]
    late = copy_of(5, 10)
    for copy in (*small, *parts[0], *parts[1], late):
        copy.start()
    for copy in small:
        copy.wait()
    offset = active[...] - lax.axis_index("ja") * (groups * LANES)
    group = jnp.broadcast_to(offset >> 7, (8, LANES))
    lane = jnp.broadcast_to(offset & (LANES - 1), (8, LANES))
    row = lax.broadcasted_iota(jnp.int32, (8, LANES), 0)
    elapsed = elapsed_of(levels[...])
    steps = jnp.zeros((8, LANES), f32)
    for t in range(0, groups, 8):
        here = group == row + t
        steps = jnp.where(here, jnp.take_along_axis(elapsed[t : t + 8], lane, axis=1), steps)
    found = [jnp.zeros((3, LANES), f32)] * 4
    for h in range(2):
        for copy in parts[h]:
            copy.wait()
        for t in range(h * half, (h + 1) * half):
            here = group[0:3] == t
            found = [
                jnp.where(here, jnp.take_along_axis(x[:, tile(t)], lane[0:3], axis=1), old)
                for x, old in zip((pos, vel, acc, jrk), found)
            ]
    steps = jnp.broadcast_to(jnp.sum(steps, axis=0, keepdims=True), (4, LANES))
    for k in range(out.shape[0]):
        for n, value in enumerate(found):
            out[k, 3 * n : 3 * n + 3, :] = value
        out[k, 12:16, :] = steps
    late.wait()


def force_kernel(
    gathered, pos, vel, acc, jrk, levels, masses, active, packed, old, sources, targets, sums
):
    groups = levels.shape[0]
    ntarget = active.shape[1]
    state = gathered[0]
    for k in range(1, gathered.shape[0]):
        state = state + gathered[k]
    old[...] = state
    tpos, tvel = predict(
        state[0:3], state[3:6], state[6:9], state[9:12], step_factors(state[12:13])
    )
    columns = jnp.transpose(
        jnp.concatenate([tpos, tvel, jnp.zeros((LANES - 6, ntarget), f32)], axis=0)
    )
    for c in range(6):
        targets[c] = jnp.broadcast_to(columns[:, c : c + 1], (ntarget, LANES))
    factors = step_factors(elapsed_of(levels[...]))
    for t in range(groups):
        spos, svel = predict(
            *(x[:, tile(t)] for x in (pos, vel, acc, jrk)), [f[t : t + 1] for f in factors]
        )
        for c in range(3):
            sources[t, c] = jnp.broadcast_to(spos[c : c + 1], (8, LANES))
            sources[t, 3 + c] = jnp.broadcast_to(svel[c : c + 1], (8, LANES))
        sources[t, 6] = jnp.broadcast_to(masses[t : t + 1, :], (8, LANES))

    def one_group(g, unused):
        rows = pl.ds(pl.multiple_of(g * 8, 8), 8)
        tx, ty, tz, tu, tv, tw = (targets[c, rows, :] for c in range(6))

        def one_tile(t, carry):
            dx, dy, dz = (sources[t, 0] - tx, sources[t, 1] - ty, sources[t, 2] - tz)
            du, dv, dw = (sources[t, 3] - tu, sources[t, 4] - tv, sources[t, 5] - tw)
            r2 = dx * dx + dy * dy + dz * dz + softening_length
            inv = lax.rsqrt(r2)
            inv_sq = inv * inv
            weight = sources[t, 6] * inv * inv_sq
            radial = (dx * du + dy * dv + dz * dw) * inv_sq
            px, py, pz = (weight * dx, weight * dy, weight * dz)
            ax, ay, az, jx, jy, jz, kx, ky, kz = carry
            return (
                ax + px,
                ay + py,
                az + pz,
                jx + weight * du,
                jy + weight * dv,
                jz + weight * dw,
                kx + radial * px,
                ky + radial * py,
                kz + radial * pz,
            )

        zero = jnp.zeros((8, LANES), f32)
        ax, ay, az, jx, jy, jz, kx, ky, kz = lax.fori_loop(
            0, groups, one_tile, (zero,) * 9, unroll=32
        )
        for c, value in enumerate((ax, ay, az, jx - 3.0 * kx, jy - 3.0 * ky, jz - 3.0 * kz)):
            sums[c, rows, :] = value
        return unused

    lax.fori_loop(0, ntarget // 8, one_group, 0)
    lane = lax.broadcasted_iota(jnp.int32, (ntarget, LANES), 1)
    table = jnp.zeros((ntarget, LANES), f32)
    for c in range(6):
        table = jnp.where(lane == c, jnp.sum(sums[c], axis=1, keepdims=True), table)
    table = jnp.transpose(table)[0:8]
    row = lax.broadcasted_iota(jnp.int32, (8, ntarget), 0)
    table = jnp.where(row == 6, active[...].astype(f32), table)
    for k in range(packed.shape[0]):
        for c in range(NEW_ROWS):
            packed[k, :, tile(c)] = table[c : c + 1]


def finish_kernel(
    rows, columns, same_core, other_core, old, pos, vel, acc, jrk, levels, targets_out, stars_out,
    targets_new, stars_new, rowed, sems
):
    groups = levels.shape[0]
    ntarget = old.shape[1]
    me = lax.axis_index("ia")
    base = lax.axis_index("ja") * (groups * LANES)

    forces, where_hi, where_lo = ([], [], [])
    mine = jnp.zeros((8, ntarget), f32)
    order = pair_order(rows, columns)
    for r in range(rows):
        everyone = same_core if r < rows // 2 else other_core
        first, *others = [k for k, (h, _) in enumerate(order) if h == r % (rows // 2)]
        total = everyone[first]
        for k in others:
            total = total + everyone[k]
        for c in range(6):
            rowed[r, c : c + 1, :] = total[:, tile(c)]
        forces.append(rowed[r])
        mine = jnp.where((me >> 1) == r, forces[r], mine)
        offset = everyone[first][:, tile(6)].astype(jnp.int32) - base
        where_hi.append(offset >> 7)
        where_lo.append(offset & (LANES - 1))

    o = old[...]
    factors = correction_factors(o[12:13])
    x1, v1 = correct(o[0:3], o[3:6], o[6:9], o[9:12], factors, mine[0:3], mine[3:6])
    targets_new[0:3, :] = x1
    targets_new[3:6, :] = v1
    targets_new[6:12, :] = mine[0:6]
    copies = [pltpu.make_async_copy(targets_new, targets_out, sems.at[0])]
    copies[0].start()
    piece = groups // PIECES

    group = lax.broadcasted_iota(jnp.int32, (groups, ntarget), 0)
    lane = lax.broadcasted_iota(jnp.int32, (LANES, ntarget), 0)
    number = lax.broadcasted_iota(jnp.int32, (groups, ntarget), 1).astype(f32) + 1.0
    spot = jnp.zeros((groups, LANES), f32)
    part = jnp.zeros((groups, LANES), f32)
    for r in range(rows):
        hit = group == where_hi[r]
        side = (lane == where_lo[r]).astype(jnp.bfloat16)
        found = lax.dot_general(
            jnp.where(hit, number, 0.0).astype(jnp.bfloat16),
            side,
            (((1,), (1,)), ((), ())),
            preferred_element_type=f32,
        )
        part = jnp.where(found > 0.5, float(r), part)
        spot = spot + found
    present = spot > 0.5
    slot = jnp.where(present, spot - 1.0, 0.0).astype(jnp.int32)
    part = jnp.where(present, part, -1.0)
    factors = correction_factors(elapsed_of(levels[...]))
    for t in range(groups):
        lanes = jnp.broadcast_to(slot[t : t + 1], (8, LANES))
        holder = jnp.broadcast_to(part[t : t + 1], (8, LANES))
        new = jnp.zeros((8, LANES), f32)
        for r in range(rows):
            new = jnp.where(holder == float(r), jnp.take_along_axis(forces[r], lanes, axis=1), new)
        there = holder[0:3] > -0.5
        x0, v0, a0, j0 = (pos[:, tile(t)], vel[:, tile(t)], acc[:, tile(t)], jrk[:, tile(t)])
        a1, j1 = (new[0:3], new[3:6])
        x1, v1 = correct(x0, v0, a0, j0, [f[t : t + 1] for f in factors], a1, j1)
        stars_new[0:3, tile(t)] = jnp.where(there, x1, x0)
        stars_new[3:6, tile(t)] = jnp.where(there, v1, v0)
        stars_new[6:9, tile(t)] = jnp.where(there, a1, a0)
        stars_new[9:12, tile(t)] = jnp.where(there, j1, j0)
        if (t + 1) % piece == 0:
            part_of = (slice(None), slice((t + 1 - piece) * LANES, (t + 1) * LANES))
            copies.append(
                pltpu.make_async_copy(
                    stars_new.at[part_of], stars_out.at[part_of], sems.at[len(copies)]
                )
            )
            copies[-1].start()
    for copy in copies:
        copy.wait()


def local(rows, columns, positions, velocities, accels, jerks, masses, levels, active):
    nlocal = positions.shape[1]
    ntarget = active.shape[0]
    groups = nlocal // LANES
    given = (
        positions,
        velocities,
        accels,
        jerks,
        levels.reshape(groups, LANES),
        masses.reshape(groups, LANES),
        active.reshape(1, ntarget),
    )
    mine, *kept = pl.pallas_call(
        gather_kernel,
        out_shape=(
            pltpu.VMEM((columns, 16, ntarget), f32),
            *(pltpu.VMEM(x.shape, x.dtype) for x in given),
        ),
        in_specs=[HBM] * 7,
        out_specs=(VMEM,) * 8,
        scratch_shapes=[pltpu.SemaphoreType.DMA((11,))],
        compiler_params=PARAMS,
        name="gather",
    )(*(pltpu.with_memory_space_constraint(x, pltpu.HBM) for x in given))
    gathered = lax.all_to_all(mine, "ja", 0, 0, axis_index_groups=[column_order(columns)])
    packed, old = pl.pallas_call(
        force_kernel,
        out_shape=(
            pltpu.VMEM((rows // 2 * columns, 1, NEW_ROWS * ntarget), f32),
            pltpu.VMEM((16, ntarget), f32),
        ),
        in_specs=[VMEM] * 8,
        out_specs=(VMEM, VMEM),
        scratch_shapes=[
            pltpu.VMEM((groups, 7, 8, LANES), f32),
            pltpu.VMEM((6, ntarget, LANES), f32),
            pltpu.VMEM((6, ntarget, LANES), f32),
        ],
        compiler_params=PARAMS,
        name="forces",
    )(gathered, *kept)
    order = pair_order(rows, columns)
    lists = [[(2 * h + core) * columns + c for h, c in order] for core in range(2)]
    same_core = lax.all_to_all(packed, ("ia", "ja"), 0, 0, axis_index_groups=lists)
    other_core = lax.ppermute(same_core, "ia", [(r, r ^ 1) for r in range(rows)])
    return pl.pallas_call(
        functools.partial(finish_kernel, rows, columns),
        out_shape=(
            jax.ShapeDtypeStruct((12, ntarget), f32),
            jax.ShapeDtypeStruct((12, nlocal), f32),
        ),
        in_specs=[VMEM] * 8,
        out_specs=(HBM, HBM),
        scratch_shapes=[
            pltpu.VMEM((12, ntarget), f32),
            pltpu.VMEM((12, nlocal), f32),
            pltpu.VMEM((rows, 8, ntarget), f32),
            pltpu.SemaphoreType.DMA((1 + PIECES,)),
        ],
        compiler_params=PARAMS,
        name="finish",
    )(same_core, other_core, old, *kept[:5])


def solution(mesh):
    rows, columns = mesh.shape["ia"], mesh.shape["ja"]

    def body(*args):
        return local(rows, columns, *args)

    return jax.shard_map(
        body,
        mesh=mesh,
        in_specs=(
            P(None, "ja"),
            P(None, "ja"),
            P(None, "ja"),
            P(None, "ja"),
            P("ja"),
            P("ja"),
            P("ia"),
        ),
        out_specs=(P(None, "ia"), P(None, "ja")),
        check_vma=False,
    )
```

```python
import functools

import jax
import jax.numpy as jnp
from jax import lax
from jax.experimental import pallas as pl
from jax.experimental.pallas import tpu as pltpu
from jax.sharding import PartitionSpec as P

softening_length = 0.01
base_step = 0.0625
LANES = 128
PIECES = 8
NEW_ROWS = 7
f32 = jnp.float32
VMEM = pl.BlockSpec(memory_space=pltpu.VMEM)
HBM = pl.BlockSpec(memory_space=pltpu.HBM)
PARAMS = pltpu.CompilerParams(vmem_limit_bytes=24 * 1024 * 1024)


def elapsed_of(levels):
    return (128 >> levels).astype(f32) * (base_step / 128.0)


def step_factors(elapsed):
    half = elapsed * elapsed * 0.5
    return (elapsed, half, half * elapsed * (1.0 / 3.0))


def predict(pos, vel, acc, jrk, factors):
    elapsed, half, sixth = factors
    pred_pos = pos + elapsed * vel + half * acc + sixth * jrk
    pred_vel = vel + elapsed * acc + half * jrk
    return (pred_pos, pred_vel)


def correction_factors(step):
    return (0.5 * step, step * step * (1.0 / 12.0))


def correct(x0, v0, a0, j0, factors, a1, j1):
    half, quad = factors
    v1 = v0 + half * (a0 + a1) + quad * (j0 - j1)
    x1 = x0 + half * (v0 + v1) + quad * (a0 - a1)
    return (x1, v1)


def column_order(columns):
    first = max(columns - 3, 0)
    return [first, *(c for c in range(columns - 1, -1, -1) if c != first)]


def pair_order(rows, columns):
    natural = [(h, c) for h in range(rows // 2) for c in range(columns)]
    return natural[-1:] + natural[:-1]


def tile(t):
    return slice(t * LANES, (t + 1) * LANES)


def gather_kernel(*refs):
    given, out, kept, sems = (refs[:7], refs[7], refs[8:15], refs[15])
    pos, vel, acc, jrk, levels, masses, active = kept
    groups = levels.shape[0]
    half = groups // 2

    def copy_of(n, sem, columns=None):
        if columns is None:
            return pltpu.make_async_copy(given[n], kept[n], sems.at[sem])
        part = (slice(None), columns)
        return pltpu.make_async_copy(given[n].at[part], kept[n].at[part], sems.at[sem])

    small = [copy_of(6, 0), copy_of(4, 1)]
    parts = [
        [copy_of(n, 2 + 4 * h + n, slice(h * half * LANES, (h + 1) * half * LANES)) for n in range(4)]
        for h in range(2)
    ]
    late = copy_of(5, 10)
    for copy in (*small, *parts[0], *parts[1], late):
        copy.start()
    for copy in small:
        copy.wait()
    offset = active[...] - lax.axis_index("ja") * (groups * LANES)
    group = jnp.broadcast_to(offset >> 7, (8, LANES))
    lane = jnp.broadcast_to(offset & (LANES - 1), (8, LANES))
    row = lax.broadcasted_iota(jnp.int32, (8, LANES), 0)
    elapsed = elapsed_of(levels[...])
    steps = jnp.zeros((8, LANES), f32)
    for t in range(0, groups, 8):
        here = group == row + t
        steps = jnp.where(here, jnp.take_along_axis(elapsed[t : t + 8], lane, axis=1), steps)
    found = [jnp.zeros((3, LANES), f32)] * 4
    for h in range(2):
        for copy in parts[h]:
            copy.wait()
        for t in range(h * half, (h + 1) * half):
            here = group[0:3] == t
            found = [
                jnp.where(here, jnp.take_along_axis(x[:, tile(t)], lane[0:3], axis=1), old)
                for x, old in zip((pos, vel, acc, jrk), found)
            ]
    steps = jnp.broadcast_to(jnp.sum(steps, axis=0, keepdims=True), (4, LANES))
    for k in range(out.shape[0]):
        for n, value in enumerate(found):
            out[k, 3 * n : 3 * n + 3, :] = value
        out[k, 12:16, :] = steps
    late.wait()


def force_kernel(
    gathered, pos, vel, acc, jrk, levels, masses, active, packed, old, sources, targets, sums
):
    groups = levels.shape[0]
    ntarget = active.shape[1]
    state = gathered[0]
    for k in range(1, gathered.shape[0]):
        state = state + gathered[k]
    old[...] = state
    tpos, tvel = predict(
        state[0:3], state[3:6], state[6:9], state[9:12], step_factors(state[12:13])
    )
    columns = jnp.transpose(
        jnp.concatenate([tpos, tvel, jnp.zeros((LANES - 6, ntarget), f32)], axis=0)
    )
    for c in range(6):
        targets[c] = jnp.broadcast_to(columns[:, c : c + 1], (ntarget, LANES))
    factors = step_factors(elapsed_of(levels[...]))
    for t in range(groups):
        spos, svel = predict(
            *(x[:, tile(t)] for x in (pos, vel, acc, jrk)), [f[t : t + 1] for f in factors]
        )
        for c in range(3):
            sources[t, c] = jnp.broadcast_to(spos[c : c + 1], (8, LANES))
            sources[t, 3 + c] = jnp.broadcast_to(svel[c : c + 1], (8, LANES))
        sources[t, 6] = jnp.broadcast_to(masses[t : t + 1, :], (8, LANES))

    def one_group(g, unused):
        rows = pl.ds(pl.multiple_of(g * 8, 8), 8)
        tx, ty, tz, tu, tv, tw = (targets[c, rows, :] for c in range(6))

        def one_tile(t, carry):
            dx, dy, dz = (sources[t, 0] - tx, sources[t, 1] - ty, sources[t, 2] - tz)
            du, dv, dw = (sources[t, 3] - tu, sources[t, 4] - tv, sources[t, 5] - tw)
            r2 = dx * dx + dy * dy + dz * dz + softening_length
            inv = lax.rsqrt(r2)
            inv_sq = inv * inv
            weight = sources[t, 6] * inv * inv_sq
            radial = (dx * du + dy * dv + dz * dw) * inv_sq
            px, py, pz = (weight * dx, weight * dy, weight * dz)
            ax, ay, az, jx, jy, jz, kx, ky, kz = carry
            return (
                ax + px,
                ay + py,
                az + pz,
                jx + weight * du,
                jy + weight * dv,
                jz + weight * dw,
                kx + radial * px,
                ky + radial * py,
                kz + radial * pz,
            )

        zero = jnp.zeros((8, LANES), f32)
        ax, ay, az, jx, jy, jz, kx, ky, kz = lax.fori_loop(
            0, groups, one_tile, (zero,) * 9, unroll=32
        )
        for c, value in enumerate((ax, ay, az, jx - 3.0 * kx, jy - 3.0 * ky, jz - 3.0 * kz)):
            sums[c, rows, :] = value
        return unused

    lax.fori_loop(0, ntarget // 8, one_group, 0)
    lane = lax.broadcasted_iota(jnp.int32, (ntarget, LANES), 1)
    table = jnp.zeros((ntarget, LANES), f32)
    for c in range(6):
        table = jnp.where(lane == c, jnp.sum(sums[c], axis=1, keepdims=True), table)
    table = jnp.transpose(table)[0:8]
    row = lax.broadcasted_iota(jnp.int32, (8, ntarget), 0)
    table = jnp.where(row == 6, active[...].astype(f32), table)
    for k in range(packed.shape[0]):
        for c in range(NEW_ROWS):
            packed[k, :, tile(c)] = table[c : c + 1]


def finish_kernel(
    rows, columns, same_core, other_core, old, pos, vel, acc, jrk, levels, targets_out, stars_out,
    targets_new, stars_new, rowed, sems
):
    groups = levels.shape[0]
    ntarget = old.shape[1]
    me = lax.axis_index("ia")
    base = lax.axis_index("ja") * (groups * LANES)

    forces, where_hi, where_lo = ([], [], [])
    mine = jnp.zeros((8, ntarget), f32)
    order = pair_order(rows, columns)
    for r in range(rows):
        everyone = same_core if r < rows // 2 else other_core
        first, *others = [k for k, (h, _) in enumerate(order) if h == r % (rows // 2)]
        total = everyone[first]
        for k in others:
            total = total + everyone[k]
        for c in range(6):
            rowed[r, c : c + 1, :] = total[:, tile(c)]
        forces.append(rowed[r])
        mine = jnp.where((me >> 1) == r, forces[r], mine)
        offset = everyone[first][:, tile(6)].astype(jnp.int32) - base
        where_hi.append(offset >> 7)
        where_lo.append(offset & (LANES - 1))

    o = old[...]
    factors = correction_factors(o[12:13])
    x1, v1 = correct(o[0:3], o[3:6], o[6:9], o[9:12], factors, mine[0:3], mine[3:6])
    targets_new[0:3, :] = x1
    targets_new[3:6, :] = v1
    targets_new[6:12, :] = mine[0:6]
    copies = [pltpu.make_async_copy(targets_new, targets_out, sems.at[0])]
    copies[0].start()
    piece = groups // PIECES

    group = lax.broadcasted_iota(jnp.int32, (groups, ntarget), 0)
    lane = lax.broadcasted_iota(jnp.int32, (LANES, ntarget), 0)
    number = lax.broadcasted_iota(jnp.int32, (groups, ntarget), 1).astype(f32) + 1.0
    spot = jnp.zeros((groups, LANES), f32)
    part = jnp.zeros((groups, LANES), f32)
    for r in range(rows):
        hit = group == where_hi[r]
        side = (lane == where_lo[r]).astype(jnp.bfloat16)
        found = lax.dot_general(
            jnp.where(hit, number, 0.0).astype(jnp.bfloat16),
            side,
            (((1,), (1,)), ((), ())),
            preferred_element_type=f32,
        )
        part = jnp.where(found > 0.5, float(r), part)
        spot = spot + found
    present = spot > 0.5
    slot = jnp.where(present, spot - 1.0, 0.0).astype(jnp.int32)
    part = jnp.where(present, part, -1.0)
    factors = correction_factors(elapsed_of(levels[...]))
    for t in range(groups):
        lanes = jnp.broadcast_to(slot[t : t + 1], (8, LANES))
        holder = jnp.broadcast_to(part[t : t + 1], (8, LANES))
        new = jnp.zeros((8, LANES), f32)
        for r in range(rows):
            new = jnp.where(holder == float(r), jnp.take_along_axis(forces[r], lanes, axis=1), new)
        there = holder[0:3] > -0.5
        x0, v0, a0, j0 = (pos[:, tile(t)], vel[:, tile(t)], acc[:, tile(t)], jrk[:, tile(t)])
        a1, j1 = (new[0:3], new[3:6])
        x1, v1 = correct(x0, v0, a0, j0, [f[t : t + 1] for f in factors], a1, j1)
        stars_new[0:3, tile(t)] = jnp.where(there, x1, x0)
        stars_new[3:6, tile(t)] = jnp.where(there, v1, v0)
        stars_new[6:9, tile(t)] = jnp.where(there, a1, a0)
        stars_new[9:12, tile(t)] = jnp.where(there, j1, j0)
        if (t + 1) % piece == 0:
            part_of = (slice(None), slice((t + 1 - piece) * LANES, (t + 1) * LANES))
            copies.append(
                pltpu.make_async_copy(
                    stars_new.at[part_of], stars_out.at[part_of], sems.at[len(copies)]
                )
            )
            copies[-1].start()
    for copy in copies:
        copy.wait()


def local(rows, columns, positions, velocities, accels, jerks, masses, levels, active):
    nlocal = positions.shape[1]
    ntarget = active.shape[0]
    groups = nlocal // LANES
    given = (
        positions,
        velocities,
        accels,
        jerks,
        levels.reshape(groups, LANES),
        masses.reshape(groups, LANES),
        active.reshape(1, ntarget),
    )
    mine, *kept = pl.pallas_call(
        gather_kernel,
        out_shape=(
            pltpu.VMEM((columns, 16, ntarget), f32),
            *(pltpu.VMEM(x.shape, x.dtype) for x in given),
        ),
        in_specs=[HBM] * 7,
        out_specs=(VMEM,) * 8,
        scratch_shapes=[pltpu.SemaphoreType.DMA((11,))],
        compiler_params=PARAMS,
        name="gather",
    )(*(pltpu.with_memory_space_constraint(x, pltpu.HBM) for x in given))
    gathered = lax.all_to_all(mine, "ja", 0, 0, axis_index_groups=[column_order(columns)])
    packed, old = pl.pallas_call(
        force_kernel,
        out_shape=(
            pltpu.VMEM((rows // 2 * columns, 1, NEW_ROWS * ntarget), f32),
            pltpu.VMEM((16, ntarget), f32),
        ),
        in_specs=[VMEM] * 8,
        out_specs=(VMEM, VMEM),
        scratch_shapes=[
            pltpu.VMEM((groups, 7, 8, LANES), f32),
            pltpu.VMEM((6, ntarget, LANES), f32),
            pltpu.VMEM((6, ntarget, LANES), f32),
        ],
        compiler_params=PARAMS,
        name="forces",
    )(gathered, *kept)
    order = pair_order(rows, columns)
    lists = [[(2 * h + core) * columns + c for h, c in order] for core in range(2)]
    same_core = lax.all_to_all(packed, ("ia", "ja"), 0, 0, axis_index_groups=lists)
    other_core = lax.ppermute(same_core, "ia", [(r, r ^ 1) for r in range(rows)])
    return pl.pallas_call(
        functools.partial(finish_kernel, rows, columns),
        out_shape=(
            jax.ShapeDtypeStruct((12, ntarget), f32),
            jax.ShapeDtypeStruct((12, nlocal), f32),
        ),
        in_specs=[VMEM] * 8,
        out_specs=(HBM, HBM),
        scratch_shapes=[
            pltpu.VMEM((12, ntarget), f32),
            pltpu.VMEM((12, nlocal), f32),
            pltpu.VMEM((rows, 8, ntarget), f32),
            pltpu.SemaphoreType.DMA((1 + PIECES,)),
        ],
        compiler_params=PARAMS,
        name="finish",
    )(same_core, other_core, old, *kept[:5])


def solution(mesh):
    rows, columns = mesh.shape["ia"], mesh.shape["ja"]

    def body(*args):
        return local(rows, columns, *args)

    return jax.shard_map(
        body,
        mesh=mesh,
        in_specs=(
            P(None, "ja"),
            P(None, "ja"),
            P(None, "ja"),
            P(None, "ja"),
            P("ja"),
            P("ja"),
            P("ia"),
        ),
        out_specs=(P(None, "ia"), P(None, "ja")),
        check_vma=False,
    )
```

```python
import functools

import jax
import jax.numpy as jnp
from jax import lax
from jax.experimental import pallas as pl
from jax.experimental.pallas import tpu as pltpu
from jax.sharding import PartitionSpec as P

softening_length = 0.01
base_step = 0.0625
LANES = 128
PIECES = 8
NEW_ROWS = 9
f32 = jnp.float32
VMEM = pl.BlockSpec(memory_space=pltpu.VMEM)
HBM = pl.BlockSpec(memory_space=pltpu.HBM)
PARAMS = pltpu.CompilerParams(vmem_limit_bytes=24 * 1024 * 1024)


def elapsed_of(levels):
    return (128 >> levels).astype(f32) * (base_step / 128.0)


def step_factors(elapsed):
    half = elapsed * elapsed * 0.5
    return (elapsed, half, half * elapsed * (1.0 / 3.0))


def predict(pos, vel, acc, jrk, factors):
    elapsed, half, sixth = factors
    pred_pos = pos + elapsed * vel + half * acc + sixth * jrk
    pred_vel = vel + elapsed * acc + half * jrk
    return (pred_pos, pred_vel)


def correction_factors(step):
    return (0.5 * step, step * step * (1.0 / 12.0))


def correct(x0, v0, a0, j0, factors, a1, j1):
    half, quad = factors
    v1 = v0 + half * (a0 + a1) + quad * (j0 - j1)
    x1 = x0 + half * (v0 + v1) + quad * (a0 - a1)
    return (x1, v1)


def column_order(columns):
    first = max(columns - 3, 0)
    return [first, *(c for c in range(columns - 1, -1, -1) if c != first)]


def pair_order(rows, columns):
    natural = [(h, c) for h in range(rows // 2) for c in range(columns)]
    return natural[-1:] + natural[:-1]


def tile(t):
    return slice(t * LANES, (t + 1) * LANES)


def gather_kernel(*refs):
    given, out, kept, sems = (refs[:7], refs[7], refs[8:15], refs[15])
    pos, vel, acc, jrk, levels, masses, active = kept
    groups = levels.shape[0]
    half = groups // 2

    def copy_of(n, sem, columns=None):
        if columns is None:
            return pltpu.make_async_copy(given[n], kept[n], sems.at[sem])
        part = (slice(None), columns)
        return pltpu.make_async_copy(given[n].at[part], kept[n].at[part], sems.at[sem])

    small = [copy_of(6, 0), copy_of(4, 1)]
    parts = [
        [copy_of(n, 2 + 4 * h + n, slice(h * half * LANES, (h + 1) * half * LANES)) for n in range(4)]
        for h in range(2)
    ]
    late = copy_of(5, 10)
    for copy in (*small, *parts[0], *parts[1], late):
        copy.start()
    for copy in small:
        copy.wait()
    offset = active[...] - lax.axis_index("ja") * (groups * LANES)
    group = jnp.broadcast_to(offset >> 7, (8, LANES))
    lane = jnp.broadcast_to(offset & (LANES - 1), (8, LANES))
    row = lax.broadcasted_iota(jnp.int32, (8, LANES), 0)
    elapsed = elapsed_of(levels[...])
    steps = jnp.zeros((8, LANES), f32)
    for t in range(0, groups, 8):
        here = group == row + t
        steps = jnp.where(here, jnp.take_along_axis(elapsed[t : t + 8], lane, axis=1), steps)
    found = [jnp.zeros((3, LANES), f32)] * 4
    for h in range(2):
        for copy in parts[h]:
            copy.wait()
        for t in range(h * half, (h + 1) * half):
            here = group[0:3] == t
            found = [
                jnp.where(here, jnp.take_along_axis(x[:, tile(t)], lane[0:3], axis=1), old)
                for x, old in zip((pos, vel, acc, jrk), found)
            ]
    steps = jnp.broadcast_to(jnp.sum(steps, axis=0, keepdims=True), (4, LANES))
    for k in range(out.shape[0]):
        for n, value in enumerate(found):
            out[k, 3 * n : 3 * n + 3, :] = value
        out[k, 12:16, :] = steps
    late.wait()


def pack(values):
    quarter = lax.broadcasted_iota(jnp.int32, (1, LANES), 1) // (LANES // 4)
    rows = []
    for part in (values[:4], values[4:]):
        row = jnp.zeros((1, LANES), f32)
        for n, value in enumerate(part):
            turned = pltpu.roll(value, (n + 1) * (LANES // 4) % LANES, 1)
            row = jnp.where(quarter == n, turned, row)
        rows.append(row)
    return rows


def unpack(rows):
    last = lax.broadcasted_iota(jnp.int32, (1, LANES), 1) >= LANES - LANES // 4
    values = []
    for c in range(6):
        turned = pltpu.roll(rows[c // 4], (3 - c % 4) * (LANES // 4), 1)
        values.append(jnp.where(last, turned, 0.0))
    return values


def spread(values, targets, rows):
    fill = jnp.zeros((LANES - 6, LANES), f32)
    columns = jnp.transpose(jnp.concatenate([*values, fill], axis=0))
    for c in range(6):
        targets[c] = jnp.broadcast_to(columns[rows, c : c + 1], targets.shape[1:])


def predicted(state):
    return predict(*(state[n : n + 3] for n in (0, 3, 6, 9)), step_factors(state[12:13]))


def summed(blocks):
    total = blocks[0]
    for k in range(1, blocks.shape[0]):
        total = total + blocks[k]
    return total


def pair_sums(sources, targets, sums, count):
    def one_group(g, unused):
        rows = pl.ds(pl.multiple_of(g * 8, 8), 8)
        tx, ty, tz, tu, tv, tw = (targets[c, rows, :] for c in range(6))

        def one_tile(t, carry):
            dx, dy, dz = (sources[t, 0] - tx, sources[t, 1] - ty, sources[t, 2] - tz)
            du, dv, dw = (sources[t, 3] - tu, sources[t, 4] - tv, sources[t, 5] - tw)
            r2 = dx * dx + dy * dy + dz * dz + softening_length
            inv = lax.rsqrt(r2)
            inv_sq = inv * inv
            weight = sources[t, 6] * inv * inv_sq
            radial = (dx * du + dy * dv + dz * dw) * inv_sq
            px, py, pz = (weight * dx, weight * dy, weight * dz)
            ax, ay, az, jx, jy, jz, kx, ky, kz = carry
            return (
                ax + px,
                ay + py,
                az + pz,
                jx + weight * du,
                jy + weight * dv,
                jz + weight * dw,
                kx + radial * px,
                ky + radial * py,
                kz + radial * pz,
            )

        zero = jnp.zeros((8, LANES), f32)
        ax, ay, az, jx, jy, jz, kx, ky, kz = lax.fori_loop(
            0, sources.shape[0], one_tile, (zero,) * 9, unroll=32
        )
        for c, value in enumerate((ax, ay, az, jx - 3.0 * kx, jy - 3.0 * ky, jz - 3.0 * kz)):
            sums[c, rows, :] = value
        return unused

    lax.fori_loop(0, count, one_group, 0)


def as_rows(sums):
    count = sums.shape[1]
    lane = lax.broadcasted_iota(jnp.int32, (count, LANES), 1)
    table = jnp.zeros((count, LANES), f32)
    for c in range(6):
        table = jnp.where(lane == c, jnp.sum(sums[c], axis=1, keepdims=True), table)
    if count < LANES:
        table = jnp.concatenate([jnp.zeros((LANES - count, LANES), f32), table], axis=0)
    return jnp.transpose(table)[0:8]


def force_kernel(
    gathered, pos, vel, acc, jrk, levels, masses, active, own, old, sources, targets, sums
):
    groups = levels.shape[0]
    ntarget = active.shape[1]
    state = summed(gathered)
    old[...] = state
    tpos, tvel = predicted(state)
    spread([tpos, tvel], targets, slice(0, ntarget))
    factors = step_factors(elapsed_of(levels[...]))
    for t in range(groups):
        spos, svel = predict(
            *(x[:, tile(t)] for x in (pos, vel, acc, jrk)), [f[t : t + 1] for f in factors]
        )
        for c in range(3):
            sources[t, c] = jnp.broadcast_to(spos[c : c + 1], (8, LANES))
            sources[t, 3 + c] = jnp.broadcast_to(svel[c : c + 1], (8, LANES))
        sources[t, 6] = jnp.broadcast_to(masses[t : t + 1, :], (8, LANES))
    given = ntarget // 4
    for c in range(6):
        sums[c, ntarget - given :] = jnp.zeros((given, LANES), f32)
    mine = (ntarget - given) // 8 + given // 8 * (lax.axis_index("ia") % 2)
    pair_sums(sources, targets, sums, mine)
    row = lax.broadcasted_iota(jnp.int32, (8, ntarget), 0)
    own[...] = jnp.where(row == 6, active[...].astype(f32), as_rows(sums))


def taken_kernel(handed, sources, own, packed, taken, targets, sums):
    given = targets.shape[1]
    taken[...] = jnp.zeros(taken.shape, f32)

    @pl.when(lax.axis_index("ia") % 2 == 1)
    def _():
        tpos, tvel = predicted(summed(handed))
        spread([tpos, tvel], targets, slice(LANES - given, LANES))
        pair_sums(sources, targets, sums, given // 8)
        for n, value in enumerate(pack([row for row in split_rows(as_rows(sums), 6)])):
            taken[n : n + 1, :] = value

    rows = [*split_rows(own[...], 7), *split_rows(taken[...], 2)]
    for k in range(packed.shape[0]):
        for c, value in enumerate(rows):
            packed[k, :, tile(c)] = value


def split_rows(x, count):
    return [x[c : c + 1] for c in range(count)]


def finish_kernel(
    rows, columns, same_core, other_core, old, pos, vel, acc, jrk, levels, targets_out, stars_out,
    targets_new, stars_new, rowed, taken, sems
):
    groups = levels.shape[0]
    ntarget = old.shape[1]
    me = lax.axis_index("ia")
    base = lax.axis_index("ja") * (groups * LANES)

    forces, where_hi, where_lo = ([], [], [])
    mine = jnp.zeros((8, ntarget), f32)
    order = pair_order(rows, columns)
    half = rows // 2
    for r in range(rows):
        everyone, other = (same_core, r + half) if r < half else (other_core, r - half)
        first, *others = [k for k, (h, _) in enumerate(order) if h == r % half]
        total = everyone[first]
        for k in others:
            total = total + everyone[k]
        for c in range(6):
            rowed[r, c : c + 1, :] = total[:, tile(c)]
        for c, value in enumerate(unpack([total[:, tile(7)], total[:, tile(8)]])):
            taken[other, c : c + 1, :] = value
        offset = everyone[first][:, tile(6)].astype(jnp.int32) - base
        where_hi.append(offset >> 7)
        where_lo.append(offset & (LANES - 1))
    for r in range(rows):
        forces.append(rowed[r] + taken[r])
        mine = jnp.where((me >> 1) == r, forces[r], mine)

    o = old[...]
    factors = correction_factors(o[12:13])
    x1, v1 = correct(o[0:3], o[3:6], o[6:9], o[9:12], factors, mine[0:3], mine[3:6])
    targets_new[0:3, :] = x1
    targets_new[3:6, :] = v1
    targets_new[6:12, :] = mine[0:6]
    copies = [pltpu.make_async_copy(targets_new, targets_out, sems.at[0])]
    copies[0].start()
    piece = groups // PIECES

    group = lax.broadcasted_iota(jnp.int32, (groups, ntarget), 0)
    lane = lax.broadcasted_iota(jnp.int32, (LANES, ntarget), 0)
    number = lax.broadcasted_iota(jnp.int32, (groups, ntarget), 1).astype(f32) + 1.0
    spot = jnp.zeros((groups, LANES), f32)
    part = jnp.zeros((groups, LANES), f32)
    for r in range(rows):
        hit = group == where_hi[r]
        side = (lane == where_lo[r]).astype(jnp.bfloat16)
        found = lax.dot_general(
            jnp.where(hit, number, 0.0).astype(jnp.bfloat16),
            side,
            (((1,), (1,)), ((), ())),
            preferred_element_type=f32,
        )
        part = jnp.where(found > 0.5, float(r), part)
        spot = spot + found
    present = spot > 0.5
    slot = jnp.where(present, spot - 1.0, 0.0).astype(jnp.int32)
    part = jnp.where(present, part, -1.0)
    factors = correction_factors(elapsed_of(levels[...]))
    for t in range(groups):
        lanes = jnp.broadcast_to(slot[t : t + 1], (8, LANES))
        holder = jnp.broadcast_to(part[t : t + 1], (8, LANES))
        new = jnp.zeros((8, LANES), f32)
        for r in range(rows):
            new = jnp.where(holder == float(r), jnp.take_along_axis(forces[r], lanes, axis=1), new)
        there = holder[0:3] > -0.5
        x0, v0, a0, j0 = (pos[:, tile(t)], vel[:, tile(t)], acc[:, tile(t)], jrk[:, tile(t)])
        a1, j1 = (new[0:3], new[3:6])
        x1, v1 = correct(x0, v0, a0, j0, [f[t : t + 1] for f in factors], a1, j1)
        stars_new[0:3, tile(t)] = jnp.where(there, x1, x0)
        stars_new[3:6, tile(t)] = jnp.where(there, v1, v0)
        stars_new[6:9, tile(t)] = jnp.where(there, a1, a0)
        stars_new[9:12, tile(t)] = jnp.where(there, j1, j0)
        if (t + 1) % piece == 0:
            part_of = (slice(None), slice((t + 1 - piece) * LANES, (t + 1) * LANES))
            copies.append(
                pltpu.make_async_copy(
                    stars_new.at[part_of], stars_out.at[part_of], sems.at[len(copies)]
                )
            )
            copies[-1].start()
    for copy in copies:
        copy.wait()


def local(rows, columns, positions, velocities, accels, jerks, masses, levels, active):
    nlocal = positions.shape[1]
    ntarget = active.shape[0]
    groups = nlocal // LANES
    given = (
        positions,
        velocities,
        accels,
        jerks,
        levels.reshape(groups, LANES),
        masses.reshape(groups, LANES),
        active.reshape(1, ntarget),
    )
    mine, *kept = pl.pallas_call(
        gather_kernel,
        out_shape=(
            pltpu.VMEM((columns, 16, ntarget), f32),
            *(pltpu.VMEM(x.shape, x.dtype) for x in given),
        ),
        in_specs=[HBM] * 7,
        out_specs=(VMEM,) * 8,
        scratch_shapes=[pltpu.SemaphoreType.DMA((11,))],
        compiler_params=PARAMS,
        name="gather",
    )(*(pltpu.with_memory_space_constraint(x, pltpu.HBM) for x in given))
    gathered = lax.all_to_all(mine, "ja", 0, 0, axis_index_groups=[column_order(columns)])
    handed = lax.ppermute(gathered, "ia", [(r, r + 1) for r in range(0, rows, 2)])
    own, old, sources = pl.pallas_call(
        force_kernel,
        out_shape=(
            pltpu.VMEM((8, ntarget), f32),
            pltpu.VMEM((16, ntarget), f32),
            pltpu.VMEM((groups, 7, 8, LANES), f32),
        ),
        in_specs=[VMEM] * 8,
        out_specs=(VMEM,) * 3,
        scratch_shapes=[pltpu.VMEM((6, ntarget, LANES), f32)] * 2,
        compiler_params=PARAMS,
        cost_estimate=pl.CostEstimate(
            flops=40 * nlocal * ntarget,
            bytes_accessed=4 * 80 * nlocal,
            transcendentals=nlocal * ntarget,
        ),
        name="forces",
    )(gathered, *kept)
    packed = pl.pallas_call(
        taken_kernel,
        out_shape=pltpu.VMEM((rows // 2 * columns, 1, NEW_ROWS * ntarget), f32),
        in_specs=[VMEM] * 3,
        out_specs=VMEM,
        scratch_shapes=[
            pltpu.VMEM((2, ntarget), f32),
            pltpu.VMEM((6, ntarget // 4, LANES), f32),
            pltpu.VMEM((6, ntarget // 4, LANES), f32),
        ],
        compiler_params=PARAMS,
        name="taken",
    )(handed, sources, own)
    order = pair_order(rows, columns)
    lists = [[(2 * h + core) * columns + c for h, c in order] for core in range(2)]
    same_core = lax.all_to_all(packed, ("ia", "ja"), 0, 0, axis_index_groups=lists)
    other_core = lax.ppermute(same_core, "ia", [(r, r ^ 1) for r in range(rows)])
    return pl.pallas_call(
        functools.partial(finish_kernel, rows, columns),
        out_shape=(
            jax.ShapeDtypeStruct((12, ntarget), f32),
            jax.ShapeDtypeStruct((12, nlocal), f32),
        ),
        in_specs=[VMEM] * 8,
        out_specs=(HBM, HBM),
        scratch_shapes=[
            pltpu.VMEM((12, ntarget), f32),
            pltpu.VMEM((12, nlocal), f32),
            pltpu.VMEM((rows, 8, ntarget), f32),
            pltpu.VMEM((rows, 8, ntarget), f32),
            pltpu.SemaphoreType.DMA((1 + PIECES,)),
        ],
        compiler_params=PARAMS,
        name="finish",
    )(same_core, other_core, old, *kept[:5])


def solution(mesh):
    rows, columns = mesh.shape["ia"], mesh.shape["ja"]

    def body(*args):
        return local(rows, columns, *args)

    return jax.shard_map(
        body,
        mesh=mesh,
        in_specs=(
            P(None, "ja"),
            P(None, "ja"),
            P(None, "ja"),
            P(None, "ja"),
            P("ja"),
            P("ja"),
            P("ia"),
        ),
        out_specs=(P(None, "ia"), P(None, "ja")),
        check_vma=False,
    )
```

```python
import functools

import jax
import jax.numpy as jnp
from jax import lax
from jax.experimental import pallas as pl
from jax.experimental.pallas import tpu as pltpu
from jax.sharding import PartitionSpec as P

softening_length = 0.01
base_step = 0.0625
LANES = 128
PIECES = 8
NEW_ROWS = 7
f32 = jnp.float32
VMEM = pl.BlockSpec(memory_space=pltpu.VMEM)
HBM = pl.BlockSpec(memory_space=pltpu.HBM)
PARAMS = pltpu.CompilerParams(vmem_limit_bytes=24 * 1024 * 1024)


def elapsed_of(levels):
    return (128 >> levels).astype(f32) * (base_step / 128.0)


def step_factors(elapsed):
    half = elapsed * elapsed * 0.5
    return (elapsed, half, half * elapsed * (1.0 / 3.0))


def predict(pos, vel, acc, jrk, factors):
    elapsed, half, sixth = factors
    pred_pos = pos + elapsed * vel + half * acc + sixth * jrk
    pred_vel = vel + elapsed * acc + half * jrk
    return (pred_pos, pred_vel)


def correction_factors(step):
    return (0.5 * step, step * step * (1.0 / 12.0))


def correct(x0, v0, a0, j0, factors, a1, j1):
    half, quad = factors
    v1 = v0 + half * (a0 + a1) + quad * (j0 - j1)
    x1 = x0 + half * (v0 + v1) + quad * (a0 - a1)
    return (x1, v1)


def column_order(columns):
    first = max(columns - 3, 0)
    return [first, *(c for c in range(columns - 1, -1, -1) if c != first)]


def pair_order(rows, columns):
    natural = [(h, c) for h in range(rows // 2) for c in range(columns)]
    return natural[-1:] + natural[:-1]


def tile(t):
    return slice(t * LANES, (t + 1) * LANES)


def gather_kernel(*refs):
    given, out, kept, sems = (refs[:7], refs[7], refs[8:15], refs[15])
    pos, vel, acc, jrk, levels, masses, active = kept
    groups = levels.shape[0]
    half = groups // 2

    def copy_of(n, sem, columns=None):
        if columns is None:
            return pltpu.make_async_copy(given[n], kept[n], sems.at[sem])
        part = (slice(None), columns)
        return pltpu.make_async_copy(given[n].at[part], kept[n].at[part], sems.at[sem])

    small = [copy_of(6, 0), copy_of(4, 1)]
    parts = [
        [copy_of(n, 2 + 4 * h + n, slice(h * half * LANES, (h + 1) * half * LANES)) for n in range(4)]
        for h in range(2)
    ]
    late = copy_of(5, 10)
    for copy in (*small, *parts[0], *parts[1], late):
        copy.start()
    for copy in small:
        copy.wait()
    offset = active[...] - lax.axis_index("ja") * (groups * LANES)
    group = jnp.broadcast_to(offset >> 7, (8, LANES))
    lane = jnp.broadcast_to(offset & (LANES - 1), (8, LANES))
    row = lax.broadcasted_iota(jnp.int32, (8, LANES), 0)
    elapsed = elapsed_of(levels[...])
    steps = jnp.zeros((8, LANES), f32)
    for t in range(0, groups, 8):
        here = group == row + t
        steps = jnp.where(here, jnp.take_along_axis(elapsed[t : t + 8], lane, axis=1), steps)
    found = [jnp.zeros((3, LANES), f32)] * 4
    for h in range(2):
        for copy in parts[h]:
            copy.wait()
        for t in range(h * half, (h + 1) * half):
            here = group[0:3] == t
            found = [
                jnp.where(here, jnp.take_along_axis(x[:, tile(t)], lane[0:3], axis=1), old)
                for x, old in zip((pos, vel, acc, jrk), found)
            ]
    steps = jnp.broadcast_to(jnp.sum(steps, axis=0, keepdims=True), (4, LANES))
    for k in range(out.shape[0]):
        for n, value in enumerate(found):
            out[k, 3 * n : 3 * n + 3, :] = value
        out[k, 12:16, :] = steps
    late.wait()


def force_kernel(
    gathered, pos, vel, acc, jrk, levels, masses, active, packed, old, sources, targets, sums
):
    groups = levels.shape[0]
    ntarget = active.shape[1]
    state = gathered[0]
    for k in range(1, gathered.shape[0]):
        state = state + gathered[k]
    old[...] = state
    tpos, tvel = predict(
        state[0:3], state[3:6], state[6:9], state[9:12], step_factors(state[12:13])
    )
    columns = jnp.transpose(
        jnp.concatenate([tpos, tvel, jnp.zeros((LANES - 6, ntarget), f32)], axis=0)
    )
    for c in range(6):
        targets[c] = jnp.broadcast_to(columns[:, c : c + 1], (ntarget, LANES))
    factors = step_factors(elapsed_of(levels[...]))
    for t in range(groups):
        spos, svel = predict(
            *(x[:, tile(t)] for x in (pos, vel, acc, jrk)), [f[t : t + 1] for f in factors]
        )
        for c in range(3):
            sources[t, c] = jnp.broadcast_to(spos[c : c + 1], (8, LANES))
            sources[t, 3 + c] = jnp.broadcast_to(svel[c : c + 1], (8, LANES))
        sources[t, 6] = jnp.broadcast_to(masses[t : t + 1, :], (8, LANES))

    def one_group(g, unused):
        rows = pl.ds(pl.multiple_of(g * 8, 8), 8)
        tx, ty, tz, tu, tv, tw = (targets[c, rows, :] for c in range(6))

        def one_tile(t, carry):
            dx, dy, dz = (sources[t, 0] - tx, sources[t, 1] - ty, sources[t, 2] - tz)
            du, dv, dw = (sources[t, 3] - tu, sources[t, 4] - tv, sources[t, 5] - tw)
            r2 = dx * dx + dy * dy + dz * dz + softening_length
            inv = lax.rsqrt(r2)
            inv_sq = inv * inv
            weight = sources[t, 6] * inv * inv_sq
            radial = (dx * du + dy * dv + dz * dw) * inv_sq
            px, py, pz = (weight * dx, weight * dy, weight * dz)
            ax, ay, az, jx, jy, jz, kx, ky, kz = carry
            return (
                ax + px,
                ay + py,
                az + pz,
                jx + weight * du,
                jy + weight * dv,
                jz + weight * dw,
                kx + radial * px,
                ky + radial * py,
                kz + radial * pz,
            )

        zero = jnp.zeros((8, LANES), f32)
        ax, ay, az, jx, jy, jz, kx, ky, kz = lax.fori_loop(
            0, groups, one_tile, (zero,) * 9, unroll=32
        )
        for c, value in enumerate((ax, ay, az, jx - 3.0 * kx, jy - 3.0 * ky, jz - 3.0 * kz)):
            sums[c, rows, :] = value
        return unused

    lax.fori_loop(0, ntarget // 8, one_group, 0)
    lane = lax.broadcasted_iota(jnp.int32, (ntarget, LANES), 1)
    table = jnp.zeros((ntarget, LANES), f32)
    for c in range(6):
        table = jnp.where(lane == c, jnp.sum(sums[c], axis=1, keepdims=True), table)
    table = jnp.transpose(table)[0:8]
    row = lax.broadcasted_iota(jnp.int32, (8, ntarget), 0)
    table = jnp.where(row == 6, active[...].astype(f32), table)
    for k in range(packed.shape[0]):
        for c in range(NEW_ROWS):
            packed[k, :, tile(c)] = table[c : c + 1]


def laid_out(rows, columns, everyone, rowed, groups, before):
    ntarget = rowed.shape[2]
    base = lax.axis_index("ja") * (groups * LANES)
    order = pair_order(rows, columns)
    group = lax.broadcasted_iota(jnp.int32, (groups, ntarget), 0)
    lane = lax.broadcasted_iota(jnp.int32, (LANES, ntarget), 0)
    number = lax.broadcasted_iota(jnp.int32, (groups, ntarget), 1).astype(f32) + 1.0
    spot = jnp.zeros((groups, LANES), f32)
    part = jnp.full((groups, LANES), -1.0, f32)
    forces = []
    for r in range(rows // 2):
        first, *others = [k for k, (h, _) in enumerate(order) if h == r]
        total = everyone[first]
        for k in others:
            total = total + everyone[k]
        for c in range(6):
            rowed[r, c : c + 1, :] = total[:, tile(c)]
        rowed[r, 6:8, :] = jnp.ones((2, ntarget), f32)
        forces.append(rowed[r])
        offset = everyone[first][:, tile(6)].astype(jnp.int32) - base
        hit = group == offset >> 7
        side = (lane == (offset & (LANES - 1))).astype(jnp.bfloat16)
        found = lax.dot_general(
            jnp.where(hit, number, 0.0).astype(jnp.bfloat16),
            side,
            (((1,), (1,)), ((), ())),
            preferred_element_type=f32,
        )
        part = jnp.where(found > 0.5, float(r), part)
        spot = spot + found
    slot = jnp.maximum(spot - 1.0, 0.0).astype(jnp.int32)
    for t in range(groups):
        lanes = jnp.broadcast_to(slot[t : t + 1], (8, LANES))
        holder = jnp.broadcast_to(part[t : t + 1], (8, LANES))
        new = before(t)
        for r in range(rows // 2):
            new = jnp.where(holder == float(r), jnp.take_along_axis(forces[r], lanes, axis=1), new)
        yield new


def same_kernel(rows, columns, same_core, old, targets_new, placed, rowed):
    zero = jnp.zeros((8, LANES), f32)
    tiles = laid_out(rows, columns, same_core, rowed, placed.shape[0], lambda t: zero)
    for t, new in enumerate(tiles):
        placed[t] = new
    me = lax.axis_index("ia") >> 1
    mine = rowed[0]
    for r in range(1, rows // 2):
        mine = jnp.where(me == r, rowed[r], mine)
    o = old[...]
    factors = correction_factors(o[12:13])
    x1, v1 = correct(o[0:3], o[3:6], o[6:9], o[9:12], factors, mine[0:3], mine[3:6])
    targets_new[0:3, :] = x1
    targets_new[3:6, :] = v1
    targets_new[6:12, :] = mine[0:6]


def finish_kernel(
    rows, columns, other_core, placed, pos, vel, acc, jrk, levels, stars_out, stars_new, rowed, sems
):
    groups = levels.shape[0]
    piece = groups // PIECES
    copies = []
    factors = correction_factors(elapsed_of(levels[...]))
    tiles = laid_out(rows, columns, other_core, rowed, groups, lambda t: placed[t])
    for t, new in enumerate(tiles):
        there = jnp.broadcast_to(new[7:8], (3, LANES)) > 0.5
        x0, v0, a0, j0 = (pos[:, tile(t)], vel[:, tile(t)], acc[:, tile(t)], jrk[:, tile(t)])
        a1, j1 = (new[0:3], new[3:6])
        x1, v1 = correct(x0, v0, a0, j0, [f[t : t + 1] for f in factors], a1, j1)
        stars_new[0:3, tile(t)] = jnp.where(there, x1, x0)
        stars_new[3:6, tile(t)] = jnp.where(there, v1, v0)
        stars_new[6:9, tile(t)] = jnp.where(there, a1, a0)
        stars_new[9:12, tile(t)] = jnp.where(there, j1, j0)
        if (t + 1) % piece == 0:
            part_of = (slice(None), slice((t + 1 - piece) * LANES, (t + 1) * LANES))
            copies.append(
                pltpu.make_async_copy(
                    stars_new.at[part_of], stars_out.at[part_of], sems.at[len(copies)]
                )
            )
            copies[-1].start()
    for copy in copies:
        copy.wait()


def local(rows, columns, positions, velocities, accels, jerks, masses, levels, active):
    nlocal = positions.shape[1]
    ntarget = active.shape[0]
    groups = nlocal // LANES
    given = (
        positions,
        velocities,
        accels,
        jerks,
        levels.reshape(groups, LANES),
        masses.reshape(groups, LANES),
        active.reshape(1, ntarget),
    )
    mine, *kept = pl.pallas_call(
        gather_kernel,
        out_shape=(
            pltpu.VMEM((columns, 16, ntarget), f32),
            *(pltpu.VMEM(x.shape, x.dtype) for x in given),
        ),
        in_specs=[HBM] * 7,
        out_specs=(VMEM,) * 8,
        scratch_shapes=[pltpu.SemaphoreType.DMA((11,))],
        compiler_params=PARAMS,
        name="gather",
    )(*(pltpu.with_memory_space_constraint(x, pltpu.HBM) for x in given))
    gathered = lax.all_to_all(mine, "ja", 0, 0, axis_index_groups=[column_order(columns)])
    packed, old = pl.pallas_call(
        force_kernel,
        out_shape=(
            pltpu.VMEM((rows // 2 * columns, 1, NEW_ROWS * ntarget), f32),
            pltpu.VMEM((16, ntarget), f32),
        ),
        in_specs=[VMEM] * 8,
        out_specs=(VMEM, VMEM),
        scratch_shapes=[
            pltpu.VMEM((groups, 7, 8, LANES), f32),
            pltpu.VMEM((6, ntarget, LANES), f32),
            pltpu.VMEM((6, ntarget, LANES), f32),
        ],
        compiler_params=PARAMS,
        name="forces",
    )(gathered, *kept)
    order = pair_order(rows, columns)
    lists = [[(2 * h + core) * columns + c for h, c in order] for core in range(2)]
    same_core = lax.all_to_all(packed, ("ia", "ja"), 0, 0, axis_index_groups=lists)
    other_core = lax.ppermute(same_core, "ia", [(r, r ^ 1) for r in range(rows)])
    targets_new, placed = pl.pallas_call(
        functools.partial(same_kernel, rows, columns),
        out_shape=(
            jax.ShapeDtypeStruct((12, ntarget), f32),
            pltpu.VMEM((groups, 8, LANES), f32),
        ),
        in_specs=[VMEM] * 2,
        out_specs=(VMEM, VMEM),
        scratch_shapes=[pltpu.VMEM((rows // 2, 8, ntarget), f32)],
        compiler_params=PARAMS,
        cost_estimate=pl.CostEstimate(
            flops=200 * nlocal, bytes_accessed=4 * 64 * nlocal, transcendentals=0
        ),
        name="same",
    )(same_core, old)
    stars_new = pl.pallas_call(
        functools.partial(finish_kernel, rows, columns),
        out_shape=jax.ShapeDtypeStruct((12, nlocal), f32),
        in_specs=[VMEM] * 7,
        out_specs=HBM,
        scratch_shapes=[
            pltpu.VMEM((12, nlocal), f32),
            pltpu.VMEM((rows // 2, 8, ntarget), f32),
            pltpu.SemaphoreType.DMA((PIECES,)),
        ],
        compiler_params=PARAMS,
        name="finish",
    )(other_core, placed, *kept[:5])
    return (targets_new, stars_new)


def solution(mesh):
    rows, columns = mesh.shape["ia"], mesh.shape["ja"]

    def body(*args):
        return local(rows, columns, *args)

    return jax.shard_map(
        body,
        mesh=mesh,
        in_specs=(
            P(None, "ja"),
            P(None, "ja"),
            P(None, "ja"),
            P(None, "ja"),
            P("ja"),
            P("ja"),
            P("ia"),
        ),
        out_specs=(P(None, "ia"), P(None, "ja")),
        check_vma=False,
    )
```

```python
import functools

import jax
import jax.numpy as jnp
from jax import lax
from jax.experimental import pallas as pl
from jax.experimental.pallas import tpu as pltpu
from jax.sharding import PartitionSpec as P

softening_length = 0.01
base_step = 0.0625
LANES = 128
PIECES = 8
NEW_ROWS = 7
f32 = jnp.float32
VMEM = pl.BlockSpec(memory_space=pltpu.VMEM)
HBM = pl.BlockSpec(memory_space=pltpu.HBM)
PARAMS = pltpu.CompilerParams(vmem_limit_bytes=24 * 1024 * 1024)


def elapsed_of(levels):
    return (128 >> levels).astype(f32) * (base_step / 128.0)


def step_factors(elapsed):
    half = elapsed * elapsed * 0.5
    return (elapsed, half, half * elapsed * (1.0 / 3.0))


def predict(pos, vel, acc, jrk, factors):
    elapsed, half, sixth = factors
    pred_pos = pos + elapsed * vel + half * acc + sixth * jrk
    pred_vel = vel + elapsed * acc + half * jrk
    return (pred_pos, pred_vel)


def correction_factors(step):
    return (0.5 * step, step * step * (1.0 / 12.0))


def correct(x0, v0, a0, j0, factors, a1, j1):
    half, quad = factors
    v1 = v0 + half * (a0 + a1) + quad * (j0 - j1)
    x1 = x0 + half * (v0 + v1) + quad * (a0 - a1)
    return (x1, v1)


def column_order(columns):
    first = max(columns - 3, 0)
    return [*range(first, columns), *range(first)]


def pair_order(rows, columns):
    return [(h, c) for h in range(rows // 2 - 1, -1, -1) for c in range(columns - 1, -1, -1)]


def tile(t):
    return slice(t * LANES, (t + 1) * LANES)


def gather_kernel(*refs):
    given, out, kept, sems = (refs[:7], refs[7], refs[8:15], refs[15])
    pos, vel, acc, jrk, levels, masses, active = kept
    groups = levels.shape[0]
    half = groups // 2

    def copy_of(n, sem, columns=None):
        if columns is None:
            return pltpu.make_async_copy(given[n], kept[n], sems.at[sem])
        part = (slice(None), columns)
        return pltpu.make_async_copy(given[n].at[part], kept[n].at[part], sems.at[sem])

    small = [copy_of(6, 0), copy_of(4, 1)]
    parts = [
        [copy_of(n, 2 + 4 * h + n, slice(h * half * LANES, (h + 1) * half * LANES)) for n in range(4)]
        for h in range(2)
    ]
    late = copy_of(5, 10)
    for copy in (*small, *parts[0], *parts[1], late):
        copy.start()
    for copy in small:
        copy.wait()
    offset = active[...] - lax.axis_index("ja") * (groups * LANES)
    group = jnp.broadcast_to(offset >> 7, (8, LANES))
    lane = jnp.broadcast_to(offset & (LANES - 1), (8, LANES))
    row = lax.broadcasted_iota(jnp.int32, (8, LANES), 0)
    elapsed = elapsed_of(levels[...])
    steps = jnp.zeros((8, LANES), f32)
    for t in range(0, groups, 8):
        here = group == row + t
        steps = jnp.where(here, jnp.take_along_axis(elapsed[t : t + 8], lane, axis=1), steps)
    found = [jnp.zeros((3, LANES), f32)] * 4
    for h in range(2):
        for copy in parts[h]:
            copy.wait()
        for t in range(h * half, (h + 1) * half):
            here = group[0:3] == t
            found = [
                jnp.where(here, jnp.take_along_axis(x[:, tile(t)], lane[0:3], axis=1), old)
                for x, old in zip((pos, vel, acc, jrk), found)
            ]
    steps = jnp.broadcast_to(jnp.sum(steps, axis=0, keepdims=True), (4, LANES))
    for k in range(out.shape[0]):
        for n, value in enumerate(found):
            out[k, 3 * n : 3 * n + 3, :] = value
        out[k, 12:16, :] = steps
    late.wait()


def force_kernel(
    gathered, pos, vel, acc, jrk, levels, masses, active, packed, old, sources, targets, sums
):
    groups = levels.shape[0]
    ntarget = active.shape[1]
    state = gathered[0]
    for k in range(1, gathered.shape[0]):
        state = state + gathered[k]
    old[...] = state
    tpos, tvel = predict(
        state[0:3], state[3:6], state[6:9], state[9:12], step_factors(state[12:13])
    )
    columns = jnp.transpose(
        jnp.concatenate([tpos, tvel, jnp.zeros((LANES - 6, ntarget), f32)], axis=0)
    )
    for c in range(6):
        targets[c] = jnp.broadcast_to(columns[:, c : c + 1], (ntarget, LANES))
    factors = step_factors(elapsed_of(levels[...]))
    for t in range(groups):
        spos, svel = predict(
            *(x[:, tile(t)] for x in (pos, vel, acc, jrk)), [f[t : t + 1] for f in factors]
        )
        for c in range(3):
            sources[t, c] = jnp.broadcast_to(spos[c : c + 1], (8, LANES))
            sources[t, 3 + c] = jnp.broadcast_to(svel[c : c + 1], (8, LANES))
        sources[t, 6] = jnp.broadcast_to(masses[t : t + 1, :], (8, LANES))

    def one_group(g, unused):
        rows = pl.ds(pl.multiple_of(g * 8, 8), 8)
        tx, ty, tz, tu, tv, tw = (targets[c, rows, :] for c in range(6))

        def one_tile(t, carry):
            dx, dy, dz = (sources[t, 0] - tx, sources[t, 1] - ty, sources[t, 2] - tz)
            du, dv, dw = (sources[t, 3] - tu, sources[t, 4] - tv, sources[t, 5] - tw)
            r2 = dx * dx + dy * dy + dz * dz + softening_length
            inv = lax.rsqrt(r2)
            inv_sq = inv * inv
            weight = sources[t, 6] * inv * inv_sq
            radial = (dx * du + dy * dv + dz * dw) * inv_sq
            px, py, pz = (weight * dx, weight * dy, weight * dz)
            ax, ay, az, jx, jy, jz, kx, ky, kz = carry
            return (
                ax + px,
                ay + py,
                az + pz,
                jx + weight * du,
                jy + weight * dv,
                jz + weight * dw,
                kx + radial * px,
                ky + radial * py,
                kz + radial * pz,
            )

        zero = jnp.zeros((8, LANES), f32)
        ax, ay, az, jx, jy, jz, kx, ky, kz = lax.fori_loop(
            0, groups, one_tile, (zero,) * 9, unroll=32
        )
        for c, value in enumerate((ax, ay, az, jx - 3.0 * kx, jy - 3.0 * ky, jz - 3.0 * kz)):
            sums[c, rows, :] = value
        return unused

    lax.fori_loop(0, ntarget // 8, one_group, 0)
    lane = lax.broadcasted_iota(jnp.int32, (ntarget, LANES), 1)
    table = jnp.zeros((ntarget, LANES), f32)
    for c in range(6):
        table = jnp.where(lane == c, jnp.sum(sums[c], axis=1, keepdims=True), table)
    table = jnp.transpose(table)[0:8]
    row = lax.broadcasted_iota(jnp.int32, (8, ntarget), 0)
    table = jnp.where(row == 6, active[...].astype(f32), table)
    for k in range(packed.shape[0]):
        for c in range(NEW_ROWS):
            packed[k, :, tile(c)] = table[c : c + 1]


def laid_out(rows, columns, everyone, rowed, groups, before):
    ntarget = rowed.shape[2]
    base = lax.axis_index("ja") * (groups * LANES)
    order = pair_order(rows, columns)
    group = lax.broadcasted_iota(jnp.int32, (groups, ntarget), 0)
    lane = lax.broadcasted_iota(jnp.int32, (LANES, ntarget), 0)
    number = lax.broadcasted_iota(jnp.int32, (groups, ntarget), 1).astype(f32) + 1.0
    spot = jnp.zeros((groups, LANES), f32)
    part = jnp.full((groups, LANES), -1.0, f32)
    forces = []
    for r in range(rows // 2):
        first, *others = [k for k, (h, _) in enumerate(order) if h == r]
        total = everyone[first]
        for k in others:
            total = total + everyone[k]
        for c in range(6):
            rowed[r, c : c + 1, :] = total[:, tile(c)]
        rowed[r, 6:8, :] = jnp.ones((2, ntarget), f32)
        forces.append(rowed[r])
        offset = everyone[first][:, tile(6)].astype(jnp.int32) - base
        hit = group == offset >> 7
        side = (lane == (offset & (LANES - 1))).astype(jnp.bfloat16)
        found = lax.dot_general(
            jnp.where(hit, number, 0.0).astype(jnp.bfloat16),
            side,
            (((1,), (1,)), ((), ())),
            preferred_element_type=f32,
        )
        part = jnp.where(found > 0.5, float(r), part)
        spot = spot + found
    slot = jnp.maximum(spot - 1.0, 0.0).astype(jnp.int32)
    for t in range(groups):
        lanes = jnp.broadcast_to(slot[t : t + 1], (8, LANES))
        holder = jnp.broadcast_to(part[t : t + 1], (8, LANES))
        new = before(t)
        for r in range(rows // 2):
            new = jnp.where(holder == float(r), jnp.take_along_axis(forces[r], lanes, axis=1), new)
        yield new


def same_kernel(rows, columns, same_core, old, targets_new, placed, rowed):
    zero = jnp.zeros((8, LANES), f32)
    tiles = laid_out(rows, columns, same_core, rowed, placed.shape[0], lambda t: zero)
    for t, new in enumerate(tiles):
        placed[t] = new
    me = lax.axis_index("ia") >> 1
    mine = rowed[0]
    for r in range(1, rows // 2):
        mine = jnp.where(me == r, rowed[r], mine)
    o = old[...]
    factors = correction_factors(o[12:13])
    x1, v1 = correct(o[0:3], o[3:6], o[6:9], o[9:12], factors, mine[0:3], mine[3:6])
    targets_new[0:3, :] = x1
    targets_new[3:6, :] = v1
    targets_new[6:12, :] = mine[0:6]


def finish_kernel(
    rows, columns, other_core, placed, pos, vel, acc, jrk, levels, stars_out, stars_new, rowed, sems
):
    groups = levels.shape[0]
    piece = groups // PIECES
    copies = []
    factors = correction_factors(elapsed_of(levels[...]))
    tiles = laid_out(rows, columns, other_core, rowed, groups, lambda t: placed[t])
    for t, new in enumerate(tiles):
        there = jnp.broadcast_to(new[7:8], (3, LANES)) > 0.5
        x0, v0, a0, j0 = (pos[:, tile(t)], vel[:, tile(t)], acc[:, tile(t)], jrk[:, tile(t)])
        a1, j1 = (new[0:3], new[3:6])
        x1, v1 = correct(x0, v0, a0, j0, [f[t : t + 1] for f in factors], a1, j1)
        stars_new[0:3, tile(t)] = jnp.where(there, x1, x0)
        stars_new[3:6, tile(t)] = jnp.where(there, v1, v0)
        stars_new[6:9, tile(t)] = jnp.where(there, a1, a0)
        stars_new[9:12, tile(t)] = jnp.where(there, j1, j0)
        if (t + 1) % piece == 0:
            part_of = (slice(None), slice((t + 1 - piece) * LANES, (t + 1) * LANES))
            copies.append(
                pltpu.make_async_copy(
                    stars_new.at[part_of], stars_out.at[part_of], sems.at[len(copies)]
                )
            )
            copies[-1].start()
    for copy in copies:
        copy.wait()


def local(rows, columns, positions, velocities, accels, jerks, masses, levels, active):
    nlocal = positions.shape[1]
    ntarget = active.shape[0]
    groups = nlocal // LANES
    given = (
        positions,
        velocities,
        accels,
        jerks,
        levels.reshape(groups, LANES),
        masses.reshape(groups, LANES),
        active.reshape(1, ntarget),
    )
    mine, *kept = pl.pallas_call(
        gather_kernel,
        out_shape=(
            pltpu.VMEM((columns, 16, ntarget), f32),
            *(pltpu.VMEM(x.shape, x.dtype) for x in given),
        ),
        in_specs=[HBM] * 7,
        out_specs=(VMEM,) * 8,
        scratch_shapes=[pltpu.SemaphoreType.DMA((11,))],
        compiler_params=PARAMS,
        name="gather",
    )(*(pltpu.with_memory_space_constraint(x, pltpu.HBM) for x in given))
    gathered = lax.all_to_all(mine, "ja", 0, 0, axis_index_groups=[column_order(columns)])
    packed, old = pl.pallas_call(
        force_kernel,
        out_shape=(
            pltpu.VMEM((rows // 2 * columns, 1, NEW_ROWS * ntarget), f32),
            pltpu.VMEM((16, ntarget), f32),
        ),
        in_specs=[VMEM] * 8,
        out_specs=(VMEM, VMEM),
        scratch_shapes=[
            pltpu.VMEM((groups, 7, 8, LANES), f32),
            pltpu.VMEM((6, ntarget, LANES), f32),
            pltpu.VMEM((6, ntarget, LANES), f32),
        ],
        compiler_params=PARAMS,
        name="forces",
    )(gathered, *kept)
    order = pair_order(rows, columns)
    lists = [[(2 * h + core) * columns + c for h, c in order] for core in range(2)]
    same_core = lax.all_to_all(packed, ("ia", "ja"), 0, 0, axis_index_groups=lists)
    other_core = lax.ppermute(same_core, "ia", [(r, r ^ 1) for r in range(rows)])
    targets_new, placed = pl.pallas_call(
        functools.partial(same_kernel, rows, columns),
        out_shape=(
            jax.ShapeDtypeStruct((12, ntarget), f32),
            pltpu.VMEM((groups, 8, LANES), f32),
        ),
        in_specs=[VMEM] * 2,
        out_specs=(VMEM, VMEM),
        scratch_shapes=[pltpu.VMEM((rows // 2, 8, ntarget), f32)],
        compiler_params=PARAMS,
        cost_estimate=pl.CostEstimate(
            flops=200 * nlocal, bytes_accessed=4 * 64 * nlocal, transcendentals=0
        ),
        name="same",
    )(same_core, old)
    stars_new = pl.pallas_call(
        functools.partial(finish_kernel, rows, columns),
        out_shape=jax.ShapeDtypeStruct((12, nlocal), f32),
        in_specs=[VMEM] * 7,
        out_specs=HBM,
        scratch_shapes=[
            pltpu.VMEM((12, nlocal), f32),
            pltpu.VMEM((rows // 2, 8, ntarget), f32),
            pltpu.SemaphoreType.DMA((PIECES,)),
        ],
        compiler_params=PARAMS,
        name="finish",
    )(other_core, placed, *kept[:5])
    return (targets_new, stars_new)


def solution(mesh):
    rows, columns = mesh.shape["ia"], mesh.shape["ja"]

    def body(*args):
        return local(rows, columns, *args)

    return jax.shard_map(
        body,
        mesh=mesh,
        in_specs=(
            P(None, "ja"),
            P(None, "ja"),
            P(None, "ja"),
            P(None, "ja"),
            P("ja"),
            P("ja"),
            P("ia"),
        ),
        out_specs=(P(None, "ia"), P(None, "ja")),
        check_vma=False,
    )
```

```python
import functools

import jax
import jax.numpy as jnp
from jax import lax
from jax.experimental import pallas as pl
from jax.experimental.pallas import tpu as pltpu
from jax.sharding import PartitionSpec as P

softening_length = 0.01
base_step = 0.0625
LANES = 128
PIECES = 8
NEW_ROWS = 7
f32 = jnp.float32
VMEM = pl.BlockSpec(memory_space=pltpu.VMEM)
HBM = pl.BlockSpec(memory_space=pltpu.HBM)
PARAMS = pltpu.CompilerParams(vmem_limit_bytes=24 * 1024 * 1024)


def elapsed_of(levels):
    return (128 >> levels).astype(f32) * (base_step / 128.0)


def step_factors(elapsed):
    half = elapsed * elapsed * 0.5
    return (elapsed, half, half * elapsed * (1.0 / 3.0))


def predict(pos, vel, acc, jrk, factors):
    elapsed, half, sixth = factors
    pred_pos = pos + elapsed * vel + half * acc + sixth * jrk
    pred_vel = vel + elapsed * acc + half * jrk
    return (pred_pos, pred_vel)


def correction_factors(step):
    return (0.5 * step, step * step * (1.0 / 12.0))


def correct(x0, v0, a0, j0, factors, a1, j1):
    half, quad = factors
    v1 = v0 + half * (a0 + a1) + quad * (j0 - j1)
    x1 = x0 + half * (v0 + v1) + quad * (a0 - a1)
    return (x1, v1)


def column_order(columns):
    first = max(columns - 3, 0)
    return [*range(first, columns), *range(first)]


def pair_order(rows, columns):
    return [(h, c) for h in range(rows // 2 - 1, -1, -1) for c in range(columns - 1, -1, -1)]


def tile(t):
    return slice(t * LANES, (t + 1) * LANES)


def gather_kernel(*refs):
    given, out, kept, sems = (refs[:7], refs[7], refs[8:15], refs[15])
    levels, masses, active = kept[4:]
    groups = levels.shape[0]
    small = [pltpu.make_async_copy(given[n], kept[n], sems.at[n]) for n in (6, 4)]
    planes = [
        [
            pltpu.make_async_copy(given[n].at[:, c, :], kept[n].at[c], sems.at[7 + 3 * n + c])
            for c in range(3)
        ]
        for n in range(4)
    ]
    late = pltpu.make_async_copy(given[5], kept[5], sems.at[5])
    for copy in (*small, *sum(planes, []), late):
        copy.start()
    for copy in small:
        copy.wait()
    offset = active[...] - lax.axis_index("ja") * (groups * LANES)
    group = jnp.broadcast_to(offset >> 7, (8, LANES))
    lane = jnp.broadcast_to(offset & (LANES - 1), (8, LANES))
    row = lax.broadcasted_iota(jnp.int32, (8, LANES), 0)
    here = [group == row + t for t in range(0, groups, 8)]

    def picked(plane):
        value = jnp.zeros((8, LANES), f32)
        for n, mask in enumerate(here):
            part = jnp.take_along_axis(plane[8 * n : 8 * n + 8], lane, axis=1)
            value = jnp.where(mask, part, value)
        return jnp.sum(value, axis=0, keepdims=True)

    found = [picked(elapsed_of(levels[...]))]
    for n in range(4):
        for c in range(3):
            planes[n][c].wait()
            found.insert(3 * n + c, picked(kept[n].at[c]))
    for k in range(out.shape[0]):
        for n, value in enumerate(found):
            out[k, n : n + 1, :] = value
        out[k, 13:16, :] = jnp.zeros((3, LANES), f32)
    late.wait()


def force_kernel(
    gathered, pos, vel, acc, jrk, levels, masses, active, packed, old, sources, targets, sums
):
    groups = levels.shape[0]
    ntarget = active.shape[1]
    state = gathered[0]
    for k in range(1, gathered.shape[0]):
        state = state + gathered[k]
    old[...] = state
    tpos, tvel = predict(
        state[0:3], state[3:6], state[6:9], state[9:12], step_factors(state[12:13])
    )
    columns = jnp.transpose(
        jnp.concatenate([tpos, tvel, jnp.zeros((LANES - 6, ntarget), f32)], axis=0)
    )
    for c in range(6):
        targets[c] = jnp.broadcast_to(columns[:, c : c + 1], (ntarget, LANES))
    factors = step_factors(elapsed_of(levels[...]))
    for c in range(3):
        spos, svel = predict(pos[c], vel[c], acc[c], jrk[c], factors)
        for t in range(groups):
            sources[t, c] = jnp.broadcast_to(spos[t : t + 1], (8, LANES))
            sources[t, 3 + c] = jnp.broadcast_to(svel[t : t + 1], (8, LANES))
    for t in range(groups):
        sources[t, 6] = jnp.broadcast_to(masses[t : t + 1, :], (8, LANES))

    def one_group(g, unused):
        rows = pl.ds(pl.multiple_of(g * 8, 8), 8)
        tx, ty, tz, tu, tv, tw = (targets[c, rows, :] for c in range(6))

        def one_tile(t, carry):
            dx, dy, dz = (sources[t, 0] - tx, sources[t, 1] - ty, sources[t, 2] - tz)
            du, dv, dw = (sources[t, 3] - tu, sources[t, 4] - tv, sources[t, 5] - tw)
            r2 = dx * dx + dy * dy + dz * dz + softening_length
            inv = lax.rsqrt(r2)
            inv_sq = inv * inv
            weight = sources[t, 6] * inv * inv_sq
            radial = (dx * du + dy * dv + dz * dw) * inv_sq
            px, py, pz = (weight * dx, weight * dy, weight * dz)
            ax, ay, az, jx, jy, jz, kx, ky, kz = carry
            return (
                ax + px,
                ay + py,
                az + pz,
                jx + weight * du,
                jy + weight * dv,
                jz + weight * dw,
                kx + radial * px,
                ky + radial * py,
                kz + radial * pz,
            )

        zero = jnp.zeros((8, LANES), f32)
        ax, ay, az, jx, jy, jz, kx, ky, kz = lax.fori_loop(
            0, groups, one_tile, (zero,) * 9, unroll=32
        )
        for c, value in enumerate((ax, ay, az, jx - 3.0 * kx, jy - 3.0 * ky, jz - 3.0 * kz)):
            sums[c, rows, :] = value
        return unused

    lax.fori_loop(0, ntarget // 8, one_group, 0)
    lane = lax.broadcasted_iota(jnp.int32, (ntarget, LANES), 1)
    table = jnp.zeros((ntarget, LANES), f32)
    for c in range(6):
        table = jnp.where(lane == c, jnp.sum(sums[c], axis=1, keepdims=True), table)
    table = jnp.transpose(table)[0:8]
    row = lax.broadcasted_iota(jnp.int32, (8, ntarget), 0)
    table = jnp.where(row == 6, active[...].astype(f32), table)
    for k in range(packed.shape[0]):
        for c in range(NEW_ROWS):
            packed[k, :, tile(c)] = table[c : c + 1]


def laid_out(rows, columns, everyone, rowed, groups, before):
    ntarget = rowed.shape[2]
    base = lax.axis_index("ja") * (groups * LANES)
    order = pair_order(rows, columns)
    group = lax.broadcasted_iota(jnp.int32, (groups, ntarget), 0)
    lane = lax.broadcasted_iota(jnp.int32, (LANES, ntarget), 0)
    number = lax.broadcasted_iota(jnp.int32, (groups, ntarget), 1).astype(f32) + 1.0
    spot = jnp.zeros((groups, LANES), f32)
    part = jnp.full((groups, LANES), -1.0, f32)
    forces = []
    for r in range(rows // 2):
        first, *others = [k for k, (h, _) in enumerate(order) if h == r]
        total = everyone[first]
        for k in others:
            total = total + everyone[k]
        for c in range(6):
            rowed[r, c : c + 1, :] = total[:, tile(c)]
        rowed[r, 6:8, :] = jnp.ones((2, ntarget), f32)
        forces.append(rowed[r])
        offset = everyone[first][:, tile(6)].astype(jnp.int32) - base
        hit = group == offset >> 7
        side = (lane == (offset & (LANES - 1))).astype(jnp.bfloat16)
        found = lax.dot_general(
            jnp.where(hit, number, 0.0).astype(jnp.bfloat16),
            side,
            (((1,), (1,)), ((), ())),
            preferred_element_type=f32,
        )
        part = jnp.where(found > 0.5, float(r), part)
        spot = spot + found
    slot = jnp.maximum(spot - 1.0, 0.0).astype(jnp.int32)
    for t in range(groups):
        lanes = jnp.broadcast_to(slot[t : t + 1], (8, LANES))
        holder = jnp.broadcast_to(part[t : t + 1], (8, LANES))
        new = before(t)
        for r in range(rows // 2):
            new = jnp.where(holder == float(r), jnp.take_along_axis(forces[r], lanes, axis=1), new)
        yield new


def same_kernel(rows, columns, same_core, old, *refs):
    given, targets_new, placed, kept, rowed, sems = (refs[:4], *refs[4:6], refs[6:10], *refs[10:])
    copies = [pltpu.make_async_copy(a, b, sems.at[n]) for n, (a, b) in enumerate(zip(given, kept))]
    for copy in copies:
        copy.start()
    zero = jnp.zeros((8, LANES), f32)
    tiles = laid_out(rows, columns, same_core, rowed, placed.shape[0], lambda t: zero)
    for t, new in enumerate(tiles):
        placed[t] = new
    me = lax.axis_index("ia") >> 1
    mine = rowed[0]
    for r in range(1, rows // 2):
        mine = jnp.where(me == r, rowed[r], mine)
    o = old[...]
    factors = correction_factors(o[12:13])
    x1, v1 = correct(o[0:3], o[3:6], o[6:9], o[9:12], factors, mine[0:3], mine[3:6])
    targets_new[0:3, :] = x1
    targets_new[3:6, :] = v1
    targets_new[6:12, :] = mine[0:6]
    for copy in copies:
        copy.wait()


def finish_kernel(
    rows, columns, other_core, placed, pos, vel, acc, jrk, levels, stars_out, stars_new, rowed, sems
):
    groups = levels.shape[0]
    piece = groups // PIECES
    copies = []
    factors = correction_factors(elapsed_of(levels[...]))
    tiles = laid_out(rows, columns, other_core, rowed, groups, lambda t: placed[t])
    for t, new in enumerate(tiles):
        there = jnp.broadcast_to(new[7:8], (3, LANES)) > 0.5
        x0, v0, a0, j0 = (pos[:, tile(t)], vel[:, tile(t)], acc[:, tile(t)], jrk[:, tile(t)])
        a1, j1 = (new[0:3], new[3:6])
        x1, v1 = correct(x0, v0, a0, j0, [f[t : t + 1] for f in factors], a1, j1)
        stars_new[0:3, tile(t)] = jnp.where(there, x1, x0)
        stars_new[3:6, tile(t)] = jnp.where(there, v1, v0)
        stars_new[6:9, tile(t)] = jnp.where(there, a1, a0)
        stars_new[9:12, tile(t)] = jnp.where(there, j1, j0)
        if (t + 1) % piece == 0:
            part_of = (slice(None), slice((t + 1 - piece) * LANES, (t + 1) * LANES))
            copies.append(
                pltpu.make_async_copy(
                    stars_new.at[part_of], stars_out.at[part_of], sems.at[len(copies)]
                )
            )
            copies[-1].start()
    for copy in copies:
        copy.wait()


def local(rows, columns, positions, velocities, accels, jerks, masses, levels, active):
    nlocal = positions.shape[1]
    ntarget = active.shape[0]
    groups = nlocal // LANES
    state = (positions, velocities, accels, jerks)
    given = (
        *(jnp.swapaxes(x.reshape(3, groups, LANES), 0, 1) for x in state),
        levels.reshape(groups, LANES),
        masses.reshape(groups, LANES),
        active.reshape(1, ntarget),
    )
    mine, *kept = pl.pallas_call(
        gather_kernel,
        out_shape=(
            pltpu.VMEM((columns, 16, ntarget), f32),
            *(pltpu.VMEM((3, groups, LANES), f32) for _ in state),
            *(pltpu.VMEM(x.shape, x.dtype) for x in given[4:]),
        ),
        in_specs=[HBM] * 7,
        out_specs=(VMEM,) * 8,
        scratch_shapes=[pltpu.SemaphoreType.DMA((19,))],
        compiler_params=PARAMS,
        name="gather",
    )(*(pltpu.with_memory_space_constraint(x, pltpu.HBM) for x in given))
    gathered = lax.all_to_all(mine, "ja", 0, 0, axis_index_groups=[column_order(columns)])
    packed, old = pl.pallas_call(
        force_kernel,
        out_shape=(
            pltpu.VMEM((rows // 2 * columns, 1, NEW_ROWS * ntarget), f32),
            pltpu.VMEM((16, ntarget), f32),
        ),
        in_specs=[VMEM] * 8,
        out_specs=(VMEM, VMEM),
        scratch_shapes=[
            pltpu.VMEM((groups, 7, 8, LANES), f32),
            pltpu.VMEM((6, ntarget, LANES), f32),
            pltpu.VMEM((6, ntarget, LANES), f32),
        ],
        compiler_params=PARAMS,
        name="forces",
    )(gathered, *kept)
    order = pair_order(rows, columns)
    lists = [[(2 * h + core) * columns + c for h, c in order] for core in range(2)]
    same_core = lax.all_to_all(packed, ("ia", "ja"), 0, 0, axis_index_groups=lists)
    other_core = lax.ppermute(same_core, "ia", [(r, r ^ 1) for r in range(rows)])
    targets_new, placed, *tiles = pl.pallas_call(
        functools.partial(same_kernel, rows, columns),
        out_shape=(
            jax.ShapeDtypeStruct((12, ntarget), f32),
            pltpu.VMEM((groups, 8, LANES), f32),
            *(pltpu.VMEM(x.shape, f32) for x in state),
        ),
        in_specs=[VMEM] * 2 + [HBM] * 4,
        out_specs=(VMEM,) * 6,
        scratch_shapes=[
            pltpu.VMEM((rows // 2, 8, ntarget), f32),
            pltpu.SemaphoreType.DMA((4,)),
        ],
        compiler_params=PARAMS,
        cost_estimate=pl.CostEstimate(
            flops=200 * nlocal, bytes_accessed=4 * 64 * nlocal, transcendentals=0
        ),
        name="same",
    )(same_core, old, *(pltpu.with_memory_space_constraint(x, pltpu.HBM) for x in state))
    stars_new = pl.pallas_call(
        functools.partial(finish_kernel, rows, columns),
        out_shape=jax.ShapeDtypeStruct((12, nlocal), f32),
        in_specs=[VMEM] * 7,
        out_specs=HBM,
        scratch_shapes=[
            pltpu.VMEM((12, nlocal), f32),
            pltpu.VMEM((rows // 2, 8, ntarget), f32),
            pltpu.SemaphoreType.DMA((PIECES,)),
        ],
        compiler_params=PARAMS,
        name="finish",
    )(other_core, placed, *tiles, kept[4])
    return (targets_new, stars_new)


def solution(mesh):
    rows, columns = mesh.shape["ia"], mesh.shape["ja"]

    def body(*args):
        return local(rows, columns, *args)

    return jax.shard_map(
        body,
        mesh=mesh,
        in_specs=(
            P(None, "ja"),
            P(None, "ja"),
            P(None, "ja"),
            P(None, "ja"),
            P("ja"),
            P("ja"),
            P("ia"),
        ),
        out_specs=(P(None, "ia"), P(None, "ja")),
        check_vma=False,
    )
```

```python
import functools

import jax
import jax.numpy as jnp
from jax import lax
from jax.experimental import pallas as pl
from jax.experimental.pallas import tpu as pltpu
from jax.sharding import PartitionSpec as P

softening_length = 0.01
base_step = 0.0625
LANES = 128
PIECES = 8
NEW_ROWS = 7
f32 = jnp.float32
VMEM = pl.BlockSpec(memory_space=pltpu.VMEM)
HBM = pl.BlockSpec(memory_space=pltpu.HBM)
PARAMS = pltpu.CompilerParams(vmem_limit_bytes=24 * 1024 * 1024)


def elapsed_of(levels):
    return (128 >> levels).astype(f32) * (base_step / 128.0)


def step_factors(elapsed):
    half = elapsed * elapsed * 0.5
    return (elapsed, half, half * elapsed * (1.0 / 3.0))


def predict(pos, vel, acc, jrk, factors):
    elapsed, half, sixth = factors
    pred_pos = pos + elapsed * vel + half * acc + sixth * jrk
    pred_vel = vel + elapsed * acc + half * jrk
    return (pred_pos, pred_vel)


def correction_factors(step):
    return (0.5 * step, step * step * (1.0 / 12.0))


def correct(x0, v0, a0, j0, factors, a1, j1):
    half, quad = factors
    v1 = v0 + half * (a0 + a1) + quad * (j0 - j1)
    x1 = x0 + half * (v0 + v1) + quad * (a0 - a1)
    return (x1, v1)


def column_order(columns):
    first = max(columns - 3, 0)
    return [*range(first, columns), *range(first)]


def pair_order(rows, columns):
    return [(h, c) for h in range(rows // 2 - 1, -1, -1) for c in range(columns - 1, -1, -1)]


def tile(t):
    return slice(t * LANES, (t + 1) * LANES)


def gather_kernel(*refs):
    given, out, kept, sems = (refs[:7], refs[7], refs[8:15], refs[15])
    pos, vel, acc, jrk, levels, masses, active = kept
    groups = levels.shape[0]
    half = groups // 2

    def copy_of(n, sem, columns=None):
        if columns is None:
            return pltpu.make_async_copy(given[n], kept[n], sems.at[sem])
        part = (slice(None), columns)
        return pltpu.make_async_copy(given[n].at[part], kept[n].at[part], sems.at[sem])

    small = [copy_of(6, 0), copy_of(4, 1)]
    parts = [
        [copy_of(n, 2 + 4 * h + n, slice(h * half * LANES, (h + 1) * half * LANES)) for n in range(4)]
        for h in range(2)
    ]
    late = copy_of(5, 10)
    for copy in (*small, *parts[0], *parts[1], late):
        copy.start()
    for copy in small:
        copy.wait()
    offset = active[...] - lax.axis_index("ja") * (groups * LANES)
    group = jnp.broadcast_to(offset >> 7, (8, LANES))
    lane = jnp.broadcast_to(offset & (LANES - 1), (8, LANES))
    row = lax.broadcasted_iota(jnp.int32, (8, LANES), 0)
    elapsed = elapsed_of(levels[...])
    steps = jnp.zeros((8, LANES), f32)
    for t in range(0, groups, 8):
        here = group == row + t
        steps = jnp.where(here, jnp.take_along_axis(elapsed[t : t + 8], lane, axis=1), steps)
    found = [jnp.zeros((3, LANES), f32)] * 4
    for h in range(2):
        for copy in parts[h]:
            copy.wait()
        for t in range(h * half, (h + 1) * half):
            here = group[0:3] == t
            found = [
                jnp.where(here, jnp.take_along_axis(x[:, tile(t)], lane[0:3], axis=1), old)
                for x, old in zip((pos, vel, acc, jrk), found)
            ]
    steps = jnp.broadcast_to(jnp.sum(steps, axis=0, keepdims=True), (4, LANES))
    for k in range(out.shape[0]):
        for n, value in enumerate(found):
            out[k, 3 * n : 3 * n + 3, :] = value
        out[k, 12:16, :] = steps
    late.wait()


def force_kernel(
    gathered, pos, vel, acc, jrk, levels, masses, active, packed, old, sources, targets, sums
):
    groups = levels.shape[0]
    ntarget = active.shape[1]
    state = gathered[0]
    for k in range(1, gathered.shape[0]):
        state = state + gathered[k]
    old[...] = state
    tpos, tvel = predict(
        state[0:3], state[3:6], state[6:9], state[9:12], step_factors(state[12:13])
    )
    columns = jnp.transpose(
        jnp.concatenate([tpos, tvel, jnp.zeros((LANES - 6, ntarget), f32)], axis=0)
    )
    for c in range(6):
        targets[c] = jnp.broadcast_to(columns[:, c : c + 1], (ntarget, LANES))
    factors = step_factors(elapsed_of(levels[...]))
    for t in range(groups):
        spos, svel = predict(
            *(x[:, tile(t)] for x in (pos, vel, acc, jrk)), [f[t : t + 1] for f in factors]
        )
        for c in range(3):
            sources[t, c] = jnp.broadcast_to(spos[c : c + 1], (8, LANES))
            sources[t, 3 + c] = jnp.broadcast_to(svel[c : c + 1], (8, LANES))
        sources[t, 6] = jnp.broadcast_to(masses[t : t + 1, :], (8, LANES))

    def one_group(g, unused):
        rows = pl.ds(pl.multiple_of(g * 8, 8), 8)
        tx, ty, tz, tu, tv, tw = (targets[c, rows, :] for c in range(6))

        def one_tile(t, carry):
            dx, dy, dz = (sources[t, 0] - tx, sources[t, 1] - ty, sources[t, 2] - tz)
            inv = lax.rsqrt(dx * dx + dy * dy + (dz * dz + softening_length))
            du, dv, dw = (sources[t, 3] - tu, sources[t, 4] - tv, sources[t, 5] - tw)
            dot = dx * du + dy * dv + dz * dw
            inv_sq = inv * inv
            weight = (sources[t, 6] * inv) * inv_sq
            radial = dot * inv_sq
            px, py, pz = (weight * dx, weight * dy, weight * dz)
            ax, ay, az, jx, jy, jz, kx, ky, kz = carry
            return (
                ax + px,
                ay + py,
                az + pz,
                jx + weight * du,
                jy + weight * dv,
                jz + weight * dw,
                kx + radial * px,
                ky + radial * py,
                kz + radial * pz,
            )

        zero = jnp.zeros((8, LANES), f32)
        ax, ay, az, jx, jy, jz, kx, ky, kz = lax.fori_loop(
            0, groups, one_tile, (zero,) * 9, unroll=16
        )
        for c, value in enumerate((ax, ay, az, jx - 3.0 * kx, jy - 3.0 * ky, jz - 3.0 * kz)):
            sums[c, rows, :] = value
        return unused

    lax.fori_loop(0, ntarget // 8, one_group, 0)
    lane = lax.broadcasted_iota(jnp.int32, (ntarget, LANES), 1)
    table = jnp.zeros((ntarget, LANES), f32)
    for c in range(6):
        table = jnp.where(lane == c, jnp.sum(sums[c], axis=1, keepdims=True), table)
    table = jnp.transpose(table)[0:8]
    row = lax.broadcasted_iota(jnp.int32, (8, ntarget), 0)
    table = jnp.where(row == 6, active[...].astype(f32), table)
    for k in range(packed.shape[0]):
        for c in range(NEW_ROWS):
            packed[k, :, tile(c)] = table[c : c + 1]


def laid_out(rows, columns, everyone, rowed, groups, before):
    ntarget = rowed.shape[2]
    base = lax.axis_index("ja") * (groups * LANES)
    order = pair_order(rows, columns)
    group = lax.broadcasted_iota(jnp.int32, (groups, ntarget), 0)
    lane = lax.broadcasted_iota(jnp.int32, (LANES, ntarget), 0)
    number = lax.broadcasted_iota(jnp.int32, (groups, ntarget), 1).astype(f32) + 1.0
    spot = jnp.zeros((groups, LANES), f32)
    part = jnp.full((groups, LANES), -1.0, f32)
    forces = []
    for r in range(rows // 2):
        first, *others = [k for k, (h, _) in enumerate(order) if h == r]
        total = everyone[first]
        for k in others:
            total = total + everyone[k]
        for c in range(6):
            rowed[r, c : c + 1, :] = total[:, tile(c)]
        rowed[r, 6:8, :] = jnp.ones((2, ntarget), f32)
        forces.append(rowed[r])
        offset = everyone[first][:, tile(6)].astype(jnp.int32) - base
        hit = group == offset >> 7
        side = (lane == (offset & (LANES - 1))).astype(jnp.bfloat16)
        found = lax.dot_general(
            jnp.where(hit, number, 0.0).astype(jnp.bfloat16),
            side,
            (((1,), (1,)), ((), ())),
            preferred_element_type=f32,
        )
        part = jnp.where(found > 0.5, float(r), part)
        spot = spot + found
    slot = jnp.maximum(spot - 1.0, 0.0).astype(jnp.int32)
    for t in range(groups):
        lanes = jnp.broadcast_to(slot[t : t + 1], (8, LANES))
        holder = jnp.broadcast_to(part[t : t + 1], (8, LANES))
        new = before(t)
        for r in range(rows // 2):
            new = jnp.where(holder == float(r), jnp.take_along_axis(forces[r], lanes, axis=1), new)
        yield new


def same_kernel(rows, columns, same_core, old, targets_new, placed, rowed):
    zero = jnp.zeros((8, LANES), f32)
    tiles = laid_out(rows, columns, same_core, rowed, placed.shape[0], lambda t: zero)
    for t, new in enumerate(tiles):
        placed[t] = new
    me = lax.axis_index("ia") >> 1
    mine = rowed[0]
    for r in range(1, rows // 2):
        mine = jnp.where(me == r, rowed[r], mine)
    o = old[...]
    factors = correction_factors(o[12:13])
    x1, v1 = correct(o[0:3], o[3:6], o[6:9], o[9:12], factors, mine[0:3], mine[3:6])
    targets_new[0:3, :] = x1
    targets_new[3:6, :] = v1
    targets_new[6:12, :] = mine[0:6]


def finish_kernel(
    rows, columns, other_core, placed, pos, vel, acc, jrk, levels, stars_out, stars_new, rowed, sems
):
    groups = levels.shape[0]
    piece = groups // PIECES
    copies = []
    factors = correction_factors(elapsed_of(levels[...]))
    tiles = laid_out(rows, columns, other_core, rowed, groups, lambda t: placed[t])
    for t, new in enumerate(tiles):
        there = jnp.broadcast_to(new[7:8], (3, LANES)) > 0.5
        x0, v0, a0, j0 = (pos[:, tile(t)], vel[:, tile(t)], acc[:, tile(t)], jrk[:, tile(t)])
        a1, j1 = (new[0:3], new[3:6])
        x1, v1 = correct(x0, v0, a0, j0, [f[t : t + 1] for f in factors], a1, j1)
        stars_new[0:3, tile(t)] = jnp.where(there, x1, x0)
        stars_new[3:6, tile(t)] = jnp.where(there, v1, v0)
        stars_new[6:9, tile(t)] = jnp.where(there, a1, a0)
        stars_new[9:12, tile(t)] = jnp.where(there, j1, j0)
        if (t + 1) % piece == 0:
            part_of = (slice(None), slice((t + 1 - piece) * LANES, (t + 1) * LANES))
            copies.append(
                pltpu.make_async_copy(
                    stars_new.at[part_of], stars_out.at[part_of], sems.at[len(copies)]
                )
            )
            copies[-1].start()
    for copy in copies:
        copy.wait()


def local(rows, columns, positions, velocities, accels, jerks, masses, levels, active):
    nlocal = positions.shape[1]
    ntarget = active.shape[0]
    groups = nlocal // LANES
    given = (
        positions,
        velocities,
        accels,
        jerks,
        levels.reshape(groups, LANES),
        masses.reshape(groups, LANES),
        active.reshape(1, ntarget),
    )
    mine, *kept = pl.pallas_call(
        gather_kernel,
        out_shape=(
            pltpu.VMEM((columns, 16, ntarget), f32),
            *(pltpu.VMEM(x.shape, x.dtype) for x in given),
        ),
        in_specs=[HBM] * 7,
        out_specs=(VMEM,) * 8,
        scratch_shapes=[pltpu.SemaphoreType.DMA((11,))],
        compiler_params=PARAMS,
        name="gather",
    )(*(pltpu.with_memory_space_constraint(x, pltpu.HBM) for x in given))
    gathered = lax.all_to_all(mine, "ja", 0, 0, axis_index_groups=[column_order(columns)])
    packed, old = pl.pallas_call(
        force_kernel,
        out_shape=(
            pltpu.VMEM((rows // 2 * columns, 1, NEW_ROWS * ntarget), f32),
            pltpu.VMEM((16, ntarget), f32),
        ),
        in_specs=[VMEM] * 8,
        out_specs=(VMEM, VMEM),
        scratch_shapes=[
            pltpu.VMEM((groups, 7, 8, LANES), f32),
            pltpu.VMEM((6, ntarget, LANES), f32),
            pltpu.VMEM((6, ntarget, LANES), f32),
        ],
        compiler_params=PARAMS,
        name="forces",
    )(gathered, *kept)
    order = pair_order(rows, columns)
    lists = [[(2 * h + core) * columns + c for h, c in order] for core in range(2)]
    same_core = lax.all_to_all(packed, ("ia", "ja"), 0, 0, axis_index_groups=lists)
    other_core = lax.ppermute(same_core, "ia", [(r, r ^ 1) for r in range(rows)])
    targets_new, placed = pl.pallas_call(
        functools.partial(same_kernel, rows, columns),
        out_shape=(
            jax.ShapeDtypeStruct((12, ntarget), f32),
            pltpu.VMEM((groups, 8, LANES), f32),
        ),
        in_specs=[VMEM] * 2,
        out_specs=(VMEM, VMEM),
        scratch_shapes=[pltpu.VMEM((rows // 2, 8, ntarget), f32)],
        compiler_params=PARAMS,
        cost_estimate=pl.CostEstimate(
            flops=200 * nlocal, bytes_accessed=4 * 64 * nlocal, transcendentals=0
        ),
        name="same",
    )(same_core, old)
    stars_new = pl.pallas_call(
        functools.partial(finish_kernel, rows, columns),
        out_shape=jax.ShapeDtypeStruct((12, nlocal), f32),
        in_specs=[VMEM] * 7,
        out_specs=HBM,
        scratch_shapes=[
            pltpu.VMEM((12, nlocal), f32),
            pltpu.VMEM((rows // 2, 8, ntarget), f32),
            pltpu.SemaphoreType.DMA((PIECES,)),
        ],
        compiler_params=PARAMS,
        name="finish",
    )(other_core, placed, *kept[:5])
    return (targets_new, stars_new)


def solution(mesh):
    rows, columns = mesh.shape["ia"], mesh.shape["ja"]

    def body(*args):
        return local(rows, columns, *args)

    return jax.shard_map(
        body,
        mesh=mesh,
        in_specs=(
            P(None, "ja"),
            P(None, "ja"),
            P(None, "ja"),
            P(None, "ja"),
            P("ja"),
            P("ja"),
            P("ia"),
        ),
        out_specs=(P(None, "ia"), P(None, "ja")),
        check_vma=False,
    )
```

```python
import functools

import jax
import jax.numpy as jnp
from jax import lax
from jax.experimental import pallas as pl
from jax.experimental.pallas import tpu as pltpu
from jax.sharding import PartitionSpec as P

softening_length = 0.01
base_step = 0.0625
LANES = 128
PIECES = 8
NEW_ROWS = 7
f32 = jnp.float32
VMEM = pl.BlockSpec(memory_space=pltpu.VMEM)
HBM = pl.BlockSpec(memory_space=pltpu.HBM)
PARAMS = pltpu.CompilerParams(vmem_limit_bytes=24 * 1024 * 1024)


def elapsed_of(levels):
    return (128 >> levels).astype(f32) * (base_step / 128.0)


def step_factors(elapsed):
    half = elapsed * elapsed * 0.5
    return (elapsed, half, half * elapsed * (1.0 / 3.0))


def predict(pos, vel, acc, jrk, factors):
    elapsed, half, sixth = factors
    pred_pos = pos + elapsed * vel + half * acc + sixth * jrk
    pred_vel = vel + elapsed * acc + half * jrk
    return (pred_pos, pred_vel)


def correction_factors(step):
    return (0.5 * step, step * step * (1.0 / 12.0))


def correct(x0, v0, a0, j0, factors, a1, j1):
    half, quad = factors
    v1 = v0 + half * (a0 + a1) + quad * (j0 - j1)
    x1 = x0 + half * (v0 + v1) + quad * (a0 - a1)
    return (x1, v1)


def column_order(columns):
    first = max(columns - 3, 0)
    return [*range(first, columns), *range(first)]


def pair_order(rows, columns):
    return [(h, c) for h in range(rows // 2 - 1, -1, -1) for c in range(columns - 1, -1, -1)]


def tile(t):
    return slice(t * LANES, (t + 1) * LANES)


def gather_kernel(*refs):
    given, out, kept, sems = (refs[:7], refs[7], refs[8:15], refs[15])
    pos, vel, acc, jrk, levels, masses, active = kept
    groups = levels.shape[0]
    half = groups // 2

    def copy_of(n, sem, columns=None):
        if columns is None:
            return pltpu.make_async_copy(given[n], kept[n], sems.at[sem])
        part = (slice(None), columns)
        return pltpu.make_async_copy(given[n].at[part], kept[n].at[part], sems.at[sem])

    small = [copy_of(6, 0), copy_of(4, 1)]
    parts = [
        [copy_of(n, 2 + 4 * h + n, slice(h * half * LANES, (h + 1) * half * LANES)) for n in range(4)]
        for h in range(2)
    ]
    late = copy_of(5, 10)
    for copy in (*small, *parts[0], *parts[1], late):
        copy.start()
    for copy in small:
        copy.wait()
    offset = active[...] - lax.axis_index("ja") * (groups * LANES)
    group = jnp.broadcast_to(offset >> 7, (8, LANES))
    lane = jnp.broadcast_to(offset & (LANES - 1), (8, LANES))
    row = lax.broadcasted_iota(jnp.int32, (8, LANES), 0)
    elapsed = elapsed_of(levels[...])
    steps = jnp.zeros((8, LANES), f32)
    for t in range(0, groups, 8):
        here = group == row + t
        steps = jnp.where(here, jnp.take_along_axis(elapsed[t : t + 8], lane, axis=1), steps)
    found = [jnp.zeros((3, LANES), f32)] * 4
    for h in range(2):
        for copy in parts[h]:
            copy.wait()
        for t in range(h * half, (h + 1) * half):
            here = group[0:3] == t
            found = [
                jnp.where(here, jnp.take_along_axis(x[:, tile(t)], lane[0:3], axis=1), old)
                for x, old in zip((pos, vel, acc, jrk), found)
            ]
    steps = jnp.broadcast_to(jnp.sum(steps, axis=0, keepdims=True), (4, LANES))
    for k in range(out.shape[0]):
        for n, value in enumerate(found):
            out[k, 3 * n : 3 * n + 3, :] = value
        out[k, 12:16, :] = steps
    late.wait()


def force_kernel(
    gathered, pos, vel, acc, jrk, levels, masses, active, packed, old, sources, targets, sums
):
    groups = levels.shape[0]
    ntarget = active.shape[1]
    state = gathered[0]
    for k in range(1, gathered.shape[0]):
        state = state + gathered[k]
    old[...] = state
    tpos, tvel = predict(
        state[0:3], state[3:6], state[6:9], state[9:12], step_factors(state[12:13])
    )
    columns = jnp.transpose(
        jnp.concatenate([tpos, tvel, jnp.zeros((LANES - 6, ntarget), f32)], axis=0)
    )
    for c in range(6):
        targets[c] = jnp.broadcast_to(columns[:, c : c + 1], (ntarget, LANES))
    factors = step_factors(elapsed_of(levels[...]))
    for t in range(groups):
        spos, svel = predict(
            *(x[:, tile(t)] for x in (pos, vel, acc, jrk)), [f[t : t + 1] for f in factors]
        )
        sources[t, 0:3, :] = spos
        sources[t, 3:6, :] = svel
        sources[t, 6:7, :] = masses[t : t + 1, :]

    def one_group(g, unused):
        rows = pl.ds(pl.multiple_of(g * 8, 8), 8)
        tx, ty, tz, tu, tv, tw = (targets[c, rows, :] for c in range(6))

        def one_tile(t, carry):
            sx, sy, sz, su, sv, sw, mass = (
                jnp.broadcast_to(sources[t, c : c + 1, :], (8, LANES)) for c in range(7)
            )
            dx, dy, dz = (sx - tx, sy - ty, sz - tz)
            du, dv, dw = (su - tu, sv - tv, sw - tw)
            r2 = dx * dx + dy * dy + dz * dz + softening_length
            inv = lax.rsqrt(r2)
            inv_sq = inv * inv
            weight = mass * inv * inv_sq
            radial = (dx * du + dy * dv + dz * dw) * inv_sq
            px, py, pz = (weight * dx, weight * dy, weight * dz)
            ax, ay, az, jx, jy, jz, kx, ky, kz = carry
            return (
                ax + px,
                ay + py,
                az + pz,
                jx + weight * du,
                jy + weight * dv,
                jz + weight * dw,
                kx + radial * px,
                ky + radial * py,
                kz + radial * pz,
            )

        zero = jnp.zeros((8, LANES), f32)
        ax, ay, az, jx, jy, jz, kx, ky, kz = lax.fori_loop(
            0, groups, one_tile, (zero,) * 9, unroll=32
        )
        for c, value in enumerate((ax, ay, az, jx - 3.0 * kx, jy - 3.0 * ky, jz - 3.0 * kz)):
            sums[c, rows, :] = value
        return unused

    lax.fori_loop(0, ntarget // 8, one_group, 0)
    lane = lax.broadcasted_iota(jnp.int32, (ntarget, LANES), 1)
    table = jnp.zeros((ntarget, LANES), f32)
    for c in range(6):
        table = jnp.where(lane == c, jnp.sum(sums[c], axis=1, keepdims=True), table)
    table = jnp.transpose(table)[0:8]
    row = lax.broadcasted_iota(jnp.int32, (8, ntarget), 0)
    table = jnp.where(row == 6, active[...].astype(f32), table)
    for k in range(packed.shape[0]):
        for c in range(NEW_ROWS):
            packed[k, :, tile(c)] = table[c : c + 1]


def laid_out(rows, columns, everyone, rowed, groups, before):
    ntarget = rowed.shape[2]
    base = lax.axis_index("ja") * (groups * LANES)
    order = pair_order(rows, columns)
    group = lax.broadcasted_iota(jnp.int32, (groups, ntarget), 0)
    lane = lax.broadcasted_iota(jnp.int32, (LANES, ntarget), 0)
    number = lax.broadcasted_iota(jnp.int32, (groups, ntarget), 1).astype(f32) + 1.0
    spot = jnp.zeros((groups, LANES), f32)
    part = jnp.full((groups, LANES), -1.0, f32)
    forces = []
    for r in range(rows // 2):
        first, *others = [k for k, (h, _) in enumerate(order) if h == r]
        total = everyone[first]
        for k in others:
            total = total + everyone[k]
        for c in range(6):
            rowed[r, c : c + 1, :] = total[:, tile(c)]
        rowed[r, 6:8, :] = jnp.ones((2, ntarget), f32)
        forces.append(rowed[r])
        offset = everyone[first][:, tile(6)].astype(jnp.int32) - base
        hit = group == offset >> 7
        side = (lane == (offset & (LANES - 1))).astype(jnp.bfloat16)
        found = lax.dot_general(
            jnp.where(hit, number, 0.0).astype(jnp.bfloat16),
            side,
            (((1,), (1,)), ((), ())),
            preferred_element_type=f32,
        )
        part = jnp.where(found > 0.5, float(r), part)
        spot = spot + found
    slot = jnp.maximum(spot - 1.0, 0.0).astype(jnp.int32)
    for t in range(groups):
        lanes = jnp.broadcast_to(slot[t : t + 1], (8, LANES))
        holder = jnp.broadcast_to(part[t : t + 1], (8, LANES))
        new = before(t)
        for r in range(rows // 2):
            new = jnp.where(holder == float(r), jnp.take_along_axis(forces[r], lanes, axis=1), new)
        yield new


def same_kernel(rows, columns, same_core, old, targets_new, placed, rowed):
    zero = jnp.zeros((8, LANES), f32)
    tiles = laid_out(rows, columns, same_core, rowed, placed.shape[0], lambda t: zero)
    for t, new in enumerate(tiles):
        placed[t] = new
    me = lax.axis_index("ia") >> 1
    mine = rowed[0]
    for r in range(1, rows // 2):
        mine = jnp.where(me == r, rowed[r], mine)
    o = old[...]
    factors = correction_factors(o[12:13])
    x1, v1 = correct(o[0:3], o[3:6], o[6:9], o[9:12], factors, mine[0:3], mine[3:6])
    targets_new[0:3, :] = x1
    targets_new[3:6, :] = v1
    targets_new[6:12, :] = mine[0:6]


def finish_kernel(
    rows, columns, other_core, placed, pos, vel, acc, jrk, levels, stars_out, stars_new, rowed, sems
):
    groups = levels.shape[0]
    piece = groups // PIECES
    copies = []
    factors = correction_factors(elapsed_of(levels[...]))
    tiles = laid_out(rows, columns, other_core, rowed, groups, lambda t: placed[t])
    for t, new in enumerate(tiles):
        there = jnp.broadcast_to(new[7:8], (3, LANES)) > 0.5
        x0, v0, a0, j0 = (pos[:, tile(t)], vel[:, tile(t)], acc[:, tile(t)], jrk[:, tile(t)])
        a1, j1 = (new[0:3], new[3:6])
        x1, v1 = correct(x0, v0, a0, j0, [f[t : t + 1] for f in factors], a1, j1)
        stars_new[0:3, tile(t)] = jnp.where(there, x1, x0)
        stars_new[3:6, tile(t)] = jnp.where(there, v1, v0)
        stars_new[6:9, tile(t)] = jnp.where(there, a1, a0)
        stars_new[9:12, tile(t)] = jnp.where(there, j1, j0)
        if (t + 1) % piece == 0:
            part_of = (slice(None), slice((t + 1 - piece) * LANES, (t + 1) * LANES))
            copies.append(
                pltpu.make_async_copy(
                    stars_new.at[part_of], stars_out.at[part_of], sems.at[len(copies)]
                )
            )
            copies[-1].start()
    for copy in copies:
        copy.wait()


def local(rows, columns, positions, velocities, accels, jerks, masses, levels, active):
    nlocal = positions.shape[1]
    ntarget = active.shape[0]
    groups = nlocal // LANES
    given = (
        positions,
        velocities,
        accels,
        jerks,
        levels.reshape(groups, LANES),
        masses.reshape(groups, LANES),
        active.reshape(1, ntarget),
    )
    mine, *kept = pl.pallas_call(
        gather_kernel,
        out_shape=(
            pltpu.VMEM((columns, 16, ntarget), f32),
            *(pltpu.VMEM(x.shape, x.dtype) for x in given),
        ),
        in_specs=[HBM] * 7,
        out_specs=(VMEM,) * 8,
        scratch_shapes=[pltpu.SemaphoreType.DMA((11,))],
        compiler_params=PARAMS,
        name="gather",
    )(*(pltpu.with_memory_space_constraint(x, pltpu.HBM) for x in given))
    gathered = lax.all_to_all(mine, "ja", 0, 0, axis_index_groups=[column_order(columns)])
    packed, old = pl.pallas_call(
        force_kernel,
        out_shape=(
            pltpu.VMEM((rows // 2 * columns, 1, NEW_ROWS * ntarget), f32),
            pltpu.VMEM((16, ntarget), f32),
        ),
        in_specs=[VMEM] * 8,
        out_specs=(VMEM, VMEM),
        scratch_shapes=[
            pltpu.VMEM((groups, 8, LANES), f32),
            pltpu.VMEM((6, ntarget, LANES), f32),
            pltpu.VMEM((6, ntarget, LANES), f32),
        ],
        compiler_params=PARAMS,
        name="forces",
    )(gathered, *kept)
    order = pair_order(rows, columns)
    lists = [[(2 * h + core) * columns + c for h, c in order] for core in range(2)]
    same_core = lax.all_to_all(packed, ("ia", "ja"), 0, 0, axis_index_groups=lists)
    other_core = lax.ppermute(same_core, "ia", [(r, r ^ 1) for r in range(rows)])
    targets_new, placed = pl.pallas_call(
        functools.partial(same_kernel, rows, columns),
        out_shape=(
            jax.ShapeDtypeStruct((12, ntarget), f32),
            pltpu.VMEM((groups, 8, LANES), f32),
        ),
        in_specs=[VMEM] * 2,
        out_specs=(VMEM, VMEM),
        scratch_shapes=[pltpu.VMEM((rows // 2, 8, ntarget), f32)],
        compiler_params=PARAMS,
        cost_estimate=pl.CostEstimate(
            flops=200 * nlocal, bytes_accessed=4 * 64 * nlocal, transcendentals=0
        ),
        name="same",
    )(same_core, old)
    stars_new = pl.pallas_call(
        functools.partial(finish_kernel, rows, columns),
        out_shape=jax.ShapeDtypeStruct((12, nlocal), f32),
        in_specs=[VMEM] * 7,
        out_specs=HBM,
        scratch_shapes=[
            pltpu.VMEM((12, nlocal), f32),
            pltpu.VMEM((rows // 2, 8, ntarget), f32),
            pltpu.SemaphoreType.DMA((PIECES,)),
        ],
        compiler_params=PARAMS,
        name="finish",
    )(other_core, placed, *kept[:5])
    return (targets_new, stars_new)


def solution(mesh):
    rows, columns = mesh.shape["ia"], mesh.shape["ja"]

    def body(*args):
        return local(rows, columns, *args)

    return jax.shard_map(
        body,
        mesh=mesh,
        in_specs=(
            P(None, "ja"),
            P(None, "ja"),
            P(None, "ja"),
            P(None, "ja"),
            P("ja"),
            P("ja"),
            P("ia"),
        ),
        out_specs=(P(None, "ia"), P(None, "ja")),
        check_vma=False,
    )
```

```python
import functools

import jax
import jax.numpy as jnp
from jax import lax
from jax.experimental import pallas as pl
from jax.experimental.pallas import tpu as pltpu
from jax.sharding import PartitionSpec as P

softening_length = 0.01
base_step = 0.0625
LANES = 128
PIECES = 8
NEW_ROWS = 7
f32 = jnp.float32
VMEM = pl.BlockSpec(memory_space=pltpu.VMEM)
HBM = pl.BlockSpec(memory_space=pltpu.HBM)
PARAMS = pltpu.CompilerParams(vmem_limit_bytes=24 * 1024 * 1024)


def elapsed_of(levels):
    return (128 >> levels).astype(f32) * (base_step / 128.0)


def step_factors(elapsed):
    half = elapsed * elapsed * 0.5
    return (elapsed, half, half * elapsed * (1.0 / 3.0))


def predict(pos, vel, acc, jrk, factors):
    elapsed, half, sixth = factors
    pred_pos = pos + elapsed * vel + half * acc + sixth * jrk
    pred_vel = vel + elapsed * acc + half * jrk
    return (pred_pos, pred_vel)


def correction_factors(step):
    return (0.5 * step, step * step * (1.0 / 12.0))


def correct(x0, v0, a0, j0, factors, a1, j1):
    half, quad = factors
    v1 = v0 + half * (a0 + a1) + quad * (j0 - j1)
    x1 = x0 + half * (v0 + v1) + quad * (a0 - a1)
    return (x1, v1)


def column_order(columns):
    first = max(columns - 3, 0)
    return [*range(first, columns), *range(first)]


def pair_order(rows, columns):
    return [(h, c) for h in range(rows // 2 - 1, -1, -1) for c in range(columns - 1, -1, -1)]


def tile(t):
    return slice(t * LANES, (t + 1) * LANES)


def gather_kernel(*refs):
    given, out, kept, sems = (refs[:7], refs[7], refs[8:15], refs[15])
    pos, vel, acc, jrk, levels, masses, active = kept
    groups = levels.shape[0]
    half = groups // 2

    def copy_of(n, sem, columns=None):
        if columns is None:
            return pltpu.make_async_copy(given[n], kept[n], sems.at[sem])
        part = (slice(None), columns)
        return pltpu.make_async_copy(given[n].at[part], kept[n].at[part], sems.at[sem])

    small = [copy_of(6, 0), copy_of(4, 1)]
    parts = [
        [copy_of(n, 2 + 4 * h + n, slice(h * half * LANES, (h + 1) * half * LANES)) for n in range(4)]
        for h in range(2)
    ]
    late = copy_of(5, 10)
    for copy in (*small, *parts[0], *parts[1], late):
        copy.start()
    for copy in small:
        copy.wait()
    offset = active[...] - lax.axis_index("ja") * (groups * LANES)
    group = jnp.broadcast_to(offset >> 7, (8, LANES))
    lane = jnp.broadcast_to(offset & (LANES - 1), (8, LANES))
    row = lax.broadcasted_iota(jnp.int32, (8, LANES), 0)
    elapsed = elapsed_of(levels[...])
    steps = jnp.zeros((8, LANES), f32)
    for t in range(0, groups, 8):
        here = group == row + t
        steps = jnp.where(here, jnp.take_along_axis(elapsed[t : t + 8], lane, axis=1), steps)
    found = [jnp.zeros((3, LANES), f32)] * 4
    for h in range(2):
        for copy in parts[h]:
            copy.wait()
        for t in range(h * half, (h + 1) * half):
            here = group[0:3] == t
            found = [
                jnp.where(here, jnp.take_along_axis(x[:, tile(t)], lane[0:3], axis=1), old)
                for x, old in zip((pos, vel, acc, jrk), found)
            ]
    steps = jnp.broadcast_to(jnp.sum(steps, axis=0, keepdims=True), (4, LANES))
    for k in range(out.shape[0]):
        for n, value in enumerate(found):
            out[k, 3 * n : 3 * n + 3, :] = value
        out[k, 12:16, :] = steps
    late.wait()


def force_kernel(
    gathered, pos, vel, acc, jrk, levels, masses, active, packed, old, sources, targets, sums
):
    groups = levels.shape[0]
    ntarget = active.shape[1]
    state = gathered[0]
    for k in range(1, gathered.shape[0]):
        state = state + gathered[k]
    old[...] = state
    tpos, tvel = predict(
        state[0:3], state[3:6], state[6:9], state[9:12], step_factors(state[12:13])
    )
    columns = jnp.transpose(
        jnp.concatenate([tpos, tvel, jnp.zeros((LANES - 6, ntarget), f32)], axis=0)
    )
    for c in range(6):
        targets[c] = jnp.broadcast_to(columns[:, c : c + 1], (ntarget, LANES))
    factors = step_factors(elapsed_of(levels[...]))
    for t in range(groups):
        spos, svel = predict(
            *(x[:, tile(t)] for x in (pos, vel, acc, jrk)), [f[t : t + 1] for f in factors]
        )
        sources[t, 0:3, :] = spos
        sources[t, 3:6, :] = svel
        sources[t, 6:7, :] = masses[t : t + 1, :]

    def one_group(g, unused):
        rows = pl.ds(pl.multiple_of(g * 8, 8), 8)
        tx, ty, tz, tu, tv, tw = (targets[c, rows, :] for c in range(6))

        def one_tile(t, carry):
            sx, sy, sz, su, sv, sw, mass = (
                jnp.broadcast_to(sources[t, c : c + 1, :], (8, LANES)) for c in range(7)
            )
            dx, dy, dz = (sx - tx, sy - ty, sz - tz)
            du, dv, dw = (su - tu, sv - tv, sw - tw)
            r2 = dx * dx + dy * dy + dz * dz + softening_length
            inv = lax.rsqrt(r2)
            inv_sq = inv * inv
            weight = mass * inv * inv_sq
            radial = (dx * du + dy * dv + dz * dw) * inv_sq
            px, py, pz = (weight * dx, weight * dy, weight * dz)
            ax, ay, az, jx, jy, jz, kx, ky, kz = carry
            return (
                ax + px,
                ay + py,
                az + pz,
                jx + weight * du,
                jy + weight * dv,
                jz + weight * dw,
                kx + radial * px,
                ky + radial * py,
                kz + radial * pz,
            )

        zero = jnp.zeros((8, LANES), f32)
        ax, ay, az, jx, jy, jz, kx, ky, kz = lax.fori_loop(
            0, groups, one_tile, (zero,) * 9, unroll=32
        )
        for c, value in enumerate((ax, ay, az, jx - 3.0 * kx, jy - 3.0 * ky, jz - 3.0 * kz)):
            sums[c, rows, :] = value
        return unused

    lax.fori_loop(0, ntarget // 8, one_group, 0)
    lane = lax.broadcasted_iota(jnp.int32, (ntarget, LANES), 1)
    table = jnp.zeros((ntarget, LANES), f32)
    for c in range(6):
        table = jnp.where(lane == c, jnp.sum(sums[c], axis=1, keepdims=True), table)
    table = jnp.transpose(table)[0:8]
    row = lax.broadcasted_iota(jnp.int32, (8, ntarget), 0)
    table = jnp.where(row == 6, active[...].astype(f32), table)
    for k in range(packed.shape[0]):
        for c in range(NEW_ROWS):
            packed[k, :, tile(c)] = table[c : c + 1]


def laid_out(rows, columns, everyone, rowed, slots, parts, before):
    ntarget = rowed.shape[2]
    groups = slots.shape[0]
    base = lax.axis_index("ja") * (groups * LANES)
    order = pair_order(rows, columns)
    group = lax.broadcasted_iota(jnp.int32, (groups, ntarget), 0)
    lane = lax.broadcasted_iota(jnp.int32, (LANES, ntarget), 0)
    number = lax.broadcasted_iota(jnp.int32, (groups, ntarget), 1).astype(f32) + 1.0
    spot = jnp.zeros((groups, LANES), f32)
    part = jnp.full((groups, LANES), -1.0, f32)
    forces = []
    for r in range(rows // 2):
        first, *others = [k for k, (h, _) in enumerate(order) if h == r]
        total = everyone[first]
        for k in others:
            total = total + everyone[k]
        for c in range(6):
            rowed[r, c : c + 1, :] = total[:, tile(c)]
        rowed[r, 6:8, :] = jnp.ones((2, ntarget), f32)
        forces.append(rowed[r])
        offset = everyone[first][:, tile(6)].astype(jnp.int32) - base
        hit = group == offset >> 7
        side = (lane == (offset & (LANES - 1))).astype(jnp.bfloat16)
        found = lax.dot_general(
            jnp.where(hit, number, 0.0).astype(jnp.bfloat16),
            side,
            (((1,), (1,)), ((), ())),
            preferred_element_type=f32,
        )
        part = jnp.where(found > 0.5, float(r), part)
        spot = spot + found
    slots[...] = jnp.maximum(spot - 1.0, 0.0).astype(jnp.int32)
    parts[...] = part
    for t in range(groups):
        lanes = jnp.broadcast_to(slots[t : t + 1, :], (8, LANES))
        holder = jnp.broadcast_to(parts[t : t + 1, :], (8, LANES))
        new = before(t)
        for r in range(rows // 2):
            new = jnp.where(holder == float(r), jnp.take_along_axis(forces[r], lanes, axis=1), new)
        yield new


def same_kernel(rows, columns, same_core, old, targets_new, placed, rowed, slots, parts):
    zero = jnp.zeros((8, LANES), f32)
    tiles = laid_out(rows, columns, same_core, rowed, slots, parts, lambda t: zero)
    for t, new in enumerate(tiles):
        placed[t] = new
    me = lax.axis_index("ia") >> 1
    mine = rowed[0]
    for r in range(1, rows // 2):
        mine = jnp.where(me == r, rowed[r], mine)
    o = old[...]
    factors = correction_factors(o[12:13])
    x1, v1 = correct(o[0:3], o[3:6], o[6:9], o[9:12], factors, mine[0:3], mine[3:6])
    targets_new[0:3, :] = x1
    targets_new[3:6, :] = v1
    targets_new[6:12, :] = mine[0:6]


def finish_kernel(
    rows, columns, other_core, placed, pos, vel, acc, jrk, levels, stars_out,
    stars_new, rowed, slots, parts, steps, sems
):
    groups = levels.shape[0]
    piece = groups // PIECES
    copies = []
    steps[0], steps[1] = correction_factors(elapsed_of(levels[...]))
    tiles = laid_out(rows, columns, other_core, rowed, slots, parts, lambda t: placed[t])
    for t, new in enumerate(tiles):
        there = jnp.broadcast_to(new[7:8], (3, LANES)) > 0.5
        x0, v0, a0, j0 = (pos[:, tile(t)], vel[:, tile(t)], acc[:, tile(t)], jrk[:, tile(t)])
        a1, j1 = (new[0:3], new[3:6])
        factors = [jnp.broadcast_to(steps[n, t : t + 1, :], (3, LANES)) for n in range(2)]
        x1, v1 = correct(x0, v0, a0, j0, factors, a1, j1)
        stars_new[0:3, tile(t)] = jnp.where(there, x1, x0)
        stars_new[3:6, tile(t)] = jnp.where(there, v1, v0)
        stars_new[6:9, tile(t)] = jnp.where(there, a1, a0)
        stars_new[9:12, tile(t)] = jnp.where(there, j1, j0)
        if (t + 1) % piece == 0:
            part_of = (slice(None), slice((t + 1 - piece) * LANES, (t + 1) * LANES))
            copies.append(
                pltpu.make_async_copy(
                    stars_new.at[part_of], stars_out.at[part_of], sems.at[len(copies)]
                )
            )
            copies[-1].start()
    for copy in copies:
        copy.wait()


def local(rows, columns, positions, velocities, accels, jerks, masses, levels, active):
    nlocal = positions.shape[1]
    ntarget = active.shape[0]
    groups = nlocal // LANES
    given = (
        positions,
        velocities,
        accels,
        jerks,
        levels.reshape(groups, LANES),
        masses.reshape(groups, LANES),
        active.reshape(1, ntarget),
    )
    mine, *kept = pl.pallas_call(
        gather_kernel,
        out_shape=(
            pltpu.VMEM((columns, 16, ntarget), f32),
            *(pltpu.VMEM(x.shape, x.dtype) for x in given),
        ),
        in_specs=[HBM] * 7,
        out_specs=(VMEM,) * 8,
        scratch_shapes=[pltpu.SemaphoreType.DMA((11,))],
        compiler_params=PARAMS,
        name="gather",
    )(*(pltpu.with_memory_space_constraint(x, pltpu.HBM) for x in given))
    gathered = lax.all_to_all(mine, "ja", 0, 0, axis_index_groups=[column_order(columns)])
    packed, old = pl.pallas_call(
        force_kernel,
        out_shape=(
            pltpu.VMEM((rows // 2 * columns, 1, NEW_ROWS * ntarget), f32),
            pltpu.VMEM((16, ntarget), f32),
        ),
        in_specs=[VMEM] * 8,
        out_specs=(VMEM, VMEM),
        scratch_shapes=[
            pltpu.VMEM((groups, 8, LANES), f32),
            pltpu.VMEM((6, ntarget, LANES), f32),
            pltpu.VMEM((6, ntarget, LANES), f32),
        ],
        compiler_params=PARAMS,
        name="forces",
    )(gathered, *kept)
    order = pair_order(rows, columns)
    lists = [[(2 * h + core) * columns + c for h, c in order] for core in range(2)]
    same_core = lax.all_to_all(packed, ("ia", "ja"), 0, 0, axis_index_groups=lists)
    other_core = lax.ppermute(same_core, "ia", [(r, r ^ 1) for r in range(rows)])
    targets_new, placed = pl.pallas_call(
        functools.partial(same_kernel, rows, columns),
        out_shape=(
            jax.ShapeDtypeStruct((12, ntarget), f32),
            pltpu.VMEM((groups, 8, LANES), f32),
        ),
        in_specs=[VMEM] * 2,
        out_specs=(VMEM, VMEM),
        scratch_shapes=[
            pltpu.VMEM((rows // 2, 8, ntarget), f32),
            pltpu.VMEM((groups, LANES), jnp.int32),
            pltpu.VMEM((groups, LANES), f32),
        ],
        compiler_params=PARAMS,
        cost_estimate=pl.CostEstimate(
            flops=200 * nlocal, bytes_accessed=4 * 64 * nlocal, transcendentals=0
        ),
        name="same",
    )(same_core, old)
    stars_new = pl.pallas_call(
        functools.partial(finish_kernel, rows, columns),
        out_shape=jax.ShapeDtypeStruct((12, nlocal), f32),
        in_specs=[VMEM] * 7,
        out_specs=HBM,
        scratch_shapes=[
            pltpu.VMEM((12, nlocal), f32),
            pltpu.VMEM((rows // 2, 8, ntarget), f32),
            pltpu.VMEM((groups, LANES), jnp.int32),
            pltpu.VMEM((groups, LANES), f32),
            pltpu.VMEM((2, groups, LANES), f32),
            pltpu.SemaphoreType.DMA((PIECES,)),
        ],
        compiler_params=PARAMS,
        name="finish",
    )(other_core, placed, *kept[:5])
    return (targets_new, stars_new)


def solution(mesh):
    rows, columns = mesh.shape["ia"], mesh.shape["ja"]

    def body(*args):
        return local(rows, columns, *args)

    return jax.shard_map(
        body,
        mesh=mesh,
        in_specs=(
            P(None, "ja"),
            P(None, "ja"),
            P(None, "ja"),
            P(None, "ja"),
            P("ja"),
            P("ja"),
            P("ia"),
        ),
        out_specs=(P(None, "ia"), P(None, "ja")),
        check_vma=False,
    )
```

```python
import functools

import jax
import jax.numpy as jnp
from jax import lax
from jax.experimental import pallas as pl
from jax.experimental.pallas import tpu as pltpu
from jax.sharding import PartitionSpec as P

softening_length = 0.01
base_step = 0.0625
LANES = 128
PIECES = 8
NEW_ROWS = 7
f32 = jnp.float32
VMEM = pl.BlockSpec(memory_space=pltpu.VMEM)
HBM = pl.BlockSpec(memory_space=pltpu.HBM)
PARAMS = pltpu.CompilerParams(vmem_limit_bytes=24 * 1024 * 1024)


def elapsed_of(levels):
    return (128 >> levels).astype(f32) * (base_step / 128.0)


def step_factors(elapsed):
    half = elapsed * elapsed * 0.5
    return (elapsed, half, half * elapsed * (1.0 / 3.0))


def predict(pos, vel, acc, jrk, factors):
    elapsed, half, sixth = factors
    pred_pos = pos + elapsed * vel + half * acc + sixth * jrk
    pred_vel = vel + elapsed * acc + half * jrk
    return (pred_pos, pred_vel)


def correction_factors(step):
    return (0.5 * step, step * step * (1.0 / 12.0))


def correct(x0, v0, a0, j0, factors, a1, j1):
    half, quad = factors
    v1 = v0 + half * (a0 + a1) + quad * (j0 - j1)
    x1 = x0 + half * (v0 + v1) + quad * (a0 - a1)
    return (x1, v1)


def column_order(columns):
    first = max(columns - 3, 0)
    return [*range(first, columns), *range(first)]


def pair_order(rows, columns):
    return [(h, c) for h in range(rows // 2 - 1, -1, -1) for c in range(columns - 1, -1, -1)]


def tile(t):
    return slice(t * LANES, (t + 1) * LANES)


def gather_kernel(*refs):
    given, out, kept, sems = (refs[:7], refs[7], refs[8:15], refs[15])
    pos, vel, acc, jrk, levels, masses, active = kept
    groups = levels.shape[0]
    half = groups // 2

    def copy_of(n, sem, columns=None):
        if columns is None:
            return pltpu.make_async_copy(given[n], kept[n], sems.at[sem])
        part = (slice(None), columns)
        return pltpu.make_async_copy(given[n].at[part], kept[n].at[part], sems.at[sem])

    small = [copy_of(6, 0), copy_of(4, 1)]
    parts = [
        [copy_of(n, 2 + 4 * h + n, slice(h * half * LANES, (h + 1) * half * LANES)) for n in range(4)]
        for h in range(2)
    ]
    late = copy_of(5, 10)
    for copy in (*small, *parts[0], *parts[1], late):
        copy.start()
    for copy in small:
        copy.wait()
    offset = active[...] - lax.axis_index("ja") * (groups * LANES)
    group = jnp.broadcast_to(offset >> 7, (8, LANES))
    lane = jnp.broadcast_to(offset & (LANES - 1), (8, LANES))
    row = lax.broadcasted_iota(jnp.int32, (8, LANES), 0)
    elapsed = elapsed_of(levels[...])
    steps = jnp.zeros((8, LANES), f32)
    for t in range(0, groups, 8):
        here = group == row + t
        steps = jnp.where(here, jnp.take_along_axis(elapsed[t : t + 8], lane, axis=1), steps)
    found = [jnp.zeros((3, LANES), f32)] * 4
    for h in range(2):
        for copy in parts[h]:
            copy.wait()
        for t in range(h * half, (h + 1) * half):
            here = group[0:3] == t
            found = [
                jnp.where(here, jnp.take_along_axis(x[:, tile(t)], lane[0:3], axis=1), old)
                for x, old in zip((pos, vel, acc, jrk), found)
            ]
    steps = jnp.broadcast_to(jnp.sum(steps, axis=0, keepdims=True), (4, LANES))
    for k in range(out.shape[0]):
        for n, value in enumerate(found):
            out[k, 3 * n : 3 * n + 3, :] = value
        out[k, 12:16, :] = steps
    late.wait()


def force_kernel(
    gathered, pos, vel, acc, jrk, levels, masses, active, packed, old, sources, targets, sums
):
    groups = levels.shape[0]
    ntarget = active.shape[1]
    state = gathered[0]
    for k in range(1, gathered.shape[0]):
        state = state + gathered[k]
    old[...] = state
    tpos, tvel = predict(
        state[0:3], state[3:6], state[6:9], state[9:12], step_factors(state[12:13])
    )
    columns = jnp.transpose(
        jnp.concatenate([tpos, tvel, tpos[0:2]], axis=0)
    )
    for c in range(6):
        targets[c] = jnp.broadcast_to(columns[:, c : c + 1], (ntarget, LANES))
    factors = step_factors(elapsed_of(levels[...]))
    for t in range(groups):
        spos, svel = predict(
            *(x[:, tile(t)] for x in (pos, vel, acc, jrk)), [f[t : t + 1] for f in factors]
        )
        sources[t, 0:3, :] = spos
        sources[t, 3:6, :] = svel
        sources[t, 6:7, :] = masses[t : t + 1, :]

    def one_group(g, unused):
        rows = pl.ds(pl.multiple_of(g * 8, 8), 8)
        tx, ty, tz, tu, tv, tw = (targets[c, rows, :] for c in range(6))

        def one_tile(t, carry):
            sx, sy, sz, su, sv, sw, mass = (
                jnp.broadcast_to(sources[t, c : c + 1, :], (8, LANES)) for c in range(7)
            )
            dx, dy, dz = (sx - tx, sy - ty, sz - tz)
            du, dv, dw = (su - tu, sv - tv, sw - tw)
            r2 = dx * dx + dy * dy + dz * dz + softening_length
            inv = lax.rsqrt(r2)
            inv_sq = inv * inv
            weight = mass * inv * inv_sq
            radial = (dx * du + dy * dv + dz * dw) * inv_sq
            px, py, pz = (weight * dx, weight * dy, weight * dz)
            ax, ay, az, jx, jy, jz, kx, ky, kz = carry
            return (
                ax + px,
                ay + py,
                az + pz,
                jx + weight * du,
                jy + weight * dv,
                jz + weight * dw,
                kx + radial * px,
                ky + radial * py,
                kz + radial * pz,
            )

        zero = jnp.zeros((8, LANES), f32)
        ax, ay, az, jx, jy, jz, kx, ky, kz = lax.fori_loop(
            0, groups, one_tile, (zero,) * 9, unroll=32
        )
        for c, value in enumerate((ax, ay, az, jx - 3.0 * kx, jy - 3.0 * ky, jz - 3.0 * kz)):
            sums[c, rows, :] = value
        return unused

    lax.fori_loop(0, ntarget // 8, one_group, 0)
    lane = lax.broadcasted_iota(jnp.int32, (ntarget, 8), 1)
    table = jnp.zeros((ntarget, 8), f32)
    for c in range(6):
        table = jnp.where(lane == c, jnp.sum(sums[c], axis=1, keepdims=True), table)
    table = jnp.transpose(table)
    row = lax.broadcasted_iota(jnp.int32, (8, ntarget), 0)
    table = jnp.where(row == 6, active[...].astype(f32), table)
    for k in range(packed.shape[0]):
        for c in range(NEW_ROWS):
            packed[k, :, tile(c)] = table[c : c + 1]


def laid_out(rows, columns, everyone, rowed, groups, before):
    ntarget = rowed.shape[2]
    base = lax.axis_index("ja") * (groups * LANES)
    order = pair_order(rows, columns)
    group = lax.broadcasted_iota(jnp.int32, (groups, ntarget), 0)
    lane = lax.broadcasted_iota(jnp.int32, (LANES, ntarget), 0)
    number = lax.broadcasted_iota(jnp.int32, (groups, ntarget), 1).astype(f32) + 1.0
    spot = jnp.zeros((groups, LANES), f32)
    part = jnp.full((groups, LANES), -1.0, f32)
    forces = []
    for r in range(rows // 2):
        first, *others = [k for k, (h, _) in enumerate(order) if h == r]
        total = everyone[first]
        for k in others:
            total = total + everyone[k]
        for c in range(6):
            rowed[r, c : c + 1, :] = total[:, tile(c)]
        rowed[r, 6:8, :] = jnp.ones((2, ntarget), f32)
        forces.append(rowed[r])
        offset = everyone[first][:, tile(6)].astype(jnp.int32) - base
        hit = group == offset >> 7
        side = (lane == (offset & (LANES - 1))).astype(jnp.bfloat16)
        found = lax.dot_general(
            jnp.where(hit, number, 0.0).astype(jnp.bfloat16),
            side,
            (((1,), (1,)), ((), ())),
            preferred_element_type=f32,
        )
        part = jnp.where(found > 0.5, float(r), part)
        spot = spot + found
    slot = jnp.maximum(spot - 1.0, 0.0).astype(jnp.int32)
    for t in range(groups):
        lanes = jnp.broadcast_to(slot[t : t + 1], (8, LANES))
        holder = jnp.broadcast_to(part[t : t + 1], (8, LANES))
        new = before(t)
        for r in range(rows // 2):
            new = jnp.where(holder == float(r), jnp.take_along_axis(forces[r], lanes, axis=1), new)
        yield new


def same_kernel(rows, columns, same_core, old, targets_new, placed, rowed):
    zero = jnp.zeros((8, LANES), f32)
    tiles = laid_out(rows, columns, same_core, rowed, placed.shape[0], lambda t: zero)
    for t, new in enumerate(tiles):
        placed[t] = new
    me = lax.axis_index("ia") >> 1
    mine = rowed[0]
    for r in range(1, rows // 2):
        mine = jnp.where(me == r, rowed[r], mine)
    o = old[...]
    factors = correction_factors(o[12:13])
    x1, v1 = correct(o[0:3], o[3:6], o[6:9], o[9:12], factors, mine[0:3], mine[3:6])
    targets_new[0:3, :] = x1
    targets_new[3:6, :] = v1
    targets_new[6:12, :] = mine[0:6]


def finish_kernel(
    rows, columns, other_core, placed, pos, vel, acc, jrk, levels, stars_out, stars_new, rowed, sems
):
    groups = levels.shape[0]
    piece = groups // PIECES
    copies = []
    factors = correction_factors(elapsed_of(levels[...]))
    tiles = laid_out(rows, columns, other_core, rowed, groups, lambda t: placed[t])
    for t, new in enumerate(tiles):
        there = jnp.broadcast_to(new[7:8], (3, LANES)) > 0.5
        x0, v0, a0, j0 = (pos[:, tile(t)], vel[:, tile(t)], acc[:, tile(t)], jrk[:, tile(t)])
        a1, j1 = (new[0:3], new[3:6])
        x1, v1 = correct(x0, v0, a0, j0, [f[t : t + 1] for f in factors], a1, j1)
        stars_new[0:3, tile(t)] = jnp.where(there, x1, x0)
        stars_new[3:6, tile(t)] = jnp.where(there, v1, v0)
        stars_new[6:9, tile(t)] = jnp.where(there, a1, a0)
        stars_new[9:12, tile(t)] = jnp.where(there, j1, j0)
        if (t + 1) % piece == 0:
            part_of = (slice(None), slice((t + 1 - piece) * LANES, (t + 1) * LANES))
            copies.append(
                pltpu.make_async_copy(
                    stars_new.at[part_of], stars_out.at[part_of], sems.at[len(copies)]
                )
            )
            copies[-1].start()
    for copy in copies:
        copy.wait()


def local(rows, columns, positions, velocities, accels, jerks, masses, levels, active):
    nlocal = positions.shape[1]
    ntarget = active.shape[0]
    groups = nlocal // LANES
    given = (
        positions,
        velocities,
        accels,
        jerks,
        levels.reshape(groups, LANES),
        masses.reshape(groups, LANES),
        active.reshape(1, ntarget),
    )
    mine, *kept = pl.pallas_call(
        gather_kernel,
        out_shape=(
            pltpu.VMEM((columns, 16, ntarget), f32),
            *(pltpu.VMEM(x.shape, x.dtype) for x in given),
        ),
        in_specs=[HBM] * 7,
        out_specs=(VMEM,) * 8,
        scratch_shapes=[pltpu.SemaphoreType.DMA((11,))],
        compiler_params=PARAMS,
        name="gather",
    )(*(pltpu.with_memory_space_constraint(x, pltpu.HBM) for x in given))
    gathered = lax.all_to_all(mine, "ja", 0, 0, axis_index_groups=[column_order(columns)])
    packed, old = pl.pallas_call(
        force_kernel,
        out_shape=(
            pltpu.VMEM((rows // 2 * columns, 1, NEW_ROWS * ntarget), f32),
            pltpu.VMEM((16, ntarget), f32),
        ),
        in_specs=[VMEM] * 8,
        out_specs=(VMEM, VMEM),
        scratch_shapes=[
            pltpu.VMEM((groups, 8, LANES), f32),
            pltpu.VMEM((6, ntarget, LANES), f32),
            pltpu.VMEM((6, ntarget, LANES), f32),
        ],
        compiler_params=PARAMS,
        name="forces",
    )(gathered, *kept)
    order = pair_order(rows, columns)
    lists = [[(2 * h + core) * columns + c for h, c in order] for core in range(2)]
    same_core = lax.all_to_all(packed, ("ia", "ja"), 0, 0, axis_index_groups=lists)
    other_core = lax.ppermute(same_core, "ia", [(r, r ^ 1) for r in range(rows)])
    targets_new, placed = pl.pallas_call(
        functools.partial(same_kernel, rows, columns),
        out_shape=(
            jax.ShapeDtypeStruct((12, ntarget), f32),
            pltpu.VMEM((groups, 8, LANES), f32),
        ),
        in_specs=[VMEM] * 2,
        out_specs=(VMEM, VMEM),
        scratch_shapes=[pltpu.VMEM((rows // 2, 8, ntarget), f32)],
        compiler_params=PARAMS,
        cost_estimate=pl.CostEstimate(
            flops=200 * nlocal, bytes_accessed=4 * 64 * nlocal, transcendentals=0
        ),
        name="same",
    )(same_core, old)
    stars_new = pl.pallas_call(
        functools.partial(finish_kernel, rows, columns),
        out_shape=jax.ShapeDtypeStruct((12, nlocal), f32),
        in_specs=[VMEM] * 7,
        out_specs=HBM,
        scratch_shapes=[
            pltpu.VMEM((12, nlocal), f32),
            pltpu.VMEM((rows // 2, 8, ntarget), f32),
            pltpu.SemaphoreType.DMA((PIECES,)),
        ],
        compiler_params=PARAMS,
        name="finish",
    )(other_core, placed, *kept[:5])
    return (targets_new, stars_new)


def solution(mesh):
    rows, columns = mesh.shape["ia"], mesh.shape["ja"]

    def body(*args):
        return local(rows, columns, *args)

    return jax.shard_map(
        body,
        mesh=mesh,
        in_specs=(
            P(None, "ja"),
            P(None, "ja"),
            P(None, "ja"),
            P(None, "ja"),
            P("ja"),
            P("ja"),
            P("ia"),
        ),
        out_specs=(P(None, "ia"), P(None, "ja")),
        check_vma=False,
    )
```

```python
import functools

import jax
import jax.numpy as jnp
from jax import lax
from jax.experimental import pallas as pl
from jax.experimental.pallas import tpu as pltpu
from jax.sharding import PartitionSpec as P

softening_length = 0.01
base_step = 0.0625
LANES = 128
PIECES = 8
NEW_ROWS = 7
f32 = jnp.float32
VMEM = pl.BlockSpec(memory_space=pltpu.VMEM)
HBM = pl.BlockSpec(memory_space=pltpu.HBM)
PARAMS = pltpu.CompilerParams(vmem_limit_bytes=24 * 1024 * 1024)


def elapsed_of(levels):
    return (128 >> levels).astype(f32) * (base_step / 128.0)


def step_factors(elapsed):
    half = elapsed * elapsed * 0.5
    return (elapsed, half, half * elapsed * (1.0 / 3.0))


def predict(pos, vel, acc, jrk, factors):
    elapsed, half, sixth = factors
    pred_pos = pos + elapsed * vel + half * acc + sixth * jrk
    pred_vel = vel + elapsed * acc + half * jrk
    return (pred_pos, pred_vel)


def correction_factors(step):
    return (0.5 * step, step * step * (1.0 / 12.0))


def correct(x0, v0, a0, j0, factors, a1, j1):
    half, quad = factors
    v1 = v0 + half * (a0 + a1) + quad * (j0 - j1)
    x1 = x0 + half * (v0 + v1) + quad * (a0 - a1)
    return (x1, v1)


def column_order(columns):
    first = max(columns - 3, 0)
    return [*range(first, columns), *range(first)]


def pair_order(rows, columns):
    back = [(h, c) for h in range(rows // 2 - 1, -1, -1) for c in range(columns - 1, -1, -1)]
    return back[1:] + back[:1]


def tile(t):
    return slice(t * LANES, (t + 1) * LANES)


def gather_kernel(*refs):
    given, out, kept, sems = (refs[:7], refs[7], refs[8:15], refs[15])
    pos, vel, acc, jrk, levels, masses, active = kept
    groups = levels.shape[0]
    half = groups // 2

    def copy_of(n, sem, columns=None):
        if columns is None:
            return pltpu.make_async_copy(given[n], kept[n], sems.at[sem])
        part = (slice(None), columns)
        return pltpu.make_async_copy(given[n].at[part], kept[n].at[part], sems.at[sem])

    small = [copy_of(6, 0), copy_of(4, 1)]
    parts = [
        [copy_of(n, 2 + 4 * h + n, slice(h * half * LANES, (h + 1) * half * LANES)) for n in range(4)]
        for h in range(2)
    ]
    late = copy_of(5, 10)
    for copy in (*small, *parts[0], *parts[1], late):
        copy.start()
    for copy in small:
        copy.wait()
    offset = active[...] - lax.axis_index("ja") * (groups * LANES)
    group = jnp.broadcast_to(offset >> 7, (8, LANES))
    lane = jnp.broadcast_to(offset & (LANES - 1), (8, LANES))
    row = lax.broadcasted_iota(jnp.int32, (8, LANES), 0)
    elapsed = elapsed_of(levels[...])
    steps = jnp.zeros((8, LANES), f32)
    for t in range(0, groups, 8):
        here = group == row + t
        steps = jnp.where(here, jnp.take_along_axis(elapsed[t : t + 8], lane, axis=1), steps)
    found = [jnp.zeros((3, LANES), f32)] * 4
    for h in range(2):
        for copy in parts[h]:
            copy.wait()
        for t in range(h * half, (h + 1) * half):
            here = group[0:3] == t
            found = [
                jnp.where(here, jnp.take_along_axis(x[:, tile(t)], lane[0:3], axis=1), old)
                for x, old in zip((pos, vel, acc, jrk), found)
            ]
    steps = jnp.broadcast_to(jnp.sum(steps, axis=0, keepdims=True), (4, LANES))
    for k in range(out.shape[0]):
        for n, value in enumerate(found):
            out[k, 3 * n : 3 * n + 3, :] = value
        out[k, 12:16, :] = steps
    late.wait()


def force_kernel(
    gathered, pos, vel, acc, jrk, levels, masses, active, packed, old, sources, targets, sums
):
    groups = levels.shape[0]
    ntarget = active.shape[1]
    state = gathered[0]
    for k in range(1, gathered.shape[0]):
        state = state + gathered[k]
    old[...] = state
    tpos, tvel = predict(
        state[0:3], state[3:6], state[6:9], state[9:12], step_factors(state[12:13])
    )
    columns = jnp.transpose(
        jnp.concatenate([tpos, tvel, tpos[0:2]], axis=0)
    )
    for c in range(6):
        targets[c] = jnp.broadcast_to(columns[:, c : c + 1], (ntarget, LANES))
    factors = step_factors(elapsed_of(levels[...]))
    for t in range(groups):
        spos, svel = predict(
            *(x[:, tile(t)] for x in (pos, vel, acc, jrk)), [f[t : t + 1] for f in factors]
        )
        sources[t, 0:3, :] = spos
        sources[t, 3:6, :] = svel
        sources[t, 6:7, :] = masses[t : t + 1, :]

    def one_group(g, unused):
        rows = pl.ds(pl.multiple_of(g * 8, 8), 8)
        tx, ty, tz, tu, tv, tw = (targets[c, rows, :] for c in range(6))

        def one_tile(t, carry):
            sx, sy, sz, su, sv, sw, mass = (
                jnp.broadcast_to(sources[t, c : c + 1, :], (8, LANES)) for c in range(7)
            )
            dx, dy, dz = (sx - tx, sy - ty, sz - tz)
            du, dv, dw = (su - tu, sv - tv, sw - tw)
            r2 = dx * dx + dy * dy + dz * dz + softening_length
            inv = lax.rsqrt(r2)
            inv_sq = inv * inv
            weight = mass * inv * inv_sq
            radial = (dx * du + dy * dv + dz * dw) * inv_sq
            px, py, pz = (weight * dx, weight * dy, weight * dz)
            ax, ay, az, jx, jy, jz, kx, ky, kz = carry
            return (
                ax + px,
                ay + py,
                az + pz,
                jx + weight * du,
                jy + weight * dv,
                jz + weight * dw,
                kx + radial * px,
                ky + radial * py,
                kz + radial * pz,
            )

        zero = jnp.zeros((8, LANES), f32)
        ax, ay, az, jx, jy, jz, kx, ky, kz = lax.fori_loop(
            0, groups, one_tile, (zero,) * 9, unroll=32
        )
        for c, value in enumerate((ax, ay, az, jx - 3.0 * kx, jy - 3.0 * ky, jz - 3.0 * kz)):
            sums[c, rows, :] = value
        return unused

    lax.fori_loop(0, ntarget // 8, one_group, 0)
    lane = lax.broadcasted_iota(jnp.int32, (ntarget, 8), 1)
    table = jnp.zeros((ntarget, 8), f32)
    for c in range(6):
        table = jnp.where(lane == c, jnp.sum(sums[c], axis=1, keepdims=True), table)
    table = jnp.transpose(table)
    row = lax.broadcasted_iota(jnp.int32, (8, ntarget), 0)
    table = jnp.where(row == 6, active[...].astype(f32), table)
    for k in range(packed.shape[0]):
        for c in range(NEW_ROWS):
            packed[k, :, tile(c)] = table[c : c + 1]


def laid_out(rows, columns, everyone, rowed, groups, before):
    ntarget = rowed.shape[2]
    base = lax.axis_index("ja") * (groups * LANES)
    order = pair_order(rows, columns)
    group = lax.broadcasted_iota(jnp.int32, (groups, ntarget), 0)
    lane = lax.broadcasted_iota(jnp.int32, (LANES, ntarget), 0)
    number = lax.broadcasted_iota(jnp.int32, (groups, ntarget), 1).astype(f32) + 1.0
    spot = jnp.zeros((groups, LANES), f32)
    part = jnp.full((groups, LANES), -1.0, f32)
    forces = []
    for r in range(rows // 2):
        first, *others = [k for k, (h, _) in enumerate(order) if h == r]
        total = everyone[first]
        for k in others:
            total = total + everyone[k]
        for c in range(6):
            rowed[r, c : c + 1, :] = total[:, tile(c)]
        rowed[r, 6:8, :] = jnp.ones((2, ntarget), f32)
        forces.append(rowed[r])
        offset = everyone[first][:, tile(6)].astype(jnp.int32) - base
        hit = group == offset >> 7
        side = (lane == (offset & (LANES - 1))).astype(jnp.bfloat16)
        found = lax.dot_general(
            jnp.where(hit, number, 0.0).astype(jnp.bfloat16),
            side,
            (((1,), (1,)), ((), ())),
            preferred_element_type=f32,
        )
        part = jnp.where(found > 0.5, float(r), part)
        spot = spot + found
    slot = jnp.maximum(spot - 1.0, 0.0).astype(jnp.int32)
    for t in range(groups):
        lanes = jnp.broadcast_to(slot[t : t + 1], (8, LANES))
        holder = jnp.broadcast_to(part[t : t + 1], (8, LANES))
        new = before(t)
        for r in range(rows // 2):
            new = jnp.where(holder == float(r), jnp.take_along_axis(forces[r], lanes, axis=1), new)
        yield new


def same_kernel(rows, columns, same_core, old, targets_new, placed, rowed):
    zero = jnp.zeros((8, LANES), f32)
    tiles = laid_out(rows, columns, same_core, rowed, placed.shape[0], lambda t: zero)
    for t, new in enumerate(tiles):
        placed[t] = new
    me = lax.axis_index("ia") >> 1
    mine = rowed[0]
    for r in range(1, rows // 2):
        mine = jnp.where(me == r, rowed[r], mine)
    o = old[...]
    factors = correction_factors(o[12:13])
    x1, v1 = correct(o[0:3], o[3:6], o[6:9], o[9:12], factors, mine[0:3], mine[3:6])
    targets_new[0:3, :] = x1
    targets_new[3:6, :] = v1
    targets_new[6:12, :] = mine[0:6]


def finish_kernel(
    rows, columns, other_core, placed, pos, vel, acc, jrk, levels, stars_out, stars_new, rowed, sems
):
    groups = levels.shape[0]
    piece = groups // PIECES
    copies = []
    factors = correction_factors(elapsed_of(levels[...]))
    tiles = laid_out(rows, columns, other_core, rowed, groups, lambda t: placed[t])
    for t, new in enumerate(tiles):
        there = jnp.broadcast_to(new[7:8], (3, LANES)) > 0.5
        x0, v0, a0, j0 = (pos[:, tile(t)], vel[:, tile(t)], acc[:, tile(t)], jrk[:, tile(t)])
        a1, j1 = (new[0:3], new[3:6])
        x1, v1 = correct(x0, v0, a0, j0, [f[t : t + 1] for f in factors], a1, j1)
        stars_new[0:3, tile(t)] = jnp.where(there, x1, x0)
        stars_new[3:6, tile(t)] = jnp.where(there, v1, v0)
        stars_new[6:9, tile(t)] = jnp.where(there, a1, a0)
        stars_new[9:12, tile(t)] = jnp.where(there, j1, j0)
        if (t + 1) % piece == 0:
            part_of = (slice(None), slice((t + 1 - piece) * LANES, (t + 1) * LANES))
            copies.append(
                pltpu.make_async_copy(
                    stars_new.at[part_of], stars_out.at[part_of], sems.at[len(copies)]
                )
            )
            copies[-1].start()
    for copy in copies:
        copy.wait()


def local(rows, columns, positions, velocities, accels, jerks, masses, levels, active):
    nlocal = positions.shape[1]
    ntarget = active.shape[0]
    groups = nlocal // LANES
    given = (
        positions,
        velocities,
        accels,
        jerks,
        levels.reshape(groups, LANES),
        masses.reshape(groups, LANES),
        active.reshape(1, ntarget),
    )
    mine, *kept = pl.pallas_call(
        gather_kernel,
        out_shape=(
            pltpu.VMEM((columns, 16, ntarget), f32),
            *(pltpu.VMEM(x.shape, x.dtype) for x in given),
        ),
        in_specs=[HBM] * 7,
        out_specs=(VMEM,) * 8,
        scratch_shapes=[pltpu.SemaphoreType.DMA((11,))],
        compiler_params=PARAMS,
        name="gather",
    )(*(pltpu.with_memory_space_constraint(x, pltpu.HBM) for x in given))
    gathered = lax.all_to_all(mine, "ja", 0, 0, axis_index_groups=[column_order(columns)])
    packed, old = pl.pallas_call(
        force_kernel,
        out_shape=(
            pltpu.VMEM((rows // 2 * columns, 1, NEW_ROWS * ntarget), f32),
            pltpu.VMEM((16, ntarget), f32),
        ),
        in_specs=[VMEM] * 8,
        out_specs=(VMEM, VMEM),
        scratch_shapes=[
            pltpu.VMEM((groups, 8, LANES), f32),
            pltpu.VMEM((6, ntarget, LANES), f32),
            pltpu.VMEM((6, ntarget, LANES), f32),
        ],
        compiler_params=PARAMS,
        name="forces",
    )(gathered, *kept)
    order = pair_order(rows, columns)
    lists = [[(2 * h + core) * columns + c for h, c in order] for core in range(2)]
    same_core = lax.all_to_all(packed, ("ia", "ja"), 0, 0, axis_index_groups=lists)
    other_core = lax.ppermute(same_core, "ia", [(r, r ^ 1) for r in range(rows)])
    targets_new, placed = pl.pallas_call(
        functools.partial(same_kernel, rows, columns),
        out_shape=(
            jax.ShapeDtypeStruct((12, ntarget), f32),
            pltpu.VMEM((groups, 8, LANES), f32),
        ),
        in_specs=[VMEM] * 2,
        out_specs=(VMEM, VMEM),
        scratch_shapes=[pltpu.VMEM((rows // 2, 8, ntarget), f32)],
        compiler_params=PARAMS,
        cost_estimate=pl.CostEstimate(
            flops=200 * nlocal, bytes_accessed=4 * 64 * nlocal, transcendentals=0
        ),
        name="same",
    )(same_core, old)
    stars_new = pl.pallas_call(
        functools.partial(finish_kernel, rows, columns),
        out_shape=jax.ShapeDtypeStruct((12, nlocal), f32),
        in_specs=[VMEM] * 7,
        out_specs=HBM,
        scratch_shapes=[
            pltpu.VMEM((12, nlocal), f32),
            pltpu.VMEM((rows // 2, 8, ntarget), f32),
            pltpu.SemaphoreType.DMA((PIECES,)),
        ],
        compiler_params=PARAMS,
        name="finish",
    )(other_core, placed, *kept[:5])
    return (targets_new, stars_new)


def solution(mesh):
    rows, columns = mesh.shape["ia"], mesh.shape["ja"]

    def body(*args):
        return local(rows, columns, *args)

    return jax.shard_map(
        body,
        mesh=mesh,
        in_specs=(
            P(None, "ja"),
            P(None, "ja"),
            P(None, "ja"),
            P(None, "ja"),
            P("ja"),
            P("ja"),
            P("ia"),
        ),
        out_specs=(P(None, "ia"), P(None, "ja")),
        check_vma=False,
    )
```

```python
import functools

import jax
import jax.numpy as jnp
from jax import lax
from jax.experimental import pallas as pl
from jax.experimental.pallas import tpu as pltpu
from jax.sharding import PartitionSpec as P

softening_length = 0.01
base_step = 0.0625
LANES = 128
PIECES = 8
NEW_ROWS = 7
f32 = jnp.float32
VMEM = pl.BlockSpec(memory_space=pltpu.VMEM)
HBM = pl.BlockSpec(memory_space=pltpu.HBM)
PARAMS = pltpu.CompilerParams(vmem_limit_bytes=24 * 1024 * 1024)


def elapsed_of(levels):
    return (128 >> levels).astype(f32) * (base_step / 128.0)


def step_factors(elapsed):
    half = elapsed * elapsed * 0.5
    return (elapsed, half, half * elapsed * (1.0 / 3.0))


def predict(pos, vel, acc, jrk, factors):
    elapsed, half, sixth = factors
    pred_pos = pos + elapsed * vel + half * acc + sixth * jrk
    pred_vel = vel + elapsed * acc + half * jrk
    return (pred_pos, pred_vel)


def correction_factors(step):
    return (0.5 * step, step * step * (1.0 / 12.0))


def correct(x0, v0, a0, j0, factors, a1, j1):
    half, quad = factors
    v1 = v0 + half * (a0 + a1) + quad * (j0 - j1)
    x1 = x0 + half * (v0 + v1) + quad * (a0 - a1)
    return (x1, v1)


def column_order(columns):
    first = max(columns - 3, 0)
    return [*range(first, columns), *range(first)]


def pair_order(rows, columns):
    return [(h, c) for h in range(rows // 2 - 1, -1, -1) for c in range(columns - 1, -1, -1)]


def tile(t):
    return slice(t * LANES, (t + 1) * LANES)


def gather_kernel(*refs):
    given, out, kept, sems = (refs[:7], refs[7], refs[8:15], refs[15])
    pos, vel, acc, jrk, levels, masses, active = kept
    groups = levels.shape[0]
    half = groups // 2

    def copy_of(n, sem, columns=None):
        if columns is None:
            return pltpu.make_async_copy(given[n], kept[n], sems.at[sem])
        part = (slice(None), columns)
        return pltpu.make_async_copy(given[n].at[part], kept[n].at[part], sems.at[sem])

    small = [copy_of(6, 0), copy_of(4, 1)]
    parts = [
        [copy_of(n, 2 + 4 * h + n, slice(h * half * LANES, (h + 1) * half * LANES)) for n in range(4)]
        for h in range(2)
    ]
    late = copy_of(5, 10)
    for copy in (*small, *parts[0], *parts[1], late):
        copy.start()
    for copy in small:
        copy.wait()
    offset = active[...] - lax.axis_index("ja") * (groups * LANES)
    group = jnp.broadcast_to(offset >> 7, (8, LANES))
    lane = jnp.broadcast_to(offset & (LANES - 1), (8, LANES))
    row = lax.broadcasted_iota(jnp.int32, (8, LANES), 0)
    elapsed = elapsed_of(levels[...])
    steps = jnp.zeros((8, LANES), f32)
    for t in range(0, groups, 8):
        here = group == row + t
        steps = jnp.where(here, jnp.take_along_axis(elapsed[t : t + 8], lane, axis=1), steps)
    found = [jnp.zeros((3, LANES), f32)] * 4
    for h in range(2):
        for copy in parts[h]:
            copy.wait()
        for t in range(h * half, (h + 1) * half):
            here = group[0:3] == t
            found = [
                jnp.where(here, jnp.take_along_axis(x[:, tile(t)], lane[0:3], axis=1), old)
                for x, old in zip((pos, vel, acc, jrk), found)
            ]
    steps = jnp.broadcast_to(jnp.sum(steps, axis=0, keepdims=True), (4, LANES))
    for k in range(out.shape[0]):
        for n, value in enumerate(found):
            out[k, 3 * n : 3 * n + 3, :] = value
        out[k, 12:16, :] = steps
    late.wait()


def force_kernel(
    gathered, pos, vel, acc, jrk, levels, masses, active, packed, old, sources, targets, sums
):
    groups = levels.shape[0]
    ntarget = active.shape[1]
    state = gathered[0]
    for k in range(1, gathered.shape[0]):
        state = state + gathered[k]
    old[...] = state
    tpos, tvel = predict(
        state[0:3], state[3:6], state[6:9], state[9:12], step_factors(state[12:13])
    )
    columns = jnp.transpose(
        jnp.concatenate([tpos, tvel, tpos[0:2]], axis=0)
    )
    for c in range(6):
        targets[c] = jnp.broadcast_to(columns[:, c : c + 1], (ntarget, LANES))
    factors = step_factors(elapsed_of(levels[...]))
    for t in range(groups):
        spos, svel = predict(
            *(x[:, tile(t)] for x in (pos, vel, acc, jrk)), [f[t : t + 1] for f in factors]
        )
        sources[t, 0:3, :] = spos
        sources[t, 3:6, :] = svel
        sources[t, 6:7, :] = masses[t : t + 1, :]

    def one_group(g, unused):
        rows = pl.ds(pl.multiple_of(g * 8, 8), 8)
        tx, ty, tz, tu, tv, tw = (targets[c, rows, :] for c in range(6))

        def one_tile(t, carry):
            sx, sy, sz, su, sv, sw, mass = (
                jnp.broadcast_to(sources[t, c : c + 1, :], (8, LANES)) for c in range(7)
            )
            dx, dy, dz = (sx - tx, sy - ty, sz - tz)
            du, dv, dw = (su - tu, sv - tv, sw - tw)
            r2 = dx * dx + dy * dy + dz * dz + softening_length
            inv = lax.rsqrt(r2)
            inv_sq = inv * inv
            weight = mass * inv * inv_sq
            radial = (dx * du + dy * dv + dz * dw) * inv_sq
            px, py, pz = (weight * dx, weight * dy, weight * dz)
            ax, ay, az, jx, jy, jz, kx, ky, kz = carry
            return (
                ax + px,
                ay + py,
                az + pz,
                jx + weight * du,
                jy + weight * dv,
                jz + weight * dw,
                kx + radial * px,
                ky + radial * py,
                kz + radial * pz,
            )

        zero = jnp.zeros((8, LANES), f32)
        ax, ay, az, jx, jy, jz, kx, ky, kz = lax.fori_loop(
            0, groups, one_tile, (zero,) * 9, unroll=32
        )
        for c, value in enumerate((ax, ay, az, jx - 3.0 * kx, jy - 3.0 * ky, jz - 3.0 * kz)):
            sums[c, rows, :] = value
        return unused

    lax.fori_loop(0, ntarget // 8, one_group, 0)
    lane = lax.broadcasted_iota(jnp.int32, (ntarget, 8), 1)
    table = jnp.zeros((ntarget, 8), f32)
    for c in range(6):
        table = jnp.where(lane == c, jnp.sum(sums[c], axis=1, keepdims=True), table)
    table = jnp.transpose(table)
    row = lax.broadcasted_iota(jnp.int32, (8, ntarget), 0)
    table = jnp.where(row == 6, active[...].astype(f32), table)
    for k in range(packed.shape[0]):
        for c in range(NEW_ROWS):
            packed[k, :, tile(c)] = table[c : c + 1]


def laid_out(rows, columns, everyone, rowed, groups, before):
    ntarget = rowed.shape[2]
    base = lax.axis_index("ja") * (groups * LANES)
    order = pair_order(rows, columns)
    group = lax.broadcasted_iota(jnp.int32, (groups, ntarget), 0)
    lane = lax.broadcasted_iota(jnp.int32, (LANES, ntarget), 0)
    number = lax.broadcasted_iota(jnp.int32, (groups, ntarget), 1).astype(f32) + 1.0
    spot = jnp.zeros((groups, LANES), f32)
    part = jnp.full((groups, LANES), -1.0, f32)
    forces = []
    for r in range(rows // 2):
        first, *others = [k for k, (h, _) in enumerate(order) if h == r]
        total = everyone[first]
        for k in others:
            total = total + everyone[k]
        for c in range(6):
            rowed[r, c : c + 1, :] = total[:, tile(c)]
        rowed[r, 6:8, :] = jnp.ones((2, ntarget), f32)
        forces.append(rowed[r])
        offset = everyone[first][:, tile(6)].astype(jnp.int32) - base
        hit = group == offset >> 7
        side = (lane == (offset & (LANES - 1))).astype(jnp.bfloat16)
        found = lax.dot_general(
            jnp.where(hit, number, 0.0).astype(jnp.bfloat16),
            side,
            (((1,), (1,)), ((), ())),
            preferred_element_type=f32,
        )
        part = jnp.where(found > 0.5, float(r), part)
        spot = spot + found
    slot = jnp.maximum(spot - 1.0, 0.0).astype(jnp.int32)
    for t in range(groups):
        lanes = jnp.broadcast_to(slot[t : t + 1], (8, LANES))
        holder = jnp.broadcast_to(part[t : t + 1], (8, LANES))
        new = before(t)
        for r in range(rows // 2):
            new = jnp.where(holder == float(r), jnp.take_along_axis(forces[r], lanes, axis=1), new)
        yield new


def same_kernel(rows, columns, same_core, old, targets_new, placed, rowed):
    zero = jnp.zeros((8, LANES), f32)
    tiles = laid_out(rows, columns, same_core, rowed, placed.shape[0], lambda t: zero)
    for t, new in enumerate(tiles):
        placed[t] = new
    me = lax.axis_index("ia") >> 1
    mine = rowed[0]
    for r in range(1, rows // 2):
        mine = jnp.where(me == r, rowed[r], mine)
    o = old[...]
    factors = correction_factors(o[12:13])
    x1, v1 = correct(o[0:3], o[3:6], o[6:9], o[9:12], factors, mine[0:3], mine[3:6])
    targets_new[0:3, :] = x1
    targets_new[3:6, :] = v1
    targets_new[6:12, :] = mine[0:6]


def finish_kernel(
    rows, columns, other_core, placed, pos, vel, acc, jrk, levels, stars_out, stars_new, rowed, sems
):
    groups = levels.shape[0]
    piece = groups // PIECES
    copies = []
    factors = correction_factors(elapsed_of(levels[...]))
    tiles = laid_out(rows, columns, other_core, rowed, groups, lambda t: placed[t])
    for t, new in enumerate(tiles):
        there = jnp.broadcast_to(new[7:8], (3, LANES)) > 0.5
        x0, v0, a0, j0 = (pos[:, tile(t)], vel[:, tile(t)], acc[:, tile(t)], jrk[:, tile(t)])
        a1, j1 = (new[0:3], new[3:6])
        x1, v1 = correct(x0, v0, a0, j0, [f[t : t + 1] for f in factors], a1, j1)
        stars_new[0:3, tile(t)] = jnp.where(there, x1, x0)
        stars_new[3:6, tile(t)] = jnp.where(there, v1, v0)
        stars_new[6:9, tile(t)] = jnp.where(there, a1, a0)
        stars_new[9:12, tile(t)] = jnp.where(there, j1, j0)
        if (t + 1) % piece == 0:
            lanes = slice((t + 1 - piece) * LANES, (t + 1) * LANES)
            for part_of in ((slice(0, 8), lanes), (slice(8, 12), lanes)):
                copies.append(
                    pltpu.make_async_copy(
                        stars_new.at[part_of], stars_out.at[part_of], sems.at[len(copies)]
                    )
                )
                copies[-1].start()
    for copy in copies:
        copy.wait()


def local(rows, columns, positions, velocities, accels, jerks, masses, levels, active):
    nlocal = positions.shape[1]
    ntarget = active.shape[0]
    groups = nlocal // LANES
    given = (
        positions,
        velocities,
        accels,
        jerks,
        levels.reshape(groups, LANES),
        masses.reshape(groups, LANES),
        active.reshape(1, ntarget),
    )
    mine, *kept = pl.pallas_call(
        gather_kernel,
        out_shape=(
            pltpu.VMEM((columns, 16, ntarget), f32),
            *(pltpu.VMEM(x.shape, x.dtype) for x in given),
        ),
        in_specs=[HBM] * 7,
        out_specs=(VMEM,) * 8,
        scratch_shapes=[pltpu.SemaphoreType.DMA((11,))],
        compiler_params=PARAMS,
        name="gather",
    )(*(pltpu.with_memory_space_constraint(x, pltpu.HBM) for x in given))
    gathered = lax.all_to_all(mine, "ja", 0, 0, axis_index_groups=[column_order(columns)])
    packed, old = pl.pallas_call(
        force_kernel,
        out_shape=(
            pltpu.VMEM((rows // 2 * columns, 1, NEW_ROWS * ntarget), f32),
            pltpu.VMEM((16, ntarget), f32),
        ),
        in_specs=[VMEM] * 8,
        out_specs=(VMEM, VMEM),
        scratch_shapes=[
            pltpu.VMEM((groups, 8, LANES), f32),
            pltpu.VMEM((6, ntarget, LANES), f32),
            pltpu.VMEM((6, ntarget, LANES), f32),
        ],
        compiler_params=PARAMS,
        name="forces",
    )(gathered, *kept)
    order = pair_order(rows, columns)
    lists = [[(2 * h + core) * columns + c for h, c in order] for core in range(2)]
    same_core = lax.all_to_all(packed, ("ia", "ja"), 0, 0, axis_index_groups=lists)
    other_core = lax.ppermute(same_core, "ia", [(r, r ^ 1) for r in range(rows)])
    targets_new, placed = pl.pallas_call(
        functools.partial(same_kernel, rows, columns),
        out_shape=(
            jax.ShapeDtypeStruct((12, ntarget), f32),
            pltpu.VMEM((groups, 8, LANES), f32),
        ),
        in_specs=[VMEM] * 2,
        out_specs=(VMEM, VMEM),
        scratch_shapes=[pltpu.VMEM((rows // 2, 8, ntarget), f32)],
        compiler_params=PARAMS,
        cost_estimate=pl.CostEstimate(
            flops=200 * nlocal, bytes_accessed=4 * 64 * nlocal, transcendentals=0
        ),
        name="same",
    )(same_core, old)
    stars_new = pl.pallas_call(
        functools.partial(finish_kernel, rows, columns),
        out_shape=jax.ShapeDtypeStruct((12, nlocal), f32),
        in_specs=[VMEM] * 7,
        out_specs=HBM,
        scratch_shapes=[
            pltpu.VMEM((12, nlocal), f32),
            pltpu.VMEM((rows // 2, 8, ntarget), f32),
            pltpu.SemaphoreType.DMA((2 * PIECES,)),
        ],
        compiler_params=PARAMS,
        name="finish",
    )(other_core, placed, *kept[:5])
    return (targets_new, stars_new)


def solution(mesh):
    rows, columns = mesh.shape["ia"], mesh.shape["ja"]

    def body(*args):
        return local(rows, columns, *args)

    return jax.shard_map(
        body,
        mesh=mesh,
        in_specs=(
            P(None, "ja"),
            P(None, "ja"),
            P(None, "ja"),
            P(None, "ja"),
            P("ja"),
            P("ja"),
            P("ia"),
        ),
        out_specs=(P(None, "ia"), P(None, "ja")),
        check_vma=False,
    )
```
